32 devices in a mesh: res: 8 (over y, x, core), hid: 4 (over z).
Axes of the slice: x: 2, y: 2, z: 4, core: 2. Of those that a mesh axis runs over, the one named last changes fastest.
Arguments:
- nodes: bfloat16 [1024, 512], P(('res', 'hid')), may hold values from -6 to 6
- edges: bfloat16 [1024, 60, 192], P(('res', 'hid')), may hold values from -6 to 6
- send_rows: int32 [32, 8, 16], P(('res', 'hid')), may hold values from 0 to 31, as said below
- neighbor_slots: int32 [1024, 60], P(('res', 'hid')), may hold values from 0 to 127, as said below
- neighbor_counts: int32 [1024], P(('res', 'hid')), may hold values from 15 to 60
- message_first: bfloat16 [1216, 512], replicated, may hold values from -0.15625 to 0.15625
- message_first_bias: float32 [512], replicated, may hold values from -3 to 3
- message_second: bfloat16 [512, 512], replicated, may hold values from -0.25 to 0.25
- message_second_bias: float32 [512], replicated, may hold values from -3 to 3
- message_third: bfloat16 [512, 512], replicated, may hold values from -0.5 to 0.5
- message_third_bias: float32 [512], replicated, may hold values from -1.75 to 1.75
- message_gain: float32 [512], replicated, may hold values from 0.5 to 1.5
- message_shift: float32 [512], replicated, may hold values from -1.25 to 1.25
- expand_weight: bfloat16 [512, 2048], P(None, 'hid'), may hold values from -0.25 to 0.25
- expand_bias: float32 [2048], P('hid'), may hold values from -3 to 3
- reduce_weight: bfloat16 [2048, 512], P('hid'), may hold values from -0.125 to 0.125
- reduce_bias: float32 [512], replicated, may hold values from -1.75 to 1.75
- feed_gain: float32 [512], replicated, may hold values from 0.5 to 1.5
- feed_shift: float32 [512], replicated, may hold values from -1.25 to 1.25
- edge_first: bfloat16 [1216, 192], replicated, may hold values from -0.15625 to 0.15625
- edge_first_bias: float32 [192], replicated, may hold values from -3 to 3
- edge_second: bfloat16 [192, 192], replicated, may hold values from -0.4375 to 0.4375
- edge_second_bias: float32 [192], replicated, may hold values from -3 to 3
- edge_third: bfloat16 [192, 192], replicated, may hold values from -0.4375 to 0.4375
- edge_third_bias: float32 [192], replicated, may hold values from -1.75 to 1.75
- edge_gain: float32 [192], replicated, may hold values from 0.5 to 1.5
- edge_shift: float32 [192], replicated, may hold values from -1.25 to 1.25
- node_cotangent: bfloat16 [1024, 512], P(('res', 'hid')), may hold values from -6 to 6
- edge_cotangent: bfloat16 [1024, 60, 192], P(('res', 'hid')), may hold values from -6 to 6
Outputs:
- node_result: float32 [1024, 512], P(('res', 'hid'))
- edge_result: float32 [1024, 60, 192], P(('res', 'hid'))
- node_gradient: float32 [1024, 512], P(('res', 'hid'))
- edge_gradient: float32 [1024, 60, 192], P(('res', 'hid'))
- message_first_gradient: float32 [1216, 512], replicated
- message_first_bias_gradient: float32 [512], replicated
- message_second_gradient: float32 [512, 512], replicated
- message_second_bias_gradient: float32 [512], replicated
- message_third_gradient: float32 [512, 512], replicated
- message_third_bias_gradient: float32 [512], replicated
- message_gain_gradient: float32 [512], replicated
- message_shift_gradient: float32 [512], replicated
- expand_weight_gradient: float32 [512, 2048], P(None, 'hid')
- expand_bias_gradient: float32 [2048], P('hid')
- reduce_weight_gradient: float32 [2048, 512], P('hid')
- reduce_bias_gradient: float32 [512], replicated
- feed_gain_gradient: float32 [512], replicated
- feed_shift_gradient: float32 [512], replicated
- edge_first_gradient: float32 [1216, 192], replicated
- edge_first_bias_gradient: float32 [192], replicated
- edge_second_gradient: float32 [192, 192], replicated
- edge_second_bias_gradient: float32 [192], replicated
- edge_third_gradient: float32 [192, 192], replicated
- edge_third_bias_gradient: float32 [192], replicated
- edge_gain_gradient: float32 [192], replicated
- edge_shift_gradient: float32 [192], replicated
The draws below stay inside these ranges and needn't reach their ends.
Inputs may be any that keep to these rules, and one draw needn't show every extreme that they name: `send_rows`: each row of 16 entries names different rows of its block. `neighbor_slots`: a residue's 60 entries are different.
All inputs are finite; a program needn't handle non-finite values.
Results may differ from the reference program's by a relative error of at most 0.024.
Values may be sent and summed in bfloat16 or wider, within the bound.
No kernel may reach another device: no remote copies, remote signals or barrier semaphores. Data moves between devices by JAX's collectives and lax.ppermute only.
A program may use at most 128 MiB of HBM per device.

```python
from functools import partial
import jax
import jax.numpy as jnp
from jax import lax

DN = 512
DE = 192
MH = 512
FFH = 2048
K = 60
RES_DEV = 32
SLOTS = 16
PEERS = 8
BLOCKS = 32
BUFFER = 128
RES = 1024
N_RES = 8
N_HID = 4


def draw_send_rows(key, part):
    key = jax.random.fold_in(key, 11)
    keys = jax.random.split(key, BLOCKS * PEERS)
    picks = jax.vmap(lambda single: jax.random.permutation(single, RES_DEV)[:SLOTS])(keys)
    return picks.reshape(BLOCKS, PEERS, SLOTS).astype(jnp.int32)


def draw_neighbor_slots(key, part):
    key = jax.random.fold_in(key, 23)
    keys = jax.random.split(key, RES)
    picks = jax.vmap(lambda single: jax.random.permutation(single, BUFFER)[:K])(keys)
    return picks.astype(jnp.int32)


def set_ends(values, stream_key, smallest, top_value):
    spot = [jax.random.randint(jax.random.fold_in(stream_key, axis), (), 0, length) for axis, length in enumerate(values.shape)]
    longest = values.shape.index(max(values.shape))
    neighbour = spot[:longest] + [(spot[longest] + 1) % values.shape[longest]] + spot[longest + 1:]
    return values.at[tuple(spot)].set(smallest).at[tuple(neighbour)].set(top_value)


def block_scale(stream_key, extent, cuts, smallest, high):
    def one(axis_at, parts):
        heights = jax.random.uniform(jax.random.fold_in(jax.random.fold_in(stream_key, 6), axis_at), (parts,), jnp.float32, smallest / len(cuts), high / len(cuts))
        return jnp.repeat(jnp.exp(heights), extent[axis_at] // parts).reshape((-1,) + (1,) * (len(extent) - axis_at - 1))

    loudness = one(*cuts[0])
    for cut in cuts[1:]:
        loudness = loudness * one(*cut)
    return loudness


def scatter_about(own_key, extent, scale, most, shards=(), kind=jnp.bfloat16):
    entries = jax.random.normal(own_key, extent, jnp.float32) * scale
    if len(shards) > 0:
        entries = block_scale(own_key, extent, shards, -0.22, 0.18) * entries
    return jnp.clip(entries, min=-most, max=most).astype(kind)


def setup_inputs(seed: int = 0) -> dict:
    arg_keys = jax.random.split(jax.random.key(seed), 30)
    return {
        "nodes": scatter_about(arg_keys[0], (RES, DN), 1.0, 6.0, ((0, 32),)),
        "edges": scatter_about(arg_keys[1], (RES, K, DE), 1.0, 6.0, ((0, 32),)),
        "send_rows": draw_send_rows(jax.random.fold_in(arg_keys[29], 71), 0),
        "neighbor_slots": draw_neighbor_slots(jax.random.fold_in(arg_keys[29], 71), 0),
        "neighbor_counts": set_ends(jax.random.randint(arg_keys[4], (RES,), K // 4, K + 1), jax.random.fold_in(arg_keys[4], 1), K // 4, K).astype(jnp.int32),
        "message_first": scatter_about(arg_keys[5], (2 * DN + DE, MH), (2 * DN + DE) ** -0.5, 0.15625),
        "message_first_bias": scatter_about(arg_keys[6], (MH,), 0.5, 3.0, (), jnp.float32),
        "message_second": scatter_about(arg_keys[7], (MH, MH), MH ** -0.5, 0.25),
        "message_second_bias": scatter_about(arg_keys[8], (MH,), 0.5, 3.0, (), jnp.float32),
        "message_third": scatter_about(arg_keys[9], (MH, DN), (MH // 4) ** -0.5, 0.5),
        "message_third_bias": scatter_about(arg_keys[10], (DN,), 0.3, 1.75, (), jnp.float32),
        "message_gain": jnp.clip(1.0 + 0.1 * jax.random.normal(arg_keys[11], (DN,), jnp.float32), 0.5, 1.5),
        "message_shift": scatter_about(arg_keys[12], (DN,), 0.2, 1.25, (), jnp.float32),
        "expand_weight": scatter_about(arg_keys[13], (DN, FFH), DN ** -0.5, 0.25, ((1, 4),)),
        "expand_bias": scatter_about(arg_keys[14], (FFH,), 0.5, 3.0, ((0, 4),), jnp.float32),
        "reduce_weight": scatter_about(arg_keys[15], (FFH, DN), FFH ** -0.5, 0.125, ((0, 4),)),
        "reduce_bias": scatter_about(arg_keys[16], (DN,), 0.3, 1.75, (), jnp.float32),
        "feed_gain": jnp.clip(1.0 + 0.1 * jax.random.normal(arg_keys[17], (DN,), jnp.float32), 0.5, 1.5),
        "feed_shift": scatter_about(arg_keys[18], (DN,), 0.2, 1.25, (), jnp.float32),
        "edge_first": scatter_about(arg_keys[19], (2 * DN + DE, DE), (2 * DN + DE) ** -0.5, 0.15625),
        "edge_first_bias": scatter_about(arg_keys[20], (DE,), 0.5, 3.0, (), jnp.float32),
        "edge_second": scatter_about(arg_keys[21], (DE, DE), DE ** -0.5, 0.4375),
        "edge_second_bias": scatter_about(arg_keys[22], (DE,), 0.5, 3.0, (), jnp.float32),
        "edge_third": scatter_about(arg_keys[23], (DE, DE), DE ** -0.5, 0.4375),
        "edge_third_bias": scatter_about(arg_keys[24], (DE,), 0.3, 1.75, (), jnp.float32),
        "edge_gain": jnp.clip(1.0 + 0.1 * jax.random.normal(arg_keys[25], (DE,), jnp.float32), 0.5, 1.5),
        "edge_shift": scatter_about(arg_keys[26], (DE,), 0.2, 1.25, (), jnp.float32),
        "node_cotangent": scatter_about(arg_keys[27], (RES, DN), 1.0, 6.0, ((0, 32),)),
        "edge_cotangent": scatter_about(arg_keys[28], (RES, K, DE), 1.0, 6.0, ((0, 32),)),
    }


HIGHEST = lax.Precision.HIGHEST

@jax.custom_vjp
def low(v):
    return lax.optimization_barrier(v.astype(jnp.bfloat16)).astype(jnp.float32)

@jax.custom_vjp
def low_back(v):
    return v

def low_keep(v):
    return (low(v), None)

def low_pass(kept, grad):
    return (grad,)

def back_keep(v):
    return (v, None)

def back_low(kept, grad):
    return (low(grad),)
low.defvjp(low_keep, low_pass)
low_back.defvjp(back_keep, back_low)

def product(left, right):
    return jnp.dot(left, right, precision=HIGHEST)

def layer_norm(values, gain, shift):
    center = values - lax.optimization_barrier(jnp.mean(values, axis=-1, keepdims=True))
    spread = lax.optimization_barrier(jnp.mean(center * center, axis=-1, keepdims=True))
    return center * lax.rsqrt(spread + 1e-05) * gain + shift

def route(values, send_rows):
    width = values.shape[-1]
    blocks = values.reshape(N_RES * N_HID, RES_DEV, width)
    table = send_rows.reshape(N_RES * N_HID, N_RES * SLOTS)
    picked = jax.vmap(lambda block, index: block[index])(blocks, table)
    picked = picked.reshape(N_RES, N_HID, N_RES, SLOTS, width)
    return jnp.transpose(picked, (2, 1, 0, 3, 4)).reshape(N_RES * N_HID, N_RES * SLOTS, width)

def message_block(weights, node_rows, buffer, edge_rows, slot_rows, count_rows):
    lower, first_bias, second, second_bias, third, third_bias = weights
    edge_term = low_back(jnp.einsum('rkd,dm->rkm', edge_rows, lower, precision=HIGHEST))
    first_pre = node_rows[:, None, :] + buffer[slot_rows] + edge_term + first_bias
    first_act = low(jax.nn.gelu(first_pre))
    second_pre = low_back(jnp.einsum('rkm,mn->rkn', first_act, second, precision=HIGHEST)) + second_bias
    second_act = low(jax.nn.gelu(second_pre))
    message_rows = low_back(jnp.einsum('rkm,mn->rkn', second_act, third, precision=HIGHEST)) + third_bias
    positions = jnp.arange(slot_rows.shape[1], dtype=jnp.int32)
    valid = (positions[None, :] < count_rows[:, None]).astype(jnp.float32)
    return lax.optimization_barrier(jnp.sum(message_rows * valid[:, :, None], axis=1)) / count_rows.astype(jnp.float32)[:, None]

def edge_block(weights, node_rows, buffer, edge_state, edge_rows, slot_rows):
    lower, first_bias, second, second_bias, third, third_bias, gain, shift = weights
    edge_term = low_back(jnp.einsum('rkd,de->rke', edge_rows, lower, precision=HIGHEST))
    edge_pre = node_rows[:, None, :] + buffer[slot_rows] + edge_term + first_bias
    edge_act = low(jax.nn.gelu(edge_pre))
    edge_mid = low_back(jnp.einsum('rkd,de->rke', edge_act, second, precision=HIGHEST)) + second_bias
    edge_mid_act = low(jax.nn.gelu(edge_mid))
    update = low_back(jnp.einsum('rkd,de->rke', edge_mid_act, third, precision=HIGHEST)) + third_bias
    return layer_norm(edge_state + update, gain, shift)

def layer(state, edge_state, params, send_rows, neighbor_slots, neighbor_counts):
    message_first, message_first_bias, message_second, message_second_bias, message_third, message_third_bias, message_gain, message_shift, expand_weight, expand_bias, reduce_weight, reduce_bias, feed_gain, feed_shift, edge_first, edge_first_bias, edge_second, edge_second_bias, edge_third, edge_third_bias, edge_gain, edge_shift = params
    node_low = low(state)
    node_part = low_back(product(node_low, message_first[:DN]))
    query = low(low_back(product(node_low, message_first[DN:2 * DN])))
    query_buffer = low_back(route(query, send_rows))
    edge_low = low(edge_state)
    edge_blocks = edge_low.reshape(N_RES * N_HID, RES_DEV, K, DE)
    slot_blocks = neighbor_slots.reshape(N_RES * N_HID, RES_DEV, K)
    count_blocks = neighbor_counts.reshape(N_RES * N_HID, RES_DEV)
    message_weights = (message_first[2 * DN:], message_first_bias, message_second, message_second_bias, message_third, message_third_bias)
    message_step = jax.checkpoint(partial(message_block, message_weights))
    message_mean = lax.map(lambda items: message_step(*items), (node_part.reshape(N_RES * N_HID, RES_DEV, MH), query_buffer, edge_blocks, slot_blocks, count_blocks)).reshape(RES, DN)
    first_sum = state + message_mean
    node_mid = layer_norm(first_sum, message_gain, message_shift)
    mid_low = low(node_mid)
    expand_pre = low_back(product(mid_low, expand_weight)) + expand_bias
    expand_act = low(jax.nn.gelu(expand_pre))
    feed_out = low_back(product(expand_act, reduce_weight)) + reduce_bias
    node_new = layer_norm(node_mid + feed_out, feed_gain, feed_shift)
    new_low = low(node_new)
    edge_node = low_back(product(new_low, edge_first[:DN]))
    key = low(low_back(product(new_low, edge_first[DN:2 * DN])))
    key_buffer = low_back(route(key, send_rows))
    edge_weights = (edge_first[2 * DN:], edge_first_bias, edge_second, edge_second_bias, edge_third, edge_third_bias, edge_gain, edge_shift)
    edge_step = jax.checkpoint(partial(edge_block, edge_weights))
    edge_new = lax.map(lambda items: edge_step(*items), (edge_node.reshape(N_RES * N_HID, RES_DEV, DE), key_buffer, edge_state.reshape(N_RES * N_HID, RES_DEV, K, DE), edge_blocks, slot_blocks)).reshape(RES, K, DE)
    return (node_new, edge_new)

def reference(nodes, edges, send_rows, neighbor_slots, neighbor_counts, message_first, message_first_bias, message_second, message_second_bias, message_third, message_third_bias, message_gain, message_shift, expand_weight, expand_bias, reduce_weight, reduce_bias, feed_gain, feed_shift, edge_first, edge_first_bias, edge_second, edge_second_bias, edge_third, edge_third_bias, edge_gain, edge_shift, node_cotangent, edge_cotangent):
    params = tuple((item.astype(jnp.float32) for item in (message_first, message_first_bias, message_second, message_second_bias, message_third, message_third_bias, message_gain, message_shift, expand_weight, expand_bias, reduce_weight, reduce_bias, feed_gain, feed_shift, edge_first, edge_first_bias, edge_second, edge_second_bias, edge_third, edge_third_bias, edge_gain, edge_shift)))
    recycled_nodes, recycled_edges = layer(nodes.astype(jnp.float32), edges.astype(jnp.float32), params, send_rows, neighbor_slots, neighbor_counts)

    def second_pass(state, edge_state, *weights):
        return layer(state, edge_state, weights, send_rows, neighbor_slots, neighbor_counts)
    (node_result, edge_result), pull = jax.vjp(second_pass, recycled_nodes, recycled_edges, *params)
    grads = pull((node_cotangent.astype(jnp.float32), edge_cotangent.astype(jnp.float32)))
    return (node_result, edge_result, grads[0], grads[1], grads[2], grads[3], grads[4], grads[5], grads[6], grads[7], grads[8], grads[9], grads[10], grads[11], grads[12], grads[13], grads[14], grads[15], grads[16], grads[17], grads[18], grads[19], grads[20], grads[21], grads[22], grads[23])
```

```python
import jax
import jax.numpy as jnp
from jax import lax
from jax.experimental import pallas as pl
from jax.experimental.pallas import tpu as pltpu
from jax.sharding import PartitionSpec as P

BF = jnp.bfloat16
F32 = jnp.float32
LEAN = 0.7978845608028654
CUBE = LEAN * 0.044715
MIB = 1 << 20
KEEP = pl.BlockSpec(memory_space=pltpu.VMEM)


def dot(left, right):
    return jnp.dot(left, right, preferred_element_type=F32)


def dot_nt(left, right):
    return lax.dot_general(left, right, (((1,), (1,)), ((), ())), preferred_element_type=F32)


def dot_tn(left, right):
    return lax.dot_general(left, right, (((0,), (0,)), ((), ())), preferred_element_type=F32)


def smooth(v):
    t = jnp.tanh(v * (LEAN + CUBE * (v * v)))
    half = 0.5 * v
    return half + half * t


def smooth_slope(v):
    v2 = v * v
    t = jnp.tanh(v * (LEAN + CUBE * v2))
    half = 0.5 * v
    slope = (0.5 + 0.5 * t) + (half - half * (t * t)) * (LEAN + (3.0 * CUBE) * v2)
    return half + half * t, slope


def centred(x):
    center = x - jnp.mean(x, axis=-1, keepdims=True)
    rate = lax.rsqrt(jnp.mean(center * center, axis=-1, keepdims=True) + 1e-05)
    return center * rate, rate


def norm_pull(hat, rate, gain, up):
    g = up * gain
    return rate * (
        g - jnp.mean(g, axis=-1, keepdims=True) - hat * jnp.mean(g * hat, axis=-1, keepdims=True)
    )


def tiled_add(rows, part):
    n, width = part.shape
    return (rows.reshape(-1, n, width) + part[None]).reshape(rows.shape)


def fold(rows, n):
    return jnp.sum(rows.reshape(-1, n, rows.shape[-1]), axis=0)


def call(body, outs, args, name, scratch=(), limit=12, spot=None):
    args = jax.tree.map(lambda v: pltpu.with_memory_space_constraint(v, pltpu.VMEM), list(args))
    specs = jax.tree.map(lambda v: KEEP, args)
    if spot is not None:
        args, specs = [spot] + args, [pl.BlockSpec(memory_space=pltpu.SMEM)] + specs
    return pl.pallas_call(
        body,
        out_shape=outs,
        in_specs=specs,
        out_specs=jax.tree.map(lambda v: KEEP, list(outs)),
        scratch_shapes=list(scratch),
        compiler_params=pltpu.CompilerParams(vmem_limit_bytes=limit * MIB),
        name=name,
    )(*args)


def struct(shape, dtype):
    return pltpu.VMEM(shape, dtype)


def feed(mid, we, web, wr, rb, slopes=None):
    mid_low = mid.astype(BF)
    total = mid + rb[...]
    for h in range(we.shape[0]):
        pre = dot(mid_low, we[h]) + web[h : h + 1, :]
        if slopes is None:
            act = smooth(pre)
        else:
            act, slope = smooth_slope(pre)
            slopes[h] = slope.astype(BF)
        total = total + dot(act.astype(BF), wr[h])
    return mid_low, total


def joined(parts):
    if len(parts) == 1:
        return parts[0][...]
    near, far = parts[: len(parts) // 2], parts[len(parts) // 2 :]
    rows = []
    for mine, other in zip(near, far):
        half = mine.shape[0] // 2
        rows += [mine[:half], other[half:]]
    return jnp.concatenate(rows, axis=0)


def dealt(outs, value):
    n = value.shape[0] // len(outs)
    for m, out in enumerate(outs):
        out[...] = value[m * n : (m + 1) * n].astype(out.dtype)


def halved(spot, pay, keep, send):
    n = keep.shape[0]
    keep[...] = pay[pl.ds(pl.multiple_of(spot[0] * n, n), n), :]
    send[...] = pay[pl.ds(pl.multiple_of((1 - spot[0]) * n, n), n), :]


def message_mean(summed, counts, mt, mtb):
    mean = summed / counts
    high = mean.astype(BF)
    rest = (mean - high.astype(F32)).astype(BF)
    return dot(high, mt) + dot(rest, mt) + mtb


def solution(mesh):
    n_res, n_hid = mesh.shape["res"], mesh.shape["hid"]
    tuned = (n_res, n_hid) == (8, 4)
    pair = [(i, i ^ 1) for i in range(n_res)]

    def to_chip(v, m):
        return lax.ppermute(v, "res", [(i, i ^ (2 * m)) for i in range(n_res)])

    def to_core(v):
        return lax.ppermute(v, "res", pair)

    def to_hid(v, m):
        return lax.ppermute(v, "hid", [(i, i ^ m) for i in range(n_hid)])

    def exchange(parts):
        if not tuned:
            n, width = parts[0].shape
            blocks = parts[0].reshape(n_res, n // n_res, width)
            return [lax.all_to_all(blocks, "res", 0, 0, tiled=True).reshape(n, width)]
        near = [parts[0]] + [to_chip(parts[m], m) for m in (1, 2, 3)]
        return near + [to_core(v) for v in near]

    def pass_one(rows, fanout, step):
        span = step * rows

        def kernel(
            arrived, nodes, edges, pick, counts, mf, mfb, ms, msb, mt, mtb, first_out, sums,
        ):
            width = nodes.shape[1]
            query = dot(joined(arrived), mf[width : 2 * width]).astype(BF)
            part = dot(nodes[...], mf[:width]) + mfb[...]
            lower = mf[2 * width :]
            lots = jnp.broadcast_to(counts[...], (rows, ms.shape[1]))
            sums[...] = jnp.zeros_like(sums)

            def chunk(i, carry):
                at = pl.ds(pl.multiple_of(i * span, span), span)
                pre = dot(pick[at, :], query) + dot(edges[at, :], lower)
                act = smooth(tiled_add(pre, part)).astype(BF)
                act = smooth(dot(act, ms[...]) + msb[...])
                total = sums[...]
                for j in range(step):
                    total = total + jnp.where(
                        lots > (i * step + j).astype(F32), act[j * rows : (j + 1) * rows], 0.0
                    )
                sums[...] = total
                return carry

            lax.fori_loop(0, fanout // step, chunk, 0)
            first_out[...] = nodes[...].astype(F32) + message_mean(
                sums[...], counts[...], mt[...], mtb[...]
            )

        return kernel

    def feed_one(first, own, near, far, mg, msh, rb, fg, fsh, send, new_out, low_out, away_out, we, web, wr):
        expand, reduce, bias = own
        if near is None:
            we[...], wr[...], web[...] = expand[...], reduce[...], bias[...]
        else:
            res, n = near[0], near[1][0][0].shape[0] // 9 * 4
            we[0], wr[0] = expand[...], reduce[...]
            web[0:1, :] = bias[...]
            for m in range(1, n_hid):
                for k, piece in enumerate(near[1][m - 1] + far[m - 1]):
                    at = pl.ds(pl.multiple_of((res[3] ^ (k % 4 * 2 + k // 4)) * n, n), n)
                    we[m, at, :] = piece[:n]
                    wr[m, at, :] = piece[n : 2 * n]
                tail = near[1][m - 1][0][2 * n :].astype(F32)
                web[m : m + 1, :] = tail[0:1] + tail[1:2]
        mid = centred(first[...])[0] * mg[...] + msh[...]
        _, second = feed(mid, we, web, wr, rb)
        new = centred(second)[0] * fg[...] + fsh[...]
        new_out[...] = new
        low = new.astype(BF)
        low_out[...] = low
        dealt(away_out, dot(send[...], low))

    def pass_two(rows, fanout, step):
        span = step * rows

        def kernel(
            arrived, state, low, edges, pick, counts, mf, mfb, ms, msb, mt, mtb, mg, msh,
            we, web, wr, rb, fg, fsh, send, ef, efb, es, esb, et, etb, eg, esh,
            edge_out, act_out, slope1_out, slope2_out, first_out, summed_out, mid_out,
            slopes_out, second_out, new_out, low_out, away_out, sums,
        ):
            width = state.shape[1]
            received = joined(arrived)
            key = dot_nt(received, ef[:, width : 2 * width]).astype(BF)
            edge_part = dot_nt(low[...], ef[:, :width]) + efb[...]
            edge_lower = ef[:, 2 * width :]
            query = dot(received, mf[width : 2 * width]).astype(BF)
            part = dot(low[...], mf[:width]) + mfb[...]
            lower = mf[2 * width :]
            lots = jnp.broadcast_to(counts[...], (rows, ms.shape[1]))
            sums[...] = jnp.zeros_like(sums)

            def chunk(i, carry):
                at = pl.ds(pl.multiple_of(i * span, span), span)
                chosen = pick[at, :]
                old = edges[at, :]
                pre = dot(chosen, key) + dot_nt(old, edge_lower)
                act = smooth(tiled_add(pre, edge_part)).astype(BF)
                act = smooth(dot(act, es[...]) + esb[...]).astype(BF)
                total = old.astype(F32) + dot(act, et[...]) + etb[...]
                fresh = centred(total)[0] * eg[...] + esh[...]
                edge_out[at, :] = fresh
                pre = dot(chosen, query) + dot(fresh.astype(BF), lower)
                act, slope = smooth_slope(tiled_add(pre, part))
                act = act.astype(BF)
                act_out[at, :] = act
                slope1_out[at, :] = slope.astype(BF)
                act, slope = smooth_slope(dot(act, ms[...]) + msb[...])
                total = sums[...]
                for j in range(step):
                    valid = lots > (i * step + j).astype(F32)
                    total = total + jnp.where(valid, act[j * rows : (j + 1) * rows], 0.0)
                    slope2_out[pl.ds(pl.multiple_of(i * span + j * rows, rows), rows), :] = jnp.where(
                        valid, slope[j * rows : (j + 1) * rows], 0.0
                    ).astype(BF)
                sums[...] = total
                return carry

            lax.fori_loop(0, fanout // step, chunk, 0)
            summed_out[...] = sums[...].astype(BF)
            first = state[...] + message_mean(sums[...], counts[...], mt[...], mtb[...])
            first_out[...] = first
            mid = centred(first)[0] * mg[...] + msh[...]
            mid_low, second = feed(mid, we, web, wr, rb, slopes_out)
            mid_out[...] = mid_low
            second_out[...] = second
            new = centred(second)[0] * fg[...] + fsh[...]
            new_out[...] = new
            new_low = new.astype(BF)
            low_out[...] = new_low
            dealt(away_out, dot(send[...], new_low))

        return kernel

    def edge_turn(rows, fanout, step):
        span = step * rows

        def kernel(
            arrived, low, edges, up, pick, ef, efb, es, esb, et, etb, eg, esh,
            result_out, grad_out, act1_out, act2_out, top_out, mid_out, bottom_out,
            slot_out, node_out, vec_out, slots, node, marks,
        ):
            width = low.shape[1]
            key = dot_nt(joined(arrived), ef[:, width : 2 * width]).astype(BF)
            edge_part = dot_nt(low[...], ef[:, :width]) + efb[...]
            edge_lower = ef[:, 2 * width :]
            slots[...] = jnp.zeros_like(slots)
            node[...] = jnp.zeros_like(node)
            marks[...] = jnp.zeros_like(marks)

            def chunk(i, carry):
                at = pl.ds(pl.multiple_of(i * span, span), span)
                chosen = pick[at, :]
                old = edges[at, :]
                pre = dot(chosen, key) + dot_nt(old.astype(BF), edge_lower)
                act, slope1 = smooth_slope(tiled_add(pre, edge_part))
                act1 = act.astype(BF)
                act1_out[at, :] = act1
                act, slope2 = smooth_slope(dot(act1, es[...]) + esb[...])
                act2 = act.astype(BF)
                act2_out[at, :] = act2
                total = old + dot(act2, et[...]) + etb[...]
                hat, rate = centred(total)
                result_out[at, :] = hat * eg[...] + esh[...]
                above = up[at, :].astype(F32)
                sum_grad = norm_pull(hat, rate, eg[...], above)
                top = sum_grad.astype(BF)
                top_out[at, :] = top
                mid = dot_nt(top, et[...]) * slope2
                mid_low = mid.astype(BF)
                mid_out[at, :] = mid_low
                bottom = dot_nt(mid_low, es[...]) * slope1
                bottom_low = bottom.astype(BF)
                bottom_out[at, :] = bottom_low
                grad_out[at, :] = sum_grad + dot(bottom_low, edge_lower)
                marks[0] += fold(above * hat, 8)
                marks[1] += fold(above, 8)
                marks[2] += fold(sum_grad, 8)
                marks[3] += fold(mid, 8)
                node[...] += fold(bottom, rows)
                slots[...] += dot_tn(chosen, bottom_low)
                return carry

            lax.fori_loop(0, fanout // step, chunk, 0)
            dealt(slot_out, slots[...])
            node_out[...] = node[...].astype(BF)
            vec_out[...] = jnp.zeros_like(vec_out)
            for j in range(4):
                vec_out[j : j + 1, :] = jnp.sum(marks[j], axis=0, keepdims=True)
            vec_out[4:5, :] = jnp.sum(node[...], axis=0, keepdims=True)

        return kernel

    def edge_weights(arrived, low, edges, act1, act2, top, mid, bottom, slot, node, pack_out):
        n, wide = act1.shape[1], low.shape[1]
        slot = jnp.concatenate([v[...] for v in slot], axis=0)
        pack_out[:n, :] = dot_tn(node[...], low[...]).astype(BF)
        pack_out[n : 2 * n, :] = dot_tn(slot, joined(arrived)).astype(BF)
        pack_out[2 * n :, :] = jnp.zeros((pack_out.shape[0] - 2 * n, wide), BF)
        pack_out[2 * n : 3 * n, :n] = dot_tn(act1[...], mid[...]).astype(BF)
        pack_out[2 * n : 3 * n, 256 : 256 + n] = dot_tn(act2[...], top[...]).astype(BF)
        lower = dot_tn(bottom[...], edges[...].astype(BF)).astype(BF)
        pack_out[3 * n :, :n] = lower[: n // 2]
        pack_out[3 * n :, 256 : 256 + n] = lower[n // 2 :]

    def node_turn(
        spot, returned, up, node, send, second, slopes, first, counts, summed, ef, mt, mg,
        we, wr, fg, pack, edge_vec, feed_out, sum_out, pull_out, pay_out, pay,
    ):
        width = up.shape[1]
        key_low = dot_tn(send[...], joined(returned)).astype(BF)
        new_grad = (
            up[...].astype(F32) + dot(node[...], ef[:, :width]) + dot(key_low, ef[:, width : 2 * width])
        )
        hat, rate = centred(second[...])
        sum_grad = norm_pull(hat, rate, fg[...], new_grad)
        vecs = [sum_grad, new_grad * hat, new_grad]
        low = sum_grad.astype(BF)
        feed_out[...] = low
        mid_grad = sum_grad
        bias = []
        for h in range(we.shape[0]):
            expand = dot_nt(low, wr[h]) * slopes[h].astype(F32)
            bias.append(jnp.sum(expand, axis=0, keepdims=True))
            mid_grad = mid_grad + dot_nt(expand.astype(BF), we[h])
        hat, rate = centred(first[...])
        first_grad = norm_pull(hat, rate, mg[...], mid_grad)
        sum_out[...] = first_grad
        vecs += [mid_grad * hat, mid_grad, first_grad]
        vecs = [jnp.sum(v, axis=0, keepdims=True) for v in vecs]
        rows_low = (first_grad / counts[...]).astype(BF)
        pull_out[...] = dot_nt(rows_low, mt[...])
        third = dot_tn(summed[...], rows_low).astype(BF)
        head, hidden = pack.shape[0], third.shape[0]
        pay[:head, :] = pack[...]
        pay[head : head + hidden, :] = third
        pay[head + hidden :, :] = jnp.zeros((pay.shape[0] - head - hidden, width), BF)
        rows = jnp.concatenate(vecs + [jnp.zeros((10, width), F32)], axis=0)
        at = lax.broadcasted_iota(jnp.int32, rows.shape, 0)
        share = bias[0].shape[1]
        for h, v in enumerate(bias):
            line = 6 + (spot[2] ^ h)
            if share < width:
                v = jnp.concatenate([v, jnp.zeros((1, width - share), F32)], axis=1)
            rows = jnp.where(at == line, v, rows)
        pay[head + hidden : head + hidden + 16, :] = rows.astype(BF)
        pay[head + hidden + 16 : head + hidden + 32, : edge_vec.shape[1]] = jnp.concatenate(
            [edge_vec[...], jnp.zeros_like(edge_vec)], axis=0
        ).astype(BF)
        if len(pay_out) == 1:
            pay_out[0][...] = pay[...]
        else:
            halved(spot, pay, *pay_out)

    def message_turn(rows, fanout, step):
        span = step * rows

        def kernel(
            spot, arrived, low, edges, pick, pull, act, slope1, slope2, ms,
            first_low_out, slot_out, node_out, pay_out,
            second_low, slots, node, marks, pay,
        ):
            width = low.shape[1]
            slots[...] = jnp.zeros_like(slots)
            node[...] = jnp.zeros_like(node)
            marks[...] = jnp.zeros_like(marks)

            def chunk(i, carry):
                at = pl.ds(pl.multiple_of(i * span, span), span)
                second = slope2[at, :].astype(F32).reshape(step, rows, -1) * pull[...][None]
                marks[...] += jnp.sum(second, axis=0)
                second = second.reshape(span, -1).astype(BF)
                second_low[at, :] = second
                first = dot_nt(second, ms[...]) * slope1[at, :].astype(F32)
                node[...] += fold(first, rows)
                first = first.astype(BF)
                first_low_out[at, :] = first
                slots[...] += dot_tn(pick[at, :], first)
                return carry

            lax.fori_loop(0, fanout // step, chunk, 0)
            slot = slots[...].astype(BF)
            dealt(slot_out, slot)
            node_low = node[...].astype(BF)
            node_out[...] = node_low
            hidden, last = ms.shape[0], 2 * width + edges.shape[1]
            pay[:width, :] = dot_tn(low[...], node_low).astype(BF)
            pay[width : 2 * width, :] = dot_tn(joined(arrived), slot).astype(BF)
            pay[2 * width : last, :] = dot_tn(edges[...].astype(BF), first_low_out[...]).astype(BF)
            pay[last : last + hidden, :] = dot_tn(act[...], second_low[...]).astype(BF)
            pay[last + hidden :, :] = jnp.zeros((pay.shape[0] - last - hidden, hidden), BF)
            vecs = [
                jnp.sum(node[...], axis=0, keepdims=True),
                jnp.sum(marks[...], axis=0, keepdims=True),
                jnp.zeros((14, hidden), F32),
            ]
            pay[last + hidden : last + hidden + 16, :] = jnp.concatenate(vecs, axis=0).astype(BF)
            if len(pay_out) == 1:
                pay_out[0][...] = pay[...]
            else:
                halved(spot, pay, *pay_out)

        return kernel

    def feed_weights(spot, mid, up, we, web, wr, pay_out, pay):
        mid = jnp.concatenate([v[...] for v in mid], axis=0)
        up = jnp.concatenate([v[...] for v in up], axis=0)
        act, slope = smooth_slope(dot(mid, we[...]) + web[...])
        expand = dot_nt(up, wr[...]) * slope
        n, share = we.shape
        expand = dot_tn(mid, expand.astype(BF)).astype(BF)
        reduce = dot_tn(act.astype(BF), up).astype(BF)
        if len(pay_out) == 2 and share != n:
            pay_out[0][...], pay_out[1][...] = expand, reduce
        else:
            pay[:n, :] = expand
            pay[n:, :] = reduce
            halved(spot, pay, *pay_out)

    def node_end(returned, send, first_grad, node, mf, out):
        width = out.shape[1]
        query_low = dot_tn(send[...], joined(returned)).astype(BF)
        out[...] = (
            first_grad[...] + dot_nt(node[...], mf[:width]) + dot_nt(query_low, mf[width : 2 * width])
        )

    def edge_end(rows, fanout, step):
        span = step * rows

        def kernel(grad, first_low, mf, out):
            lower = mf[mf.shape[0] - grad.shape[1] :]

            def chunk(i, carry):
                at = pl.ds(pl.multiple_of(i * span, span), span)
                out[at, :] = grad[at, :] + dot_nt(first_low[at, :], lower)
                return carry

            lax.fori_loop(0, fanout // step, chunk, 0)

        return kernel

    def split_chips(spot, keep, got, outs, total):
        total[...] = (keep[...].astype(F32) + got[...].astype(F32)).astype(BF)
        for m, out in enumerate(outs):
            n = out.shape[0]
            out[...] = total[pl.ds(pl.multiple_of((spot[1] ^ m) * n, n), n), :]

    def summed_up(parts):
        total = parts[0][...].astype(F32)
        for v in parts[1:]:
            total = total + v[...].astype(F32)
        return total.astype(BF)

    def split_hid(spot, parts, outs, total):
        total[...] = summed_up(parts)
        for m, out in enumerate(outs):
            n = out.shape[1]
            out[...] = total[:, pl.ds(pl.multiple_of((spot[2] ^ m) * n, n), n)]

    def add_up(parts, out):
        out[...] = summed_up(parts)

    def join_hid(spot, parts, out):
        for m, v in enumerate(parts):
            n = v.shape[1]
            out[:, pl.ds(pl.multiple_of((spot[2] ^ m) * n, n), n)] = v[...]

    def reduced(spot, keep, send, along_hid, name):
        half, width = keep.shape
        n = half // 4
        got = to_core(send)
        (parts,) = call(
            split_chips, [[struct((n, width), BF)] * 4], (keep, got), name + "_chips",
            [pltpu.VMEM((half, width), BF)], spot=spot,
        )
        parts = [parts[0]] + [to_chip(parts[m], m) for m in (1, 2, 3)]
        if along_hid:
            part = struct((n, width // 4), BF)
            (parts,) = call(
                split_hid, [[part] * 4], (parts,), name + "_hid", [pltpu.VMEM((n, width), BF)], spot=spot
            )
            parts = [parts[0]] + [to_hid(parts[m], m) for m in (1, 2, 3)]
            (own,) = call(add_up, [part], (parts,), name + "_sum")
            parts = [own] + [to_hid(own, m) for m in (1, 2, 3)]
            (own,) = call(join_hid, [struct((n, width), BF)], (parts,), name + "_join", spot=spot)
        else:
            (own,) = call(add_up, [struct((n, width), BF)], (parts,), name + "_sum")
        parts = [own] + [to_chip(own, m) for m in (1, 2, 3)]
        return parts + [to_core(v) for v in parts]

    def laid_out(spot, parts, total):
        if len(parts) == 1:
            total[...] = parts[0][...].astype(F32)
            return
        n = parts[0].shape[0]
        for k, v in enumerate(parts):
            at = ((spot[0] ^ (k // 4)) * 4 + (spot[1] ^ (k % 4))) * n
            total[pl.ds(pl.multiple_of(at, n), n), :] = v[...].astype(F32)

    def unpack_early(spot, parts, first_out, second_out, third_out, message_out, vec_out, total):
        laid_out(spot, parts, total)
        n, wide = second_out.shape[0], message_out.shape[1]
        first_out[:, :wide] = total[:n, :]
        first_out[:, wide : 2 * wide] = total[n : 2 * n, :]
        second_out[...] = total[2 * n : 3 * n, :n]
        third_out[...] = total[2 * n : 3 * n, 256 : 256 + n]
        at = 3 * n + n // 2
        first_out[: n // 2, 2 * wide :] = total[3 * n : at, :n]
        first_out[n // 2 :, 2 * wide :] = total[3 * n : at, 256 : 256 + n]
        hidden = message_out.shape[0]
        message_out[...] = total[at : at + hidden, :]
        vec_out[...] = total[at + hidden : at + hidden + 32, :]

    def unpack_late(spot, parts, first_out, second_out, vec_out, total):
        laid_out(spot, parts, total)
        n, hidden = first_out.shape[0], second_out.shape[0]
        first_out[...] = total[:n, :]
        second_out[...] = total[n : n + hidden, :]
        vec_out[...] = total[n + hidden : n + hidden + 16, :]

    def unpack_feed(spot, parts, expand_out, reduce_out, total):
        laid_out(spot, parts, total)
        n = expand_out.shape[0]
        expand_out[...] = total[:n, :]
        reduce_out[...] = total[n:, :]

    def body(
        nodes, edges, send_rows, neighbor_slots, neighbor_counts, mf, mfb, ms, msb, mt, mtb, mg, msh,
        expand_weight, expand_bias, reduce_weight, rb, fg, fsh, ef, efb, es, esb, et, etb, eg, esh,
        node_up, edge_up,
    ):
        rows, fanout, edge_width = edges.shape
        width, hidden = nodes.shape[1], ms.shape[0]
        share = expand_weight.shape[1]
        n_edges = rows * fanout
        step = 10 if fanout % 10 == 0 else 1
        slots_each = send_rows.shape[2]
        buffer = n_res * slots_each
        row = lambda v: v.reshape(1, -1)
        if tuned:
            res, hid = lax.axis_index("res"), lax.axis_index("hid")
            spot = jnp.stack([res % 2, res // 2, hid, res]).astype(jnp.int32)
            table = send_rows[0].reshape(2, 2, 2, slots_each)
            for bit in range(3):
                table = jnp.where((res >> (2 - bit)) % 2 == 1, jnp.flip(table, bit), table)
            slots = neighbor_slots ^ (res * slots_each)
        else:
            spot = jnp.zeros((4,), jnp.int32)
            table, slots = send_rows[0], neighbor_slots
        edges = edges.transpose(1, 0, 2).reshape(n_edges, edge_width)
        edge_up = edge_up.transpose(1, 0, 2).reshape(n_edges, edge_width)
        ef = ef.T
        send = jax.nn.one_hot(table.reshape(-1), rows, dtype=BF)
        pick = jax.nn.one_hot(slots.T.reshape(-1), buffer, dtype=BF)
        counts = neighbor_counts.astype(F32).reshape(-1, 1)
        mfb, msb, mtb, mg, msh, rb, fg, fsh = map(row, (mfb, msb, mtb, mg, msh, rb, fg, fsh))
        efb, esb, etb, eg, esh = map(row, (efb, esb, etb, eg, esh))
        edge_args = (ef, efb, es, esb, et, etb, eg, esh)
        bias = row(expand_bias)

        if tuned:
            deal = [struct((rows, width), BF)] * 4
            away = jnp.split(dot(send, nodes).astype(BF), 4)
        else:
            deal = [struct((buffer, width), BF)]
            away = [dot(send, nodes).astype(BF)]
        arrived = exchange(away)
        if tuned:
            high = bias.astype(BF)
            rest = (bias - high.astype(F32)).astype(BF)
            n = width // 8
            piece = jnp.concatenate(
                [
                    lax.dynamic_slice_in_dim(expand_weight, res * n, n),
                    lax.dynamic_slice_in_dim(reduce_weight, res * n, n),
                    high, rest, jnp.zeros((n // 4 - 2, width), BF),
                ]
            )
            near = []
            for m in (1, 2, 3):
                got = to_hid(piece, m)
                near.append([got] + [to_chip(got, k) for k in (1, 2, 3)])
            far = [[to_core(v) for v in group] for group in near]
            own = (expand_weight, reduce_weight, bias)
        else:
            near, far = None, None
            own = (
                lax.all_gather(expand_weight, "hid"),
                lax.all_gather(reduce_weight, "hid"),
                lax.all_gather(expand_bias, "hid"),
            )
        (first_one,) = call(
            pass_one(rows, fanout, step),
            [struct((rows, width), F32)],
            (arrived, nodes, edges, pick, counts, mf, mfb, ms, msb, mt, mtb),
            "message_one",
            [pltpu.VMEM((rows, hidden), F32)],
        )
        tail = (first_one, own, near, far, mg, msh, rb, fg, fsh, send)
        state, low, away, we, web, wr = call(
            (lambda spot, first, own, near, *more: feed_one(first, own, near and (spot, near), *more)),
            [
                struct((rows, width), F32), struct((rows, width), BF), deal,
                struct((n_hid, width, share), BF), struct((n_hid, share), F32),
                struct((n_hid, share, width), BF),
            ],
            tail,
            "feed_one",
            spot=spot,
        )
        feed_args = (we, web, wr, rb, fg, fsh)
        message_args = (mf, mfb, ms, msb, mt, mtb, mg, msh)
        arrived2, low2 = exchange(away), low
        (
            edge_state, act, slope1, slope2, first, summed, mid_low, slopes, second, node_result, low3, away,
        ) = call(
            pass_two(rows, fanout, step),
            [
                struct((n_edges, edge_width), F32),
                struct((n_edges, hidden), BF),
                struct((n_edges, hidden), BF),
                struct((n_edges, hidden), BF),
                struct((rows, width), F32),
                struct((rows, hidden), BF),
                struct((rows, width), BF),
                struct((n_hid, rows, share), BF),
                struct((rows, width), F32),
                jax.ShapeDtypeStruct((rows, width), F32),
                struct((rows, width), BF),
                deal,
            ],
            (arrived2, state, low2, edges, pick, counts, *message_args, *feed_args, send, *edge_args),
            "layer_two",
            [pltpu.VMEM((rows, hidden), F32)],
        )
        arrived3 = exchange(away)
        wide = lambda dtype: struct((n_edges, edge_width), dtype)
        edge_result, edge_grad, act1, act2, top, mid, bottom, slot, node, edge_vec = call(
            edge_turn(rows, fanout, step),
            [
                jax.ShapeDtypeStruct((n_edges, edge_width), F32),
                wide(F32), wide(BF), wide(BF), wide(BF), wide(BF), wide(BF),
                [struct((buffer // len(deal), edge_width), BF)] * len(deal),
                struct((rows, edge_width), BF),
                struct((8, edge_width), F32),
            ],
            (arrived3, low3, edge_state, edge_up, pick, *edge_args),
            "edge_turn",
            [
                pltpu.VMEM((buffer, edge_width), F32),
                pltpu.VMEM((rows, edge_width), F32),
                pltpu.VMEM((4, 8, edge_width), F32),
            ],
        )
        returned = exchange(slot)
        head = 3 * edge_width + edge_width // 2
        (pack,) = call(
            edge_weights,
            [struct((head, width), BF)],
            (arrived3, low3, edge_state, act1, act2, top, mid, bottom, slot, node),
            "edge_weights",
        )
        sized = lambda n: -(-n // 128) * 128
        n_early, n_late = sized(head + hidden + 32), sized(mf.shape[0] + hidden + 16)
        cut = lambda n: [struct((n // 2, width), BF)] * 2 if tuned else [struct((n, width), BF)]
        feed_low, first_grad, pull, early = call(
            node_turn,
            [struct((rows, width), BF), struct((rows, width), F32), struct((rows, hidden), F32), cut(n_early)],
            (
                returned, node_up, node, send, second, slopes, first, counts, summed, ef, mt, mg, we, wr, fg,
                pack, edge_vec,
            ),
            "node_turn",
            [pltpu.VMEM((n_early, width), BF)],
            spot=spot,
        )
        if tuned:
            mids = [mid_low] + [to_hid(mid_low, m) for m in (1, 2, 3)]
            feeds = [feed_low] + [to_hid(feed_low, m) for m in (1, 2, 3)]
            early = reduced(spot, *early, True, "early")
        else:
            mids = [lax.all_gather(mid_low, "hid", axis=0, tiled=True)]
            feeds = [lax.all_gather(feed_low, "hid", axis=0, tiled=True)]
            early = [lax.psum(early[0].astype(F32), ("res", "hid"))]
        first_low, slot, node, late = call(
            message_turn(rows, fanout, step),
            [
                struct((n_edges, hidden), BF),
                [struct((buffer // len(deal), hidden), BF)] * len(deal),
                struct((rows, hidden), BF),
                cut(n_late),
            ],
            (arrived2, low2, edge_state, pick, pull, act, slope1, slope2, ms),
            "message_turn",
            [
                pltpu.VMEM((n_edges, hidden), BF),
                pltpu.VMEM((buffer, hidden), F32),
                pltpu.VMEM((rows, hidden), F32),
                pltpu.VMEM((rows, hidden), F32),
                pltpu.VMEM((n_late, hidden), BF),
            ],
            limit=16,
            spot=spot,
        )
        returned = exchange(slot)
        (feed_pay,) = call(
            feed_weights,
            [cut(2 * width) if tuned else [struct((width, share), BF), struct((share, width), BF)]],
            (mids, feeds, expand_weight, bias, reduce_weight),
            "feed_weights",
            [pltpu.VMEM((2 * width, width), BF)],
            spot=spot,
        )
        if tuned:
            late = reduced(spot, *late, True, "late")
            feed_parts = reduced(spot, *feed_pay, False, "feed")
        else:
            late = [lax.psum(late[0].astype(F32), ("res", "hid"))]
        (node_gradient,) = call(
            node_end,
            [jax.ShapeDtypeStruct((rows, width), F32)],
            (returned, send, first_grad, node, mf),
            "node_end",
        )
        (edge_gradient,) = call(
            edge_end(rows, fanout, step),
            [jax.ShapeDtypeStruct((n_edges, edge_width), F32)],
            (edge_grad, first_low, mf),
            "edge_end",
        )
        final = lambda *shape: jax.ShapeDtypeStruct(shape, F32)
        edge_first_grad, edge_second_grad, edge_third_grad, third_grad, vec = call(
            unpack_early,
            [
                final(edge_width, ef.shape[1]), final(edge_width, edge_width), final(edge_width, edge_width),
                final(hidden, width), final(32, width),
            ],
            (early,),
            "unpack_early",
            [pltpu.VMEM((n_early, width), F32)],
            spot=spot,
        )
        first_weight_grad, second_weight_grad, message_vec = call(
            unpack_late,
            [final(*mf.shape), final(hidden, hidden), final(16, hidden)],
            (late,),
            "unpack_late",
            [pltpu.VMEM((n_late, width), F32)],
            spot=spot,
        )
        if tuned:
            expand_grad, reduce_grad = call(
                unpack_feed,
                [final(width, share), final(share, width)],
                (feed_parts,),
                "unpack_feed",
                [pltpu.VMEM((2 * width, width), F32)],
                spot=spot,
            )
        else:
            expand_grad, reduce_grad = [lax.psum(v.astype(F32), "res") for v in feed_pay]
        bias_rows = lax.dynamic_index_in_dim(vec, 6 + lax.axis_index("hid"), 0, keepdims=False)
        edge_vecs = vec[16:24, :edge_width]

        back = lambda v: v.reshape(fanout, rows, edge_width).transpose(1, 0, 2)
        return (
            node_result,
            back(edge_result),
            node_gradient,
            back(edge_gradient),
            first_weight_grad,
            message_vec[0],
            second_weight_grad,
            message_vec[1],
            third_grad,
            vec[5],
            vec[3],
            vec[4],
            expand_grad,
            bias_rows[:share],
            reduce_grad,
            vec[0],
            vec[1],
            vec[2],
            edge_first_grad.T,
            edge_vecs[4],
            edge_second_grad,
            edge_vecs[3],
            edge_third_grad,
            edge_vecs[2],
            edge_vecs[0],
            edge_vecs[1],
        )

    both = ("res", "hid")
    rows2, rows3 = P(both, None), P(both, None, None)
    placed = (
        rows2, rows3, rows3, rows2, P(both),
        P(), P(), P(), P(), P(), P(), P(), P(),
        P(None, "hid"), P("hid"), P("hid", None),
        P(), P(), P(), P(), P(), P(), P(), P(), P(), P(), P(),
        rows2, rows3,
    )
    given = (
        rows2, rows3, rows2, rows3,
        P(), P(), P(), P(), P(), P(), P(), P(),
        P(None, "hid"), P("hid"), P("hid", None),
        P(), P(), P(), P(), P(), P(), P(), P(), P(), P(), P(),
    )
    return jax.shard_map(body, mesh=mesh, in_specs=placed, out_specs=given, check_vma=False)
```

```python
import jax
import jax.numpy as jnp
from jax import lax
from jax.experimental import pallas as pl
from jax.experimental.pallas import tpu as pltpu
from jax.sharding import PartitionSpec as P

BF = jnp.bfloat16
F32 = jnp.float32
LEAN = 0.7978845608028654
CUBE = LEAN * 0.044715
MIB = 1 << 20
KEEP = pl.BlockSpec(memory_space=pltpu.VMEM)


def dot(left, right):
    return jnp.dot(left, right, preferred_element_type=F32)


def dot_nt(left, right):
    return lax.dot_general(left, right, (((1,), (1,)), ((), ())), preferred_element_type=F32)


def dot_tn(left, right):
    return lax.dot_general(left, right, (((0,), (0,)), ((), ())), preferred_element_type=F32)


def smooth(v):
    t = jnp.tanh(v * (LEAN + CUBE * (v * v)))
    half = 0.5 * v
    return half + half * t


def smooth_slope(v):
    v2 = v * v
    t = jnp.tanh(v * (LEAN + CUBE * v2))
    half = 0.5 * v
    slope = (0.5 + 0.5 * t) + (half - half * (t * t)) * (LEAN + (3.0 * CUBE) * v2)
    return half + half * t, slope


def centred(x):
    center = x - jnp.mean(x, axis=-1, keepdims=True)
    rate = lax.rsqrt(jnp.mean(center * center, axis=-1, keepdims=True) + 1e-05)
    return center * rate, rate


def norm_pull(hat, rate, gain, up):
    g = up * gain
    return rate * (
        g - jnp.mean(g, axis=-1, keepdims=True) - hat * jnp.mean(g * hat, axis=-1, keepdims=True)
    )


def tiled_add(rows, part):
    n, width = part.shape
    return (rows.reshape(-1, n, width) + part[None]).reshape(rows.shape)


def over(count, chunk):
    if count == 1:
        chunk(0, 0)
    else:
        lax.fori_loop(0, count, chunk, 0)


def aligned(index, size):
    return index if isinstance(index, int) else pl.multiple_of(index, size)


def fold(rows, n):
    return jnp.sum(rows.reshape(-1, n, rows.shape[-1]), axis=0)


class Final:
    def __init__(self, *shape):
        self.shape, self.dtype = shape, F32


def call(body, outs, args, name, scratch=(), limit=28, spot=None, after=(), far=False, token=False):
    if token:
        outs = list(outs) + [pltpu.VMEM((8, 128), F32)]
    flat_outs, out_tree = jax.tree.flatten(list(outs), is_leaf=lambda v: hasattr(v, "dtype"))
    ends = [k for k, v in enumerate(flat_outs) if isinstance(v, Final)]
    held_outs = [pltpu.VMEM(flat_outs[k].shape, flat_outs[k].dtype) for k in ends]
    if ends:
        held_outs.append(pltpu.SemaphoreType.DMA((len(ends),)))
    shapes = [pltpu.HBM(v.shape, v.dtype) if isinstance(v, Final) else v for v in flat_outs]
    out_specs = [pl.BlockSpec(memory_space=pltpu.HBM) if isinstance(v, Final) else KEEP for v in flat_outs]
    space = pltpu.HBM if far else pltpu.VMEM
    args = jax.tree.map(lambda v: pltpu.with_memory_space_constraint(v, space), list(args))
    specs = jax.tree.map(lambda v: pl.BlockSpec(memory_space=space), args)
    lead = 0
    if spot is not None:
        args, specs, lead = [spot] + args, [pl.BlockSpec(memory_space=pltpu.SMEM)] + specs, 1
    n, more = len(args), len(after)
    scratch = list(scratch)
    if far:
        flat, tree = jax.tree.flatten(args[lead:])
        scratch += [pltpu.VMEM(v.shape, v.dtype) for v in flat] + [pltpu.SemaphoreType.DMA((len(flat),))]

    def run(*refs):
        given, rest = refs[:n], refs[n + more :]
        results, rest = list(jax.tree.leaves(list(rest[: len(outs)]))), rest[len(outs) :]
        targets = [results[k] for k in ends]
        if ends:
            rest, kept, out_sems = rest[: -len(ends) - 1], rest[-len(ends) - 1 : -1], rest[-1]
            for k, v in zip(ends, kept):
                results[k] = v
        if far:
            count = len(flat)
            rest, held, sems = rest[: -count - 1], rest[-count - 1 : -1], rest[-1]
            copies = [
                pltpu.make_async_copy(src, dst, sems.at[k])
                for k, (src, dst) in enumerate(zip(jax.tree.leaves(list(given[lead:])), held))
            ]
            for copy in copies:
                copy.start()
            for copy in copies:
                copy.wait()
            given = list(given[:lead]) + jax.tree.unflatten(tree, held)
        produced = list(jax.tree.unflatten(out_tree, results))
        if token:
            produced.pop()[...] = jnp.zeros((8, 128), F32)
        body(*given, *produced, *rest)
        if ends:
            copies = [
                pltpu.make_async_copy(src, dst, out_sems.at[k])
                for k, (src, dst) in enumerate(zip(kept, targets))
            ]
            for copy in copies:
                copy.start()
            for copy in copies:
                copy.wait()

    return pl.pallas_call(
        run,
        out_shape=jax.tree.unflatten(out_tree, shapes),
        in_specs=specs + [pl.BlockSpec(memory_space=pl.ANY)] * more,
        out_specs=jax.tree.unflatten(out_tree, out_specs),
        scratch_shapes=scratch + held_outs,
        compiler_params=pltpu.CompilerParams(vmem_limit_bytes=limit * MIB),
        name=name,
    )(*args, *after)


def struct(shape, dtype):
    return pltpu.VMEM(shape, dtype)


def shards(own, packed):
    if len(packed) == 3:
        we, web, wr = packed
        for h in range(we.shape[0]):
            yield we[h], web[h : h + 1, :], wr[h]
        return
    yield own[0][...], own[1][...], own[2][...]
    (ref,) = packed
    n, width = ref.shape[0] // 8, ref.shape[1] // 3
    part = n // 9 * 4
    for h in range(3):
        at = slice(h * width, (h + 1) * width)
        we = jnp.concatenate([ref[r * n : r * n + part, at] for r in range(8)], axis=0)
        wr = jnp.concatenate([ref[r * n + part : r * n + 2 * part, at] for r in range(8)], axis=0)
        bias = ref[2 * part : n, at].astype(F32)
        yield we, bias[0:1] + bias[1:2], wr


def feed(mid, own, packed, rb, slopes):
    mid_low = mid.astype(BF)
    total = mid + rb
    for h, (we, web, wr) in enumerate(shards(own, packed)):
        act, slope = smooth_slope(dot(mid_low, we) + web)
        slopes[h] = slope.astype(BF)
        total = total + dot(act.astype(BF), wr)
    return mid_low, total


def joined(parts):
    if len(parts) == 1:
        return parts[0][...]
    near, far = parts[: len(parts) // 2], parts[len(parts) // 2 :]
    rows = []
    for mine, other in zip(near, far):
        half = mine.shape[0] // 2
        rows += [mine[:half], other[half:]]
    return jnp.concatenate(rows, axis=0)


def dealt(outs, value):
    n = value.shape[0] // len(outs)
    for m, out in enumerate(outs):
        out[...] = value[m * n : (m + 1) * n].astype(out.dtype)


def halved(spot, pay, keep, send):
    n = keep.shape[0] // 4
    for m in range(4):
        chip = (spot[1] ^ m) * 2
        keep[m * n : (m + 1) * n, :] = pay[pl.ds(pl.multiple_of((chip + spot[0]) * n, n), n), :]
        send[m * n : (m + 1) * n, :] = pay[pl.ds(pl.multiple_of((chip + 1 - spot[0]) * n, n), n), :]


def message_mean(summed, counts, mt, mtb):
    mean = summed / counts
    high = mean.astype(BF)
    rest = (mean - high.astype(F32)).astype(BF)
    return dot(high, mt) + dot(rest, mt) + mtb


def solution(mesh):
    n_res, n_hid = mesh.shape["res"], mesh.shape["hid"]
    tuned = (n_res, n_hid) == (8, 4)
    pair = [(i, i ^ 1) for i in range(n_res)]

    def to_chip(v, m):
        return lax.ppermute(v, "res", [(i, i ^ (2 * m)) for i in range(n_res)])

    def to_core(v):
        return lax.ppermute(v, "res", pair)

    def to_hid(v, m):
        return lax.ppermute(v, "hid", [(i, i ^ m) for i in range(n_hid)])

    def exchange(parts):
        if not tuned:
            n, width = parts[0].shape
            blocks = parts[0].reshape(n_res, n // n_res, width)
            return [lax.all_to_all(blocks, "res", 0, 0, tiled=True).reshape(n, width)]
        near = [parts[0]] + [to_chip(parts[m], m) for m in (1, 2, 3)]
        return near + [to_core(v) for v in near]

    def prepare_send(spot, table, nodes, weights, away_out, send_out, piece_out):
        rows, width = nodes.shape
        n = table.shape[1]
        lines = lax.broadcasted_iota(jnp.int32, (rows, n), 0)
        same = lax.broadcasted_iota(jnp.int32, (rows, rows), 0) == lax.broadcasted_iota(
            jnp.int32, (rows, rows), 1
        )
        same = same.astype(F32).astype(BF)
        each = n_res // len(away_out)
        for q in range(n_res):
            line = table[pl.ds(q ^ spot[3], 1), :]
            chosen = (lines == line).astype(F32).astype(BF)
            at = slice(q % each * n, (q % each + 1) * n)
            away_out[q // each][at, :] = dot_tn(chosen, nodes[...]).astype(BF)
            send_out[q * n : (q + 1) * n, :] = dot_tn(chosen, same).astype(BF)
        if piece_out:
            (out,) = piece_out
            we, wr, bias = weights
            n = width // 8
            at = pl.ds(pl.multiple_of(spot[3] * n, n), n)
            out[:n, :] = we[at, :]
            out[n : 2 * n, :] = wr[at, :]
            high = bias[...].astype(BF).astype(F32)
            rest = jnp.concatenate([high, bias[...] - high, jnp.zeros((n // 4 - 2, width), F32)], axis=0)
            out[2 * n :, :] = rest.astype(BF)

    def prepare_rest(spot, slots, counts, vecs, edge_vecs, pick_out, counts_out, vecs_out, edge_out):
        rows, fanout = slots.shape
        lanes = lax.broadcasted_iota(jnp.int32, (rows, pick_out.shape[1]), 1)
        moved = slots[...] ^ (spot[3] * (pick_out.shape[1] // n_res))
        for k in range(fanout):
            chosen = (lanes == moved[:, k : k + 1]).astype(F32).astype(BF)
            pick_out[k * rows : (k + 1) * rows, :] = chosen
        same = lax.broadcasted_iota(jnp.int32, (rows, rows), 0) == lax.broadcasted_iota(
            jnp.int32, (rows, rows), 1
        )
        many = jnp.where(same, jnp.broadcast_to(counts[...].astype(F32), (rows, rows)), 0.0)
        counts_out[...] = jnp.sum(many, axis=1, keepdims=True)
        edge_out[...] = jnp.zeros_like(edge_out)
        for k, v in enumerate(vecs):
            vecs_out[k : k + 1, :] = v[...]
        for k, v in enumerate(edge_vecs):
            edge_out[k : k + 1, :] = v[...]

    def pass_one(rows, fanout, step):
        span = step * rows

        def kernel(
            arrived, nodes, edges, pick, counts, mf, ms, mt, vecs, mid_out, sums,
        ):
            mfb, msb, mtb, mg, msh = [vecs[k : k + 1, :] for k in range(5)]
            width = nodes.shape[1]
            query = dot(joined(arrived), mf[width : 2 * width]).astype(BF)
            part = dot(nodes[...], mf[:width]) + mfb
            lower = mf[2 * width :]
            lots = jnp.broadcast_to(counts[...], (rows, ms.shape[1]))
            sums[...] = jnp.zeros_like(sums)

            def chunk(i, carry):
                at = pl.ds(aligned(i * span, span), span)
                pre = dot(pick[at, :], query) + dot(edges[at, :], lower)
                act = smooth(tiled_add(pre, part)).astype(BF)
                act = smooth(dot(act, ms[...]) + msb)
                total = sums[...]
                for j in range(step):
                    total = total + jnp.where(
                        lots > jnp.float32(i * step + j), act[j * rows : (j + 1) * rows], 0.0
                    )
                sums[...] = total
                return carry

            over(fanout // step, chunk)
            first = nodes[...].astype(F32) + message_mean(sums[...], counts[...], mt[...], mtb)
            mid_out[...] = centred(first)[0] * mg + msh

        return kernel

    def feed_pass(mid, own, packed, vecs, send, slopes_out, second_out, new_out, low_out, away_out):
        rb, fg, fsh = [vecs[k : k + 1, :] for k in (5, 6, 7)]
        _, second = feed(mid[...], own, packed, rb, slopes_out)
        second_out[...] = second
        new = centred(second)[0] * fg + fsh
        new_out[...] = new
        low = new.astype(BF)
        low_out[...] = low
        dealt(away_out, dot(send[...], low))

    def pass_two(rows, fanout, step):
        span = step * rows

        def kernel(
            arrived, state, low, edges, pick, counts, mf, ms, mt, vecs, ef, es, et, edge_vecs,
            edge_out, act_out, slope1_out, slope2_out, first_out, summed_out, mid_out, mid_low_out, sums,
        ):
            mfb, msb, mtb, mg, msh = [vecs[k : k + 1, :] for k in range(5)]
            efb, esb, etb, eg, esh = [edge_vecs[k : k + 1, :] for k in range(5)]
            width = state.shape[1]
            received = joined(arrived)
            key = dot_nt(received, ef[:, width : 2 * width]).astype(BF)
            edge_part = dot_nt(low[...], ef[:, :width]) + efb
            edge_lower = ef[:, 2 * width :]
            query = dot(received, mf[width : 2 * width]).astype(BF)
            part = dot(low[...], mf[:width]) + mfb
            lower = mf[2 * width :]
            lots = jnp.broadcast_to(counts[...], (rows, ms.shape[1]))
            sums[...] = jnp.zeros_like(sums)

            def chunk(i, carry):
                at = pl.ds(aligned(i * span, span), span)
                chosen = pick[at, :]
                old = edges[at, :]
                pre = dot(chosen, key) + dot_nt(old, edge_lower)
                act = smooth(tiled_add(pre, edge_part)).astype(BF)
                act = smooth(dot(act, es[...]) + esb).astype(BF)
                total = old.astype(F32) + dot(act, et[...]) + etb
                fresh = centred(total)[0] * eg + esh
                edge_out[at, :] = fresh
                pre = dot(chosen, query) + dot(fresh.astype(BF), lower)
                act, slope = smooth_slope(tiled_add(pre, part))
                act = act.astype(BF)
                act_out[at, :] = act
                slope1_out[at, :] = slope.astype(BF)
                act, slope = smooth_slope(dot(act, ms[...]) + msb)
                total = sums[...]
                for j in range(step):
                    valid = lots > jnp.float32(i * step + j)
                    total = total + jnp.where(valid, act[j * rows : (j + 1) * rows], 0.0)
                    slope2_out[pl.ds(aligned(i * span + j * rows, rows), rows), :] = jnp.where(
                        valid, slope[j * rows : (j + 1) * rows], 0.0
                    ).astype(BF)
                sums[...] = total
                return carry

            over(fanout // step, chunk)
            summed_out[...] = sums[...].astype(BF)
            first = state[...] + message_mean(sums[...], counts[...], mt[...], mtb)
            first_out[...] = first
            mid = centred(first)[0] * mg + msh
            mid_out[...] = mid
            mid_low_out[...] = mid.astype(BF)

        return kernel

    def edge_turn(rows, fanout, step):
        span = step * rows

        def kernel(
            arrived, low, edges, up, pick, ef, es, et, edge_vecs,
            result_out, grad_out, act1_out, act2_out, top_out, mid_out, bottom_out,
            slot_out, node_out, vec_out, slots, node, marks,
        ):
            width = low.shape[1]
            efb, esb, etb, eg, esh = [edge_vecs[k : k + 1, :] for k in range(5)]
            key = dot_nt(joined(arrived), ef[:, width : 2 * width]).astype(BF)
            edge_part = dot_nt(low[...], ef[:, :width]) + efb
            edge_lower = ef[:, 2 * width :]
            slots[...] = jnp.zeros_like(slots)
            node[...] = jnp.zeros_like(node)
            marks[...] = jnp.zeros_like(marks)

            def chunk(i, carry):
                at = pl.ds(aligned(i * span, span), span)
                chosen = pick[at, :]
                old = edges[at, :]
                pre = dot(chosen, key) + dot_nt(old.astype(BF), edge_lower)
                act, slope1 = smooth_slope(tiled_add(pre, edge_part))
                act1 = act.astype(BF)
                act1_out[at, :] = act1
                act, slope2 = smooth_slope(dot(act1, es[...]) + esb)
                act2 = act.astype(BF)
                act2_out[at, :] = act2
                total = old + dot(act2, et[...]) + etb
                hat, rate = centred(total)
                result_out[at, :] = hat * eg + esh
                above = up[at, :].astype(F32)
                sum_grad = norm_pull(hat, rate, eg, above)
                top = sum_grad.astype(BF)
                top_out[at, :] = top
                mid = dot_nt(top, et[...]) * slope2
                mid_low = mid.astype(BF)
                mid_out[at, :] = mid_low
                bottom = dot_nt(mid_low, es[...]) * slope1
                bottom_low = bottom.astype(BF)
                bottom_out[at, :] = bottom_low
                grad_out[at, :] = sum_grad + dot(bottom_low, edge_lower)
                marks[0] += fold(above * hat, 8)
                marks[1] += fold(above, 8)
                marks[2] += fold(sum_grad, 8)
                marks[3] += fold(mid, 8)
                node[...] += fold(bottom, rows)
                slots[...] += dot_tn(chosen, bottom_low)
                return carry

            over(fanout // step, chunk)
            dealt(slot_out, slots[...])
            node_out[...] = node[...].astype(BF)
            vec_out[...] = jnp.zeros_like(vec_out)
            for j in range(4):
                vec_out[j : j + 1, :] = jnp.sum(marks[j], axis=0, keepdims=True)
            vec_out[4:5, :] = jnp.sum(node[...], axis=0, keepdims=True)

        return kernel

    def edge_weights(arrived, low, edges, act1, act2, top, mid, bottom, slot, node, pack_out):
        n, wide = act1.shape[1], low.shape[1]
        slot = jnp.concatenate([v[...] for v in slot], axis=0)
        pack_out[:n, :] = dot_tn(node[...], low[...]).astype(BF)
        pack_out[n : 2 * n, :] = dot_tn(slot, joined(arrived)).astype(BF)
        pack_out[2 * n :, :] = jnp.zeros((pack_out.shape[0] - 2 * n, wide), BF)
        pack_out[2 * n : 3 * n, :n] = dot_tn(act1[...], mid[...]).astype(BF)
        pack_out[2 * n : 3 * n, 256 : 256 + n] = dot_tn(act2[...], top[...]).astype(BF)
        lower = dot_tn(bottom[...], edges[...].astype(BF)).astype(BF)
        pack_out[3 * n :, :n] = lower[: n // 2]
        pack_out[3 * n :, 256 : 256 + n] = lower[n // 2 :]

    def node_turn(
        spot, returned, up, node, send, second, slopes, first, counts, summed, ef, mt, vecs,
        own, packed, pack, edge_vec, mid_low, pair_out, sum_out, pull_out, pay_out, pay,
    ):
        width = up.shape[1]
        key_low = dot_tn(send[...], joined(returned)).astype(BF)
        new_grad = (
            up[...].astype(F32) + dot(node[...], ef[:, :width]) + dot(key_low, ef[:, width : 2 * width])
        )
        hat, rate = centred(second[...])
        sum_grad = norm_pull(hat, rate, vecs[6:7, :], new_grad)
        marks = [sum_grad, new_grad * hat, new_grad]
        low = sum_grad.astype(BF)
        pair_out[:, :width] = mid_low[...]
        pair_out[:, width:] = low
        mid_grad = sum_grad
        bias = []
        for h, (we, _, wr) in enumerate(shards(own, packed)):
            expand = dot_nt(low, wr) * slopes[h].astype(F32)
            bias.append(jnp.sum(expand, axis=0, keepdims=True))
            mid_grad = mid_grad + dot_nt(expand.astype(BF), we)
        hat, rate = centred(first[...])
        first_grad = norm_pull(hat, rate, vecs[3:4, :], mid_grad)
        sum_out[...] = first_grad
        marks += [mid_grad * hat, mid_grad, first_grad]
        marks = [jnp.sum(v, axis=0, keepdims=True) for v in marks]
        rows_low = (first_grad / counts[...]).astype(BF)
        pull_out[...] = dot_nt(rows_low, mt[...])
        third = dot_tn(summed[...], rows_low).astype(BF)
        head, hidden = pack.shape[0], third.shape[0]
        pay[:head, :] = pack[...]
        pay[head : head + hidden, :] = third
        pay[head + hidden :, :] = jnp.zeros((pay.shape[0] - head - hidden, width), BF)
        rows = jnp.concatenate(marks + [jnp.zeros((10, width), F32)], axis=0)
        at = lax.broadcasted_iota(jnp.int32, rows.shape, 0)
        share = bias[0].shape[1]
        for h, v in enumerate(bias):
            line = 6 + ((spot[2] ^ h) if tuned else h)
            if share < width:
                v = jnp.concatenate([v, jnp.zeros((1, width - share), F32)], axis=1)
            rows = jnp.where(at == line, v, rows)
        pay[head + hidden : head + hidden + 16, :] = rows.astype(BF)
        pay[head + hidden + 16 : head + hidden + 32, : edge_vec.shape[1]] = jnp.concatenate(
            [edge_vec[...], jnp.zeros_like(edge_vec)], axis=0
        ).astype(BF)
        if len(pay_out) == 1:
            pay_out[0][...] = pay[...]
        else:
            halved(spot, pay, *pay_out)

    def message_second(rows, fanout, step):
        span = step * rows

        def kernel(pull, act, slope2, second_out, weight_out, vec_out, marks):
            marks[...] = jnp.zeros_like(marks)

            def chunk(i, carry):
                at = pl.ds(aligned(i * span, span), span)
                second = slope2[at, :].astype(F32).reshape(step, rows, -1) * pull[...][None]
                marks[...] += jnp.sum(second, axis=0)
                second_out[at, :] = second.reshape(span, -1).astype(BF)
                return carry

            over(fanout // step, chunk)
            weight_out[...] = dot_tn(act[...], second_out[...]).astype(BF)
            vec_out[...] = jnp.zeros_like(vec_out)
            vec_out[0:1, :] = jnp.sum(marks[...], axis=0, keepdims=True)

        return kernel

    def message_first(rows, fanout, step):
        span = step * rows

        def kernel(
            arrived, low, edges, pick, second, slope1, ms, weight, vec,
            first_low_out, slot_out, node_out, pay, slots, node,
        ):
            width = low.shape[1]
            slots[...] = jnp.zeros_like(slots)
            node[...] = jnp.zeros_like(node)

            def chunk(i, carry):
                at = pl.ds(aligned(i * span, span), span)
                first = dot_nt(second[at, :], ms[...]) * slope1[at, :].astype(F32)
                node[...] += fold(first, rows)
                first = first.astype(BF)
                first_low_out[at, :] = first
                slots[...] += dot_tn(pick[at, :], first)
                return carry

            over(fanout // step, chunk)
            slot = slots[...].astype(BF)
            dealt(slot_out, slot)
            node_low = node[...].astype(BF)
            node_out[...] = node_low
            hidden, last = ms.shape[0], 2 * width + edges.shape[1]
            pay[:width, :] = dot_tn(low[...], node_low).astype(BF)
            pay[width : 2 * width, :] = dot_tn(joined(arrived), slot).astype(BF)
            pay[2 * width : last, :] = dot_tn(edges[...].astype(BF), first_low_out[...]).astype(BF)
            pay[last : last + hidden, :] = weight[...]
            pay[last + hidden :, :] = jnp.zeros((pay.shape[0] - last - hidden, hidden), BF)
            vecs = [jnp.sum(node[...], axis=0, keepdims=True), vec[0:1, :], jnp.zeros((14, hidden), F32)]
            pay[last + hidden : last + hidden + 16, :] = jnp.concatenate(vecs, axis=0).astype(BF)

        return kernel

    def feed_weights(pairs, we, web, wr, pay_out):
        n, share = we.shape
        mid = jnp.concatenate([v[:, :n] for v in pairs], axis=0)
        up = jnp.concatenate([v[:, n:] for v in pairs], axis=0)
        act, slope = smooth_slope(dot(mid, we[...]) + web[...])
        expand = dot_nt(up, wr[...]) * slope
        expand = dot_tn(mid, expand.astype(BF)).astype(BF)
        reduce = dot_tn(act.astype(BF), up).astype(BF)
        if len(pay_out) == 2:
            pay_out[0][...], pay_out[1][...] = expand, reduce
        else:
            pay_out[0][:n, :] = expand
            pay_out[0][n:, :] = reduce

    def node_end(returned, send, first_grad, node, mf, out):
        width = out.shape[1]
        if len(returned) == 2:
            mine, twin = returned
            n = mine.shape[0] // 4
            rows = [v[m * n : (m + 1) * n, :] for m in range(4) for v in (mine, twin)]
            back = jnp.concatenate(rows, axis=0)
        else:
            back = joined(returned)
        query_low = dot_tn(send[...], back).astype(BF)
        out[...] = (
            first_grad[...] + dot_nt(node[...], mf[:width]) + dot_nt(query_low, mf[width : 2 * width])
        )

    def edge_end(rows, fanout, step):
        span = step * rows

        def kernel(grad, first_low, mf, out):
            lower = mf[mf.shape[0] - grad.shape[1] :]

            def chunk(i, carry):
                at = pl.ds(aligned(i * span, span), span)
                out[at, :] = grad[at, :] + dot_nt(first_low[at, :], lower)
                return carry

            over(fanout // step, chunk)

        return kernel

    def split_chips(keep, got, outs):
        n = keep.shape[0] // len(outs)
        for m, out in enumerate(outs):
            at = slice(m * n, (m + 1) * n)
            out[:n, :] = (keep[at, :].astype(F32) + got[at, :].astype(F32)).astype(BF)

    def split_chips_more(keep, got, more, outs):
        split_chips(keep, got, outs)
        for v, out in zip(more, outs):
            out[out.shape[0] - v.shape[0] :, :] = v[...]

    def add_up(parts, out):
        n = out.shape[0]
        total = parts[0][:n, :].astype(F32)
        for v in parts[1:]:
            total = total + v[:n, :].astype(F32)
        out[...] = total.astype(BF)

    def add_up_more(parts, out, mine, twin):
        add_up(parts, out)
        n = mine.shape[0] // len(parts)
        for m, v in enumerate(parts):
            at, top = slice(m * n, (m + 1) * n), out.shape[0]
            mine[at, :] = v[top : top + n, :]
            twin[at, :] = v[top + n : top + 2 * n, :]

    def add_two(left, right, more, out):
        n = left.shape[0]
        out[:n, :] = (left[...].astype(F32) + right[...].astype(F32)).astype(BF)
        if more:
            out[n:, :] = more[0][...]

    def to_chips(parts):
        return [parts[0]] + [to_chip(parts[m], m) for m in (1, 2, 3)]

    def spread(own):
        parts = [own] + [to_chip(own, m) for m in (1, 2, 3)]
        return parts + [to_core(v) for v in parts]

    def laid_out(spot, parts, total):
        n = parts[0].shape[0]
        for k, v in enumerate(parts):
            at = (2 * (spot[1] ^ (k % 4)) + (spot[0] ^ (k // 4))) * n
            total[pl.ds(pl.multiple_of(at, n), n), :] = v[...].astype(total.dtype)

    def lay_pair(spot, stacks, total, skip=0):
        n = total.shape[0] // 8
        step = stacks[0].shape[0] // 4
        for k in range(8):
            at = (2 * (spot[1] ^ (k % 4)) + (spot[0] ^ (k // 4))) * n
            top = k % 4 * step + skip
            total[pl.ds(pl.multiple_of(at, n), n), :] = stacks[k // 4][top : top + n, :].astype(total.dtype)

    def stack_up(parts, out):
        n = parts[0].shape[0]
        for m, v in enumerate(parts):
            out[m * n : (m + 1) * n, :] = v[...]

    def unpack_early(
        spot, parts, first_out, second_out, third_out, message_out, vec_out, edge_vec_out, bias_out, feed_out,
        total, rest,
    ):
        if len(parts) == 1:
            total[...] = parts[0][...]
        else:
            lay_pair(spot, parts, total)
            lay_pair(spot, parts, rest, total.shape[0] // 8)
            n = rest.shape[0] // 2
            feed_out[0][...] = rest[:n, :]
            feed_out[1][...] = rest[n:, :]
        n, wide = second_out.shape[0], message_out.shape[1]
        first_out[:, :wide] = total[:n, :]
        first_out[:, wide : 2 * wide] = total[n : 2 * n, :]
        second_out[...] = total[2 * n : 3 * n, :n]
        third_out[...] = total[2 * n : 3 * n, 256 : 256 + n]
        at = 3 * n + n // 2
        first_out[: n // 2, 2 * wide :] = total[3 * n : at, :n]
        first_out[n // 2 :, 2 * wide :] = total[3 * n : at, 256 : 256 + n]
        hidden = message_out.shape[0]
        message_out[...] = total[at : at + hidden, :]
        for k, out in enumerate(vec_out):
            out[...] = total[at + hidden + k : at + hidden + k + 1, :]
        for k, out in enumerate(edge_vec_out):
            out[...] = total[at + hidden + 16 + k : at + hidden + 17 + k, :n]
        vecs = total[at + hidden : at + hidden + 16, :]
        line = lax.broadcasted_iota(jnp.int32, vecs.shape, 0) == 6 + spot[2]
        bias = jnp.sum(jnp.where(line, vecs, 0.0), axis=0, keepdims=True)
        bias_out[...] = bias[:, : bias_out.shape[1]]

    def unpack_late(spot, parts, first_out, second_out, vec_out, total):
        if len(parts) == 1:
            total[...] = parts[0][...]
        else:
            lay_pair(spot, parts, total)
        n, hidden = first_out.shape[0], second_out.shape[0]
        first_out[...] = total[:n, :]
        second_out[...] = total[n : n + hidden, :]
        for k, out in enumerate(vec_out):
            out[...] = total[n + hidden + k : n + hidden + k + 1, :]

    def join_pieces(parts, out):
        for m, v in enumerate(parts):
            n = v.shape[1]
            out[:, m * n : (m + 1) * n] = v[...]

    def body(
        nodes, edges, send_rows, neighbor_slots, neighbor_counts, mf, mfb, ms, msb, mt, mtb, mg, msh,
        expand_weight, expand_bias, reduce_weight, rb, fg, fsh, ef, efb, es, esb, et, etb, eg, esh,
        node_up, edge_up,
    ):
        rows, fanout, edge_width = edges.shape
        width, hidden = nodes.shape[1], ms.shape[0]
        share = expand_weight.shape[1]
        n_edges = rows * fanout
        step, half_step = fanout, fanout // 2 if fanout % 2 == 0 else fanout
        slots_each = send_rows.shape[2]
        buffer = n_res * slots_each
        row = lambda v: v.reshape(1, -1)
        if tuned:
            res, hid = lax.axis_index("res"), lax.axis_index("hid")
            spot = jnp.stack([res % 2, res // 2, hid, res]).astype(jnp.int32)
        else:
            spot = jnp.stack([0, 0, lax.axis_index("hid"), 0]).astype(jnp.int32)
        edges = edges.transpose(1, 0, 2).reshape(n_edges, edge_width)
        edge_up = edge_up.transpose(1, 0, 2).reshape(n_edges, edge_width)
        ef = ef.T
        bias = row(expand_bias)
        own = (expand_weight, bias, reduce_weight)
        one = struct((rows, width), BF)
        deal = [one] * 4 if tuned else [struct((buffer, width), BF)]
        n_piece = width // 8 * 9 // 4
        away, send, piece = call(
            prepare_send,
            [deal, struct((buffer, rows), BF), [struct((n_piece, width), BF)] if tuned else []],
            (send_rows[0], nodes, (expand_weight, reduce_weight, bias) if tuned else ()),
            "prepare_send",
            spot=spot,
            far=True,
        )
        arrived = exchange(away)
        pick, counts, vecs, edge_vecs = call(
            prepare_rest,
            [
                struct((n_edges, buffer), BF),
                struct((rows, 1), F32),
                struct((8, width), F32),
                struct((8, edge_width), F32),
            ],
            (
                neighbor_slots,
                row(neighbor_counts),
                [row(v) for v in (mfb, msb, mtb, mg, msh, rb, fg, fsh)],
                [row(v) for v in (efb, esb, etb, eg, esh)],
            ),
            "prepare_rest",
            spot=spot,
            after=away[:1],
            far=True,
        )
        edge_args = (ef, es, et, edge_vecs)
        if tuned:
            pieces = [to_hid(piece[0], m) for m in (1, 2, 3)]
            (piece,) = call(
                join_pieces, [struct((n_piece, 3 * width), BF)], (pieces,), "join_pieces", after=arrived
            )
            packed, first = [piece] + [to_chip(piece, m) for m in (1, 2, 3)], [piece]
        else:
            packed, first = [
                lax.all_gather(expand_weight, "hid"),
                lax.all_gather(expand_bias, "hid"),
                lax.all_gather(reduce_weight, "hid"),
            ], []
        (mid,) = call(
            pass_one(rows, fanout, step),
            [struct((rows, width), F32)],
            (arrived, nodes, edges, pick, counts, mf, ms, mt, vecs),
            "message_one",
            [pltpu.VMEM((rows, hidden), F32)],
            after=first,
        )
        if tuned:
            (packed,) = call(
                stack_up, [struct((4 * n_piece, 3 * width), BF)], (packed,), "stack_weights", after=[mid]
            )
            (packed,) = call(
                lay_pair,
                [struct((8 * n_piece, 3 * width), BF)],
                ([packed, to_core(packed)],),
                "lay_weights",
                spot=spot,
            )
            packed = [packed]
        feed_outs = [
            struct((n_hid, rows, share), BF),
            struct((rows, width), F32),
            struct((rows, width), F32),
            one,
            deal,
        ]
        _, _, state, low, away = call(
            feed_pass, feed_outs, (mid, own, packed, vecs, send), "feed_one"
        )
        arrived2, low2 = exchange(away), low
        edge_state, act, slope1, slope2, first, summed, mid, mid_low = call(
            pass_two(rows, fanout, step),
            [
                struct((n_edges, edge_width), F32),
                struct((n_edges, hidden), BF),
                struct((n_edges, hidden), BF),
                struct((n_edges, hidden), BF),
                struct((rows, width), F32),
                struct((rows, hidden), BF),
                struct((rows, width), F32),
                one,
            ],
            (arrived2, state, low2, edges, pick, counts, mf, ms, mt, vecs, *edge_args),
            "layer_two",
            [pltpu.VMEM((rows, hidden), F32)],
        )
        feed_outs[2] = jax.ShapeDtypeStruct((rows, width), F32)
        slopes, second, node_result, low3, away = call(
            feed_pass, feed_outs, (mid, own, packed, vecs, send), "feed_two"
        )
        arrived3 = exchange(away)
        wide = lambda dtype: struct((n_edges, edge_width), dtype)
        edge_result, edge_grad, act1, act2, top, mid, bottom, slot, node, edge_vec = call(
            edge_turn(rows, fanout, half_step),
            [
                jax.ShapeDtypeStruct((n_edges, edge_width), F32),
                wide(F32), wide(BF), wide(BF), wide(BF), wide(BF), wide(BF),
                [struct((buffer // len(deal), edge_width), BF)] * len(deal),
                struct((rows, edge_width), BF),
                struct((8, edge_width), F32),
            ],
            (arrived3, low3, edge_state, edge_up, pick, *edge_args),
            "edge_turn",
            [
                pltpu.VMEM((buffer, edge_width), F32),
                pltpu.VMEM((rows, edge_width), F32),
                pltpu.VMEM((4, 8, edge_width), F32),
            ],
        )
        returned = exchange(slot)
        head = 3 * edge_width + edge_width // 2
        (pack,) = call(
            edge_weights,
            [struct((head, width), BF)],
            (arrived3, low3, edge_state, act1, act2, top, mid, bottom, slot, node),
            "edge_weights",
        )
        sized = lambda n: -(-n // 128) * 128
        n_early, n_late, n_feed = sized(head + hidden + 32), sized(mf.shape[0] + hidden + 16), 2 * width
        cut = lambda n: [struct((n // 2, width), BF)] * 2 if tuned else [struct((n, width), BF)]
        pair, first_grad, pull, early = call(
            node_turn,
            [struct((rows, 2 * width), BF), struct((rows, width), F32), struct((rows, hidden), F32), cut(n_early)],
            (
                returned, node_up, node, send, second, slopes, first, counts, summed, ef, mt, vecs,
                own, packed, pack, edge_vec, mid_low,
            ),
            "node_turn",
            [pltpu.VMEM((n_early, width), BF)],
            spot=spot,
        )
        eighth = lambda n: struct((n // 8, width), BF)
        second_low, second_weight, message_vec = call(
            message_second(rows, fanout, step),
            [struct((n_edges, hidden), BF), struct((hidden, hidden), BF), struct((8, hidden), F32)],
            (pull, act, slope2),
            "message_second",
            [pltpu.VMEM((rows, hidden), F32)],
        )
        feed_outs = [
            [struct((n_feed, width), BF)] if tuned else [struct((width, share), BF), struct((share, width), BF)]
        ]

        def feed_grads_of(pairs, after):
            return call(
                feed_weights, feed_outs, (pairs, expand_weight, bias, reduce_weight), "feed_weights", after=after
            )

        first = []
        if tuned:
            (pair,) = call(
                stack_up, [struct((2 * rows, 2 * width), BF)], ([pair, to_hid(pair, 1)],), "pair_stack",
                after=[second_weight],
            )
            (early,) = call(
                split_chips, [[eighth(n_early)] * 4], (early[0], to_core(early[1])), "early_chips",
                after=[pair],
            )
            first = early[:1]
            early = to_chips(early)
        else:
            early = lax.psum(early[0].astype(F32), ("res", "hid"))
        first_low, slot, node, late = call(
            message_first(rows, fanout, step),
            [
                struct((n_edges, hidden), BF),
                [struct((buffer // len(deal), hidden), BF)] * len(deal),
                struct((rows, hidden), BF),
                struct((n_late, hidden), BF),
            ],
            (arrived2, low2, edge_state, pick, second_low, slope1, ms, second_weight, message_vec),
            "message_first",
            [
                pltpu.VMEM((buffer, hidden), F32),
                pltpu.VMEM((rows, hidden), F32),
            ],
            after=first,
        )
        final = Final
        if tuned:
            (early,) = call(add_up, [eighth(n_early)], (early,), "early_plane", after=[node])
            ((feed_pay,),) = feed_grads_of([pair, to_hid(pair, 2)], [early])
            keep, send_late = call(halved, cut(n_late), (late,), "late_pay", spot=spot, after=[feed_pay])
            (late,) = call(
                split_chips_more,
                [[struct((n_late // 8 + rows, width), BF)] * 4],
                (keep, to_core(send_late), slot),
                "late_chips",
            )
            last = late[0]
            late = to_chips(late)
            keep, send_feed = call(halved, cut(n_feed), [feed_pay], "feed_pay", spot=spot, after=[last])
            (early,) = call(
                add_two, [eighth(n_early)], (early, to_hid(early, 1), []), "early_line", after=[keep]
            )
            (feed_parts,) = call(
                split_chips, [[eighth(n_feed)] * 4], (keep, to_core(send_feed)), "feed_chips", after=[early]
            )
            last = feed_parts[0]
            half = struct((rows * 2, width), BF)
            late, mine, twin = call(
                add_up_more, [eighth(n_late), half, half], (late,), "late_plane", after=[last]
            )
            feed_parts = to_chips(feed_parts)
            (late,) = call(add_two, [eighth(n_late)], (late, to_hid(late, 1), []), "late_line")
            (feed_own,) = call(add_up, [eighth(n_feed)], (feed_parts,), "feed_plane", after=[late])
            (early,) = call(
                add_two,
                [struct(((n_early + n_feed) // 8, width), BF)],
                (early, to_hid(early, 2), [feed_own]),
                "early_line",
            )
            last = early
            early = [early] + [to_chip(early, m) for m in (1, 2, 3)]
            edge_gradient, last = call(
                edge_end(rows, fanout, step),
                [final(n_edges, edge_width)],
                (edge_grad, first_low, mf),
                "edge_end",
                after=[last],
                token=True,
            )
            returned = [mine, to_core(twin)]
            node_gradient, last = call(
                node_end,
                [final(rows, width)],
                (returned, send, first_grad, node, mf),
                "node_end",
                after=[last],
                token=True,
            )
            (late,) = call(
                add_two, [eighth(n_late)], (late, to_hid(late, 2), []), "late_line", after=[last]
            )
            (early,) = call(
                stack_up,
                [struct(((n_early + n_feed) // 2, width), BF)],
                (early,),
                "early_stack",
                after=[late],
            )
            early = [early, to_core(early)]
            late = [late] + [to_chip(late, m) for m in (1, 2, 3)]
        else:
            late = [lax.psum(late.astype(F32), ("res", "hid"))]
            early = [early]
            pairs = [lax.all_gather(pair, "hid", axis=0, tiled=True)]
            (feed_pay,) = feed_grads_of(pairs, [node])
            returned = exchange(slot)
            (edge_gradient,) = call(
                edge_end(rows, fanout, step), [final(n_edges, edge_width)], (edge_grad, first_low, mf), "edge_end"
            )
            (node_gradient,) = call(
                node_end, [final(rows, width)], (returned, send, first_grad, node, mf), "node_end"
            )
        (
            edge_first_grad, edge_second_grad, edge_third_grad, third_grad, vec, edge_vecs, expand_bias_grad,
            feed_grads, last,
        ) = call(
            unpack_early,
            [
                final(edge_width, ef.shape[1]), final(edge_width, edge_width), final(edge_width, edge_width),
                final(hidden, width), [final(1, width)] * 6, [final(1, edge_width)] * 5, final(1, share),
                [final(width, share), final(share, width)] if tuned else [],
            ],
            (early,),
            "unpack_early",
            [pltpu.VMEM((n_early, width), F32), pltpu.VMEM((n_feed, width), F32)],
            limit=16,
            spot=spot,
            token=True,
        )
        if tuned:
            (late,) = call(
                stack_up, [struct((n_late // 2, width), BF)], (late,), "late_stack", after=[last]
            )
            late = [late, to_core(late)]
        first_weight_grad, second_weight_grad, message_vec = call(
            unpack_late,
            [final(*mf.shape), final(hidden, hidden), [final(1, hidden)] * 2],
            (late,),
            "unpack_late",
            [pltpu.VMEM((n_late, width), F32)],
            limit=16,
            spot=spot,
        )
        if tuned:
            expand_grad, reduce_grad = feed_grads
        else:
            expand_grad, reduce_grad = [lax.psum(v.astype(F32), "res") for v in feed_pay]
        vec, edge_vecs, message_vec = [[v[0] for v in group] for group in (vec, edge_vecs, message_vec)]

        back = lambda v: v.reshape(fanout, rows, edge_width).transpose(1, 0, 2)
        return (
            node_result,
            back(edge_result),
            node_gradient,
            back(edge_gradient),
            first_weight_grad,
            message_vec[0],
            second_weight_grad,
            message_vec[1],
            third_grad,
            vec[5],
            vec[3],
            vec[4],
            expand_grad,
            expand_bias_grad[0],
            reduce_grad,
            vec[0],
            vec[1],
            vec[2],
            edge_first_grad.T,
            edge_vecs[4],
            edge_second_grad,
            edge_vecs[3],
            edge_third_grad,
            edge_vecs[2],
            edge_vecs[0],
            edge_vecs[1],
        )

    both = ("res", "hid")
    rows2, rows3 = P(both, None), P(both, None, None)
    placed = (
        rows2, rows3, rows3, rows2, P(both),
        P(), P(), P(), P(), P(), P(), P(), P(),
        P(None, "hid"), P("hid"), P("hid", None),
        P(), P(), P(), P(), P(), P(), P(), P(), P(), P(), P(),
        rows2, rows3,
    )
    given = (
        rows2, rows3, rows2, rows3,
        P(), P(), P(), P(), P(), P(), P(), P(),
        P(None, "hid"), P("hid"), P("hid", None),
        P(), P(), P(), P(), P(), P(), P(), P(), P(), P(), P(),
    )
    return jax.shard_map(body, mesh=mesh, in_specs=placed, out_specs=given, check_vma=False)
```

```python
import jax
import jax.numpy as jnp
from jax import lax
from jax.experimental import pallas as pl
from jax.experimental.pallas import tpu as pltpu
from jax.sharding import PartitionSpec as P

BF = jnp.bfloat16
F32 = jnp.float32
LEAN = 0.7978845608028654
CUBE = LEAN * 0.044715
MIB = 1 << 20
KEEP = pl.BlockSpec(memory_space=pltpu.VMEM)


def dot(left, right):
    return jnp.dot(left, right, preferred_element_type=F32)


def dot_nt(left, right):
    return lax.dot_general(left, right, (((1,), (1,)), ((), ())), preferred_element_type=F32)


def dot_tn(left, right):
    return lax.dot_general(left, right, (((0,), (0,)), ((), ())), preferred_element_type=F32)


def smooth(v):
    t = jnp.tanh(v * (LEAN + CUBE * (v * v)))
    half = 0.5 * v
    return half + half * t


def smooth_slope(v):
    v2 = v * v
    t = jnp.tanh(v * (LEAN + CUBE * v2))
    half = 0.5 * v
    slope = (0.5 + 0.5 * t) + (half - half * (t * t)) * (LEAN + (3.0 * CUBE) * v2)
    return half + half * t, slope


def smooth_low(v):
    v = v.astype(BF)
    t = jnp.tanh(v * (BF(LEAN) + BF(CUBE) * (v * v)))
    half = BF(0.5) * v
    return half + half * t


def smooth_slope_low(v):
    v = v.astype(BF)
    v2 = v * v
    t = jnp.tanh(v * (BF(LEAN) + BF(CUBE) * v2))
    half = BF(0.5) * v
    slope = (BF(0.5) + BF(0.5) * t) + (half - half * (t * t)) * (BF(LEAN) + BF(3.0 * CUBE) * v2)
    return half + half * t, slope


def centred(x):
    center = x - jnp.mean(x, axis=-1, keepdims=True)
    rate = lax.rsqrt(jnp.mean(center * center, axis=-1, keepdims=True) + 1e-05)
    return center * rate, rate


def norm_pull(hat, rate, gain, up):
    g = up * gain
    return rate * (
        g - jnp.mean(g, axis=-1, keepdims=True) - hat * jnp.mean(g * hat, axis=-1, keepdims=True)
    )


def tiled_add(rows, part):
    n, width = part.shape
    return (rows.reshape(-1, n, width) + part[None]).reshape(rows.shape)


def over(count, chunk):
    if count == 1:
        chunk(0, 0)
    else:
        lax.fori_loop(0, count, chunk, 0)


def aligned(index, size):
    return index if isinstance(index, int) else pl.multiple_of(index, size)


def fold(rows, n):
    return jnp.sum(rows.reshape(-1, n, rows.shape[-1]), axis=0)


class Final:
    def __init__(self, *shape):
        self.shape, self.dtype = shape, F32


class Cut(Final):
    def __init__(self, n, width, stop, start=0):
        super().__init__(stop - start, width)
        self.whole, self.start = (n, width), start


def call(body, outs, args, name, scratch=(), limit=28, spot=None, after=(), far=False, token=False):
    if token:
        outs = list(outs) + [pltpu.VMEM((8, 128), F32)]
    flat_outs, out_tree = jax.tree.flatten(list(outs), is_leaf=lambda v: hasattr(v, "dtype"))
    ends = [k for k, v in enumerate(flat_outs) if isinstance(v, Final)]
    cuts = [v for v in flat_outs if isinstance(v, Cut)]
    held_outs = [pltpu.VMEM(flat_outs[k].shape, flat_outs[k].dtype) for k in ends if not cuts]
    if cuts:
        held_outs = [pltpu.VMEM(cuts[0].whole, F32)]
    if ends:
        held_outs.append(pltpu.SemaphoreType.DMA((len(ends),)))
    shapes = [pltpu.HBM(v.shape, v.dtype) if isinstance(v, Final) else v for v in flat_outs]
    out_specs = [pl.BlockSpec(memory_space=pltpu.HBM) if isinstance(v, Final) else KEEP for v in flat_outs]
    space = pltpu.HBM if far else pltpu.VMEM
    args = jax.tree.map(lambda v: pltpu.with_memory_space_constraint(v, space), list(args))
    specs = jax.tree.map(lambda v: pl.BlockSpec(memory_space=space), args)
    lead = 0
    if spot is not None:
        args, specs, lead = [spot] + args, [pl.BlockSpec(memory_space=pltpu.SMEM)] + specs, 1
    n, more = len(args), len(after)
    scratch = list(scratch)
    if far:
        flat, tree = jax.tree.flatten(args[lead:])
        scratch += [pltpu.VMEM(v.shape, v.dtype) for v in flat] + [pltpu.SemaphoreType.DMA((len(flat),))]

    def run(*refs):
        given, rest = refs[:n], refs[n + more :]
        results, rest = list(jax.tree.leaves(list(rest[: len(outs)]))), rest[len(outs) :]
        targets = [results[k] for k in ends]
        if ends:
            count = len(held_outs)
            rest, kept, out_sems = rest[:-count], rest[-count:-1], rest[-1]
            for k, v in zip(ends, kept):
                results[k] = v
        if far:
            count = len(flat)
            rest, held, sems = rest[: -count - 1], rest[-count - 1 : -1], rest[-1]
            copies = [
                pltpu.make_async_copy(src, dst, sems.at[k])
                for k, (src, dst) in enumerate(zip(jax.tree.leaves(list(given[lead:])), held))
            ]
            for copy in copies:
                copy.start()
            for copy in copies:
                copy.wait()
            given = list(given[:lead]) + jax.tree.unflatten(tree, held)
        produced = list(jax.tree.unflatten(out_tree, results))
        if token:
            produced.pop()[...] = jnp.zeros((8, 128), F32)
        if cuts:
            produced = [kept[0]]
        body(*given, *produced, *rest)
        if cuts:
            kept = [kept[0].at[v.start : v.start + v.shape[0], :] for v in cuts]
        if ends:
            copies = [
                pltpu.make_async_copy(src, dst, out_sems.at[k])
                for k, (src, dst) in enumerate(zip(kept, targets))
            ]
            for copy in copies:
                copy.start()
            for copy in copies:
                copy.wait()

    return pl.pallas_call(
        run,
        out_shape=jax.tree.unflatten(out_tree, shapes),
        in_specs=specs + [pl.BlockSpec(memory_space=pl.ANY)] * more,
        out_specs=jax.tree.unflatten(out_tree, out_specs),
        scratch_shapes=scratch + held_outs,
        compiler_params=pltpu.CompilerParams(vmem_limit_bytes=limit * MIB),
        name=name,
    )(*args, *after)


def struct(shape, dtype):
    return pltpu.VMEM(shape, dtype)


def shards(own, packed):
    if len(packed) == 3:
        we, web, wr = packed
        for h in range(we.shape[0]):
            yield we[h], web[h : h + 1, :], wr[h]
        return
    yield own[0][...], own[1][...], own[2][...]
    (ref,) = packed
    n, width = ref.shape[0] // 8, ref.shape[1] // 3
    part = n // 9 * 4
    for h in range(3):
        at = slice(h * width, (h + 1) * width)
        we = jnp.concatenate([ref[r * n : r * n + part, at] for r in range(8)], axis=0)
        wr = jnp.concatenate([ref[r * n + part : r * n + 2 * part, at] for r in range(8)], axis=0)
        bias = ref[2 * part : n, at].astype(F32)
        yield we, bias[0:1] + bias[1:2], wr


def feed(mid, own, packed, rb, slopes):
    mid_low = mid.astype(BF)
    total = mid + rb
    for h, (we, web, wr) in enumerate(shards(own, packed)):
        act, slope = smooth_slope(dot(mid_low, we) + web)
        slopes[h] = slope.astype(BF)
        total = total + dot(act.astype(BF), wr)
    return mid_low, total


def joined(parts):
    if len(parts) == 1:
        return parts[0][...]
    if len(parts) == 2:
        n = parts[0].shape[0] // 4
        return jnp.concatenate([v[m * n : (m + 1) * n] for m in range(4) for v in parts], axis=0)
    near, far = parts[: len(parts) // 2], parts[len(parts) // 2 :]
    rows = []
    for mine, other in zip(near, far):
        half = mine.shape[0] // 2
        rows += [mine[:half], other[half:]]
    return jnp.concatenate(rows, axis=0)


def dealt(outs, value):
    n = value.shape[0] // len(outs)
    for m, out in enumerate(outs):
        out[...] = value[m * n : (m + 1) * n].astype(out.dtype)


def halved(spot, pay, keep, send):
    n = keep.shape[0] // 4
    for m in range(4):
        chip = (spot[1] ^ m) * 2
        keep[m * n : (m + 1) * n, :] = pay[pl.ds(pl.multiple_of((chip + spot[0]) * n, n), n), :]
        send[m * n : (m + 1) * n, :] = pay[pl.ds(pl.multiple_of((chip + 1 - spot[0]) * n, n), n), :]


def message_mean(summed, counts, mt, mtb):
    mean = summed / counts
    high = mean.astype(BF)
    rest = (mean - high.astype(F32)).astype(BF)
    return dot(high, mt) + dot(rest, mt) + mtb


def solution(mesh):
    n_res, n_hid = mesh.shape["res"], mesh.shape["hid"]
    tuned = (n_res, n_hid) == (8, 4)
    pair = [(i, i ^ 1) for i in range(n_res)]

    def to_chip(v, m):
        return lax.ppermute(v, "res", [(i, i ^ (2 * m)) for i in range(n_res)])

    def to_core(v):
        return lax.ppermute(v, "res", pair)

    def to_hid(v, m):
        return lax.ppermute(v, "hid", [(i, i ^ m) for i in range(n_hid)])

    def exchange(parts):
        if not tuned:
            n, width = parts[0].shape
            blocks = parts[0].reshape(n_res, n // n_res, width)
            return [lax.all_to_all(blocks, "res", 0, 0, tiled=True).reshape(n, width)]
        near = [parts[0]] + [to_chip(parts[m], m) for m in (1, 2, 3)]
        return near + [to_core(v) for v in near]

    def prepare_send(spot, table, nodes, weights, away_out, send_out, piece_out):
        rows, width = nodes.shape
        n = table.shape[1]
        lines = lax.broadcasted_iota(jnp.int32, (rows, n), 0)
        same = lax.broadcasted_iota(jnp.int32, (rows, rows), 0) == lax.broadcasted_iota(
            jnp.int32, (rows, rows), 1
        )
        same = same.astype(F32).astype(BF)
        each = n_res // len(away_out)
        for q in range(n_res):
            line = table[pl.ds(q ^ spot[3], 1), :]
            chosen = (lines == line).astype(F32).astype(BF)
            at = slice(q % each * n, (q % each + 1) * n)
            away_out[q // each][at, :] = dot_tn(chosen, nodes[...]).astype(BF)
            send_out[q * n : (q + 1) * n, :] = dot_tn(chosen, same).astype(BF)
        if piece_out:
            (out,) = piece_out
            we, wr, bias = weights
            n = width // 8
            at = pl.ds(pl.multiple_of(spot[3] * n, n), n)
            out[:n, :] = we[at, :]
            out[n : 2 * n, :] = wr[at, :]
            high = bias[...].astype(BF).astype(F32)
            rest = jnp.concatenate([high, bias[...] - high, jnp.zeros((n // 4 - 2, width), F32)], axis=0)
            out[2 * n :, :] = rest.astype(BF)

    def prepare_rest(
        spot, slots, counts, vecs, edge_vecs, edges, pick_out, counts_out, vecs_out, edge_out, edges_out
    ):
        edges_out[...] = edges[...]
        rows, fanout = slots.shape
        lanes = lax.broadcasted_iota(jnp.int32, (rows, pick_out.shape[1]), 1)
        moved = slots[...] ^ (spot[3] * (pick_out.shape[1] // n_res))
        for k in range(fanout):
            chosen = (lanes == moved[:, k : k + 1]).astype(F32).astype(BF)
            pick_out[k * rows : (k + 1) * rows, :] = chosen
        same = lax.broadcasted_iota(jnp.int32, (rows, rows), 0) == lax.broadcasted_iota(
            jnp.int32, (rows, rows), 1
        )
        many = jnp.where(same, jnp.broadcast_to(counts[...].astype(F32), (rows, rows)), 0.0)
        counts_out[...] = jnp.sum(many, axis=1, keepdims=True)
        edge_out[...] = jnp.zeros_like(edge_out)
        for k, v in enumerate(vecs):
            vecs_out[k : k + 1, :] = v[...]
        for k, v in enumerate(edge_vecs):
            edge_out[k : k + 1, :] = v[...]

    def pass_one(rows, fanout, step):
        span = step * rows

        def kernel(
            arrived, nodes, edges, pick, counts, mf, ms, mt, vecs, mid_out, mid_low_out, sums,
        ):
            mfb, msb, mtb, mg, msh = [vecs[k : k + 1, :] for k in range(5)]
            width = nodes.shape[1]
            query = dot(joined(arrived), mf[width : 2 * width]).astype(BF)
            part = dot(nodes[...], mf[:width]) + mfb
            lower = mf[2 * width :]
            lots = jnp.broadcast_to(counts[...], (rows, ms.shape[1]))
            sums[...] = jnp.zeros_like(sums)

            def chunk(i, carry):
                at = pl.ds(aligned(i * span, span), span)
                pre = dot(pick[at, :], query) + dot(edges[at, :], lower)
                act = smooth_low(tiled_add(pre, part)).astype(BF)
                act = smooth_low(dot(act, ms[...]) + msb)
                total = sums[...]
                for j in range(step):
                    total = total + jnp.where(
                        lots > jnp.float32(i * step + j), act[j * rows : (j + 1) * rows], 0.0
                    )
                sums[...] = total
                return carry

            over(fanout // step, chunk)
            first = nodes[...].astype(F32) + message_mean(sums[...], counts[...], mt[...], mtb)
            mid = centred(first)[0] * mg + msh
            mid_out[...] = mid
            mid_low_out[...] = mid.astype(BF)

        return kernel

    def feed_shard(mids, we, web, wr, outs):
        mid = jnp.concatenate([v[...] for v in mids], axis=0)
        act = smooth(dot(mid, we[...]) + web[...]).astype(BF)
        dealt(outs, dot(act, wr[...]))

    def feed_end(mid, parts, vecs, send, new_out, low_out, away_out):
        rb, fg, fsh = [vecs[k : k + 1, :] for k in (5, 6, 7)]
        second = mid[...] + rb
        for v in parts:
            second = second + v[...].astype(F32)
        new = centred(second)[0] * fg + fsh
        new_out[...] = new
        low = new.astype(BF)
        low_out[...] = low
        dealt(away_out, dot(send[...], low))

    def feed_pass(mid, own, packed, vecs, send, slopes_out, second_out, new_out, low_out, away_out):
        rb, fg, fsh = [vecs[k : k + 1, :] for k in (5, 6, 7)]
        _, second = feed(mid[...], own, packed, rb, slopes_out)
        second_out[...] = second
        new = centred(second)[0] * fg + fsh
        new_out[...] = new
        low = new.astype(BF)
        low_out[...] = low
        dealt(away_out, dot(send[...], low))

    def pass_two(rows, fanout, step):
        span = step * rows

        def kernel(
            arrived, state, low, edges, pick, counts, mf, ms, mt, vecs, ef, es, et, edge_vecs,
            edge_out, act_out, slope1_out, slope2_out, first_out, summed_out, mid_out, mid_low_out, sums,
        ):
            mfb, msb, mtb, mg, msh = [vecs[k : k + 1, :] for k in range(5)]
            efb, esb, etb, eg, esh = [edge_vecs[k : k + 1, :] for k in range(5)]
            width = state.shape[1]
            received = joined(arrived)
            key = dot_nt(received, ef[:, width : 2 * width]).astype(BF)
            edge_part = dot_nt(low[...], ef[:, :width]) + efb
            edge_lower = ef[:, 2 * width :]
            query = dot(received, mf[width : 2 * width]).astype(BF)
            part = dot(low[...], mf[:width]) + mfb
            lower = mf[2 * width :]
            lots = jnp.broadcast_to(counts[...], (rows, ms.shape[1]))
            sums[...] = jnp.zeros_like(sums)

            def chunk(i, carry):
                at = pl.ds(aligned(i * span, span), span)
                chosen = pick[at, :]
                old = edges[at, :]
                pre = dot(chosen, key) + dot_nt(old, edge_lower)
                act = smooth_low(tiled_add(pre, edge_part)).astype(BF)
                act = smooth_low(dot(act, es[...]) + esb).astype(BF)
                total = old.astype(F32) + dot(act, et[...]) + etb
                fresh = centred(total)[0] * eg + esh
                edge_out[at, :] = fresh
                pre = dot(chosen, query) + dot(fresh.astype(BF), lower)
                act, slope = smooth_slope_low(tiled_add(pre, part))
                act = act.astype(BF)
                act_out[at, :] = act
                slope1_out[at, :] = slope.astype(BF)
                act, slope = smooth_slope_low(dot(act, ms[...]) + msb)
                total = sums[...]
                for j in range(step):
                    valid = lots > jnp.float32(i * step + j)
                    total = total + jnp.where(valid, act[j * rows : (j + 1) * rows], 0.0)
                    slope2_out[pl.ds(aligned(i * span + j * rows, rows), rows), :] = jnp.where(
                        valid, slope[j * rows : (j + 1) * rows], 0.0
                    ).astype(BF)
                sums[...] = total
                return carry

            over(fanout // step, chunk)
            summed_out[...] = sums[...].astype(BF)
            first = state[...] + message_mean(sums[...], counts[...], mt[...], mtb)
            first_out[...] = first
            mid = centred(first)[0] * mg + msh
            mid_out[...] = mid
            mid_low_out[...] = mid.astype(BF)

        return kernel

    def edge_turn(rows, fanout, step):
        span = step * rows

        def kernel(
            arrived, low, edges, up, pick, ef, es, et, edge_vecs,
            result_out, grad_out, act1_out, act2_out, top_out, mid_out, bottom_out,
            slot_out, node_out, vec_out, slots, node, marks,
        ):
            width = low.shape[1]
            efb, esb, etb, eg, esh = [edge_vecs[k : k + 1, :] for k in range(5)]
            key = dot_nt(joined(arrived), ef[:, width : 2 * width]).astype(BF)
            edge_part = dot_nt(low[...], ef[:, :width]) + efb
            edge_lower = ef[:, 2 * width :]
            slots[...] = jnp.zeros_like(slots)
            node[...] = jnp.zeros_like(node)
            marks[...] = jnp.zeros_like(marks)

            def chunk(i, carry):
                at = pl.ds(aligned(i * span, span), span)
                chosen = pick[at, :]
                old = edges[at, :]
                pre = dot(chosen, key) + dot_nt(old.astype(BF), edge_lower)
                act, slope1 = smooth_slope_low(tiled_add(pre, edge_part))
                act1 = act.astype(BF)
                act1_out[at, :] = act1
                act, slope2 = smooth_slope_low(dot(act1, es[...]) + esb)
                act2 = act.astype(BF)
                act2_out[at, :] = act2
                total = old + dot(act2, et[...]) + etb
                hat, rate = centred(total)
                result_out[at, :] = hat * eg + esh
                above = up[at, :].astype(F32)
                sum_grad = norm_pull(hat, rate, eg, above)
                top = sum_grad.astype(BF)
                top_out[at, :] = top
                mid = dot_nt(top, et[...]) * slope2
                mid_low = mid.astype(BF)
                mid_out[at, :] = mid_low
                bottom = dot_nt(mid_low, es[...]) * slope1
                bottom_low = bottom.astype(BF)
                bottom_out[at, :] = bottom_low
                grad_out[at, :] = sum_grad + dot(bottom_low, edge_lower)
                marks[0] += fold(above * hat, 8)
                marks[1] += fold(above, 8)
                marks[2] += fold(sum_grad, 8)
                marks[3] += fold(mid, 8)
                node[...] += fold(bottom, rows)
                slots[...] += dot_tn(chosen, bottom_low)
                return carry

            over(fanout // step, chunk)
            dealt(slot_out, slots[...])
            node_out[...] = node[...].astype(BF)
            vec_out[...] = jnp.zeros_like(vec_out)
            for j in range(4):
                vec_out[j : j + 1, :] = jnp.sum(marks[j], axis=0, keepdims=True)
            vec_out[4:5, :] = jnp.sum(node[...], axis=0, keepdims=True)

        return kernel

    def edge_weights(arrived, low, edges, act1, act2, top, mid, bottom, slot, node, pack_out):
        n, wide = act1.shape[1], low.shape[1]
        slot = jnp.concatenate([v[...] for v in slot], axis=0)
        pack_out[:n, :] = dot_tn(node[...], low[...]).astype(BF)
        pack_out[n : 2 * n, :] = dot_tn(slot, joined(arrived)).astype(BF)
        pack_out[2 * n :, :] = jnp.zeros((pack_out.shape[0] - 2 * n, wide), BF)
        pack_out[2 * n : 3 * n, :n] = dot_tn(act1[...], mid[...]).astype(BF)
        pack_out[2 * n : 3 * n, 256 : 256 + n] = dot_tn(act2[...], top[...]).astype(BF)
        lower = dot_tn(bottom[...], edges[...].astype(BF)).astype(BF)
        pack_out[3 * n :, :n] = lower[: n // 2]
        pack_out[3 * n :, 256 : 256 + n] = lower[n // 2 :]

    def node_turn(
        spot, returned, up, node, send, second, slopes, first, counts, summed, ef, mt, vecs,
        own, packed, pack, edge_vec, mid_low, pair_out, sum_out, pull_out, pay_out, pay,
    ):
        width = up.shape[1]
        key_low = dot_tn(send[...], joined(returned)).astype(BF)
        new_grad = (
            up[...].astype(F32) + dot(node[...], ef[:, :width]) + dot(key_low, ef[:, width : 2 * width])
        )
        hat, rate = centred(second[...])
        sum_grad = norm_pull(hat, rate, vecs[6:7, :], new_grad)
        marks = [sum_grad, new_grad * hat, new_grad]
        low = sum_grad.astype(BF)
        pair_out[:, :width] = mid_low[...]
        pair_out[:, width:] = low
        mid_grad = sum_grad
        bias = []
        for h, (we, _, wr) in enumerate(shards(own, packed)):
            expand = dot_nt(low, wr) * slopes[h].astype(F32)
            bias.append(jnp.sum(expand, axis=0, keepdims=True))
            mid_grad = mid_grad + dot_nt(expand.astype(BF), we)
        hat, rate = centred(first[...])
        first_grad = norm_pull(hat, rate, vecs[3:4, :], mid_grad)
        sum_out[...] = first_grad
        marks += [mid_grad * hat, mid_grad, first_grad]
        marks = [jnp.sum(v, axis=0, keepdims=True) for v in marks]
        rows_low = (first_grad / counts[...]).astype(BF)
        pull_out[...] = dot_nt(rows_low, mt[...])
        third = dot_tn(summed[...], rows_low).astype(BF)
        head, hidden = pack.shape[0], third.shape[0]
        pay[:head, :] = pack[...]
        pay[head : head + hidden, :] = third
        pay[head + hidden :, :] = jnp.zeros((pay.shape[0] - head - hidden, width), BF)
        rows = jnp.concatenate(marks + [jnp.zeros((10, width), F32)], axis=0)
        at = lax.broadcasted_iota(jnp.int32, rows.shape, 0)
        share = bias[0].shape[1]
        for h, v in enumerate(bias):
            line = 6 + ((spot[2] ^ h) if tuned else h)
            if share < width:
                v = jnp.concatenate([v, jnp.zeros((1, width - share), F32)], axis=1)
            rows = jnp.where(at == line, v, rows)
        pay[head + hidden : head + hidden + 16, :] = rows.astype(BF)
        pay[head + hidden + 16 : head + hidden + 32, : edge_vec.shape[1]] = jnp.concatenate(
            [edge_vec[...], jnp.zeros_like(edge_vec)], axis=0
        ).astype(BF)
        if len(pay_out) == 1:
            pay_out[0][...] = pay[...]
        else:
            halved(spot, pay, *pay_out)

    def message_second(rows, fanout, step):
        span = step * rows

        def kernel(pull, act, slope2, second_out, weight_out, vec_out, marks):
            marks[...] = jnp.zeros_like(marks)

            def chunk(i, carry):
                at = pl.ds(aligned(i * span, span), span)
                second = slope2[at, :].astype(F32).reshape(step, rows, -1) * pull[...][None]
                marks[...] += jnp.sum(second, axis=0)
                second_out[at, :] = second.reshape(span, -1).astype(BF)
                return carry

            over(fanout // step, chunk)
            weight_out[...] = dot_tn(act[...], second_out[...]).astype(BF)
            vec_out[...] = jnp.zeros_like(vec_out)
            vec_out[0:1, :] = jnp.sum(marks[...], axis=0, keepdims=True)

        return kernel

    def message_first(rows, fanout, step):
        span = step * rows

        def kernel(
            arrived, low, edges, pick, second, slope1, ms, weight, vec,
            first_low_out, slot_out, node_out, pay, slots, node,
        ):
            width = low.shape[1]
            slots[...] = jnp.zeros_like(slots)
            node[...] = jnp.zeros_like(node)

            def chunk(i, carry):
                at = pl.ds(aligned(i * span, span), span)
                first = dot_nt(second[at, :], ms[...]) * slope1[at, :].astype(F32)
                node[...] += fold(first, rows)
                first = first.astype(BF)
                first_low_out[at, :] = first
                slots[...] += dot_tn(pick[at, :], first)
                return carry

            over(fanout // step, chunk)
            slot = slots[...].astype(BF)
            dealt(slot_out, slot)
            node_low = node[...].astype(BF)
            node_out[...] = node_low
            hidden, last = ms.shape[0], 2 * width + edges.shape[1]
            pay[:width, :] = dot_tn(low[...], node_low).astype(BF)
            pay[width : 2 * width, :] = dot_tn(joined(arrived), slot).astype(BF)
            pay[2 * width : last, :] = dot_tn(edges[...].astype(BF), first_low_out[...]).astype(BF)
            pay[last : last + hidden, :] = weight[...]
            pay[last + hidden :, :] = jnp.zeros((pay.shape[0] - last - hidden, hidden), BF)
            vecs = [jnp.sum(node[...], axis=0, keepdims=True), vec[0:1, :], jnp.zeros((14, hidden), F32)]
            pay[last + hidden : last + hidden + 16, :] = jnp.concatenate(vecs, axis=0).astype(BF)

        return kernel

    def feed_products(pairs, we, web, wr):
        n = we.shape[0]
        mid = jnp.concatenate([v[:, :n] for v in pairs], axis=0)
        up = jnp.concatenate([v[:, n:] for v in pairs], axis=0)
        act, slope = smooth_slope_low(dot(mid, we[...]) + web[...])
        expand = dot_nt(up, wr[...]) * slope
        return dot_tn(mid, expand.astype(BF)), dot_tn(act, up)

    def feed_weights(pairs, we, web, wr, expand_out, reduce_out):
        expand_out[...], reduce_out[...] = feed_products(pairs, we, web, wr)

    def feed_weights_more(pairs, we, web, wr, expand, reduce, expand_out, reduce_out):
        left, right = feed_products(pairs, we, web, wr)
        expand_out[...], reduce_out[...] = expand[...] + left, reduce[...] + right

    def node_end(returned, send, first_grad, node, mf, out):
        width = out.shape[1]
        query_low = dot_tn(send[...], joined(returned)).astype(BF)
        out[...] = (
            first_grad[...] + dot_nt(node[...], mf[:width]) + dot_nt(query_low, mf[width : 2 * width])
        )

    def edge_end(rows, fanout, step):
        span = step * rows

        def kernel(grad, first_low, mf, out):
            lower = mf[mf.shape[0] - grad.shape[1] :]

            def chunk(i, carry):
                at = pl.ds(aligned(i * span, span), span)
                out[at, :] = grad[at, :] + dot_nt(first_low[at, :], lower)
                return carry

            over(fanout // step, chunk)

        return kernel

    def split_chips(keep, got, outs):
        n = keep.shape[0] // len(outs)
        for m, out in enumerate(outs):
            at = slice(m * n, (m + 1) * n)
            out[:n, :] = (keep[at, :].astype(F32) + got[at, :].astype(F32)).astype(BF)

    def split_chips_more(keep, got, more, outs):
        split_chips(keep, got, outs)
        for v, out in zip(more, outs):
            out[out.shape[0] - v.shape[0] :, :] = v[...]

    def add_up(parts, out):
        n = out.shape[0]
        total = parts[0][:n, :].astype(F32)
        for v in parts[1:]:
            total = total + v[:n, :].astype(F32)
        out[...] = total.astype(BF)

    def add_up_more(parts, out, mine, twin):
        add_up(parts, out)
        n = mine.shape[0] // len(parts)
        for m, v in enumerate(parts):
            at, top = slice(m * n, (m + 1) * n), out.shape[0]
            mine[at, :] = v[top : top + n, :]
            twin[at, :] = v[top + n : top + 2 * n, :]

    def add_up_join(parts, more, out):
        n = more.shape[0]
        out[:n, :] = more[...]
        total = parts[0][...].astype(F32)
        for v in parts[1:]:
            total = total + v[...].astype(F32)
        out[n:, :] = total.astype(BF)

    def add_up_sides(spot, parts, pay, keep, send, pay_keep, pay_send, total):
        add_up(parts, total)
        halved(spot, pay, pay_keep, pay_send)
        n, side = keep.shape[1], spot[2] // 2
        keep[...] = total[:, pl.ds(pl.multiple_of(side * n, n), n)]
        send[...] = total[:, pl.ds(pl.multiple_of((1 - side) * n, n), n)]

    def join_sides(spot, mine, other, out):
        n, side = mine.shape[1], spot[2] // 2
        out[:, pl.ds(pl.multiple_of(side * n, n), n)] = mine[...]
        out[:, pl.ds(pl.multiple_of((1 - side) * n, n), n)] = other[...]

    def sort_cores(parts, mine, twin):
        n = mine.shape[0] // len(parts)
        for m, v in enumerate(parts):
            at = slice(m * n, (m + 1) * n)
            mine[at, :] = v[:n, :]
            twin[at, :] = v[n : 2 * n, :]

    def add_two(left, right, more, out):
        n = left.shape[0]
        out[:n, :] = (left[...].astype(F32) + right[...].astype(F32)).astype(BF)
        if more:
            out[n:, :] = more[0][...]

    def to_chips(parts):
        return [parts[0]] + [to_chip(parts[m], m) for m in (1, 2, 3)]

    def spread(own):
        parts = [own] + [to_chip(own, m) for m in (1, 2, 3)]
        return parts + [to_core(v) for v in parts]

    def laid_out(spot, parts, total):
        n = parts[0].shape[0]
        for k, v in enumerate(parts):
            at = (2 * (spot[1] ^ (k % 4)) + (spot[0] ^ (k // 4))) * n
            total[pl.ds(pl.multiple_of(at, n), n), :] = v[...].astype(total.dtype)

    def lay_pair(spot, stacks, total):
        n = total.shape[0] // 8
        for k in range(8):
            at = (2 * (spot[1] ^ (k % 4)) + (spot[0] ^ (k // 4))) * n
            top = k % 4 * n
            total[pl.ds(pl.multiple_of(at, n), n), :] = stacks[k // 4][top : top + n, :].astype(total.dtype)

    def stack_up(parts, out):
        n = parts[0].shape[0]
        for m, v in enumerate(parts):
            out[m * n : (m + 1) * n, :] = v[...]

    def unpack_early(
        spot, parts, first_out, second_out, third_out, message_out, vec_out, edge_vec_out, bias_out, total,
    ):
        if len(parts) == 1:
            total[...] = parts[0][...]
        else:
            lay_pair(spot, parts, total)
        n, wide = second_out.shape[0], message_out.shape[1]
        first_out[:, :wide] = total[:n, :]
        first_out[:, wide : 2 * wide] = total[n : 2 * n, :]
        second_out[...] = total[2 * n : 3 * n, :n]
        third_out[...] = total[2 * n : 3 * n, 256 : 256 + n]
        at = 3 * n + n // 2
        first_out[: n // 2, 2 * wide :] = total[3 * n : at, :n]
        first_out[n // 2 :, 2 * wide :] = total[3 * n : at, 256 : 256 + n]
        hidden = message_out.shape[0]
        message_out[...] = total[at : at + hidden, :]
        for k, out in enumerate(vec_out):
            out[...] = total[at + hidden + k : at + hidden + k + 1, :]
        for k, out in enumerate(edge_vec_out):
            out[...] = total[at + hidden + 16 + k : at + hidden + 17 + k, :n]
        vecs = total[at + hidden : at + hidden + 16, :]
        line = lax.broadcasted_iota(jnp.int32, vecs.shape, 0) == 6 + spot[2]
        bias = jnp.sum(jnp.where(line, vecs, 0.0), axis=0, keepdims=True)
        bias_out[...] = bias[:, : bias_out.shape[1]]

    def unpack_late(spot, parts, total):
        if len(parts) == 1:
            total[...] = parts[0][...]
        else:
            lay_pair(spot, parts, total)

    def split_relay(left, right, left_out, right_out):
        n = left_out.shape[1]
        left_out[...] = left[:, :n]
        right_out[...] = right[:, n:]

    def stack_relay(parts, left, right, out):
        n, half = left.shape
        for m, v in enumerate(parts):
            out[m * n : (m + 1) * n, :] = v[...]
        out[len(parts) * n :, :half] = left[...]
        out[len(parts) * n :, half:] = right[...]

    def join_pieces(parts, out):
        for m, v in enumerate(parts):
            n = v.shape[1]
            out[:, m * n : (m + 1) * n] = v[...]

    def body(
        nodes, edges, send_rows, neighbor_slots, neighbor_counts, mf, mfb, ms, msb, mt, mtb, mg, msh,
        expand_weight, expand_bias, reduce_weight, rb, fg, fsh, ef, efb, es, esb, et, etb, eg, esh,
        node_up, edge_up,
    ):
        rows, fanout, edge_width = edges.shape
        width, hidden = nodes.shape[1], ms.shape[0]
        share = expand_weight.shape[1]
        n_edges = rows * fanout
        step = fanout
        slots_each = send_rows.shape[2]
        buffer = n_res * slots_each
        row = lambda v: v.reshape(1, -1)
        if tuned:
            res, hid = lax.axis_index("res"), lax.axis_index("hid")
            spot = jnp.stack([res % 2, res // 2, hid, res]).astype(jnp.int32)
        else:
            spot = jnp.stack([0, 0, lax.axis_index("hid"), 0]).astype(jnp.int32)
        edges = edges.transpose(1, 0, 2).reshape(n_edges, edge_width)
        edge_up = edge_up.transpose(1, 0, 2).reshape(n_edges, edge_width)
        ef = ef.T
        bias = row(expand_bias)
        own = (expand_weight, bias, reduce_weight)
        one = struct((rows, width), BF)
        deal = [one] * 4 if tuned else [struct((buffer, width), BF)]
        n_piece = width // 8 * 9 // 4
        away, send, piece = call(
            prepare_send,
            [deal, struct((buffer, rows), BF), [struct((n_piece, width), BF)] if tuned else []],
            (send_rows[0], nodes, (expand_weight, reduce_weight, bias) if tuned else ()),
            "prepare_send",
            spot=spot,
            far=True,
        )
        pick, counts, vecs, edge_vecs, edges = call(
            prepare_rest,
            [
                struct((n_edges, buffer), BF),
                struct((rows, 1), F32),
                struct((8, width), F32),
                struct((8, edge_width), F32),
                struct((n_edges, edge_width), BF),
            ],
            (
                neighbor_slots,
                row(neighbor_counts),
                [row(v) for v in (mfb, msb, mtb, mg, msh, rb, fg, fsh)],
                [row(v) for v in (efb, esb, etb, eg, esh)],
                edges,
            ),
            "prepare_rest",
            spot=spot,
            after=away[:1],
            far=True,
        )
        if tuned:
            half = struct((rows * 2, width), BF)
            mine, twin = call(sort_cores, [half, half], (to_chips(away),), "first_sort", after=[counts])
            arrived = [mine, to_core(twin)]
        else:
            arrived = exchange(away)
        edge_args = (ef, es, et, edge_vecs)
        if tuned:
            pieces = [to_hid(piece[0], m) for m in (1, 2, 3)]
            (piece,) = call(
                join_pieces, [struct((n_piece, 3 * width), BF)], (pieces,), "join_pieces", after=[counts] + arrived
            )
            packed, first = [piece] + [to_chip(piece, m) for m in (1, 2)], [piece]
        else:
            packed, first = [
                lax.all_gather(expand_weight, "hid"),
                lax.all_gather(expand_bias, "hid"),
                lax.all_gather(reduce_weight, "hid"),
            ], []
        mid, mid_low = call(
            pass_one(rows, fanout, step),
            [struct((rows, width), F32), one],
            (arrived, nodes, edges, pick, counts, mf, ms, mt, vecs),
            "message_one",
            [pltpu.VMEM((rows, hidden), F32)],
            after=first,
        )
        if tuned:
            mids = [mid_low] + [to_hid(mid_low, m) for m in (1, 2, 3)]
            (parts,) = call(
                feed_shard, [[one] * 4], (mids, expand_weight, bias, reduce_weight), "feed_shard"
            )
            relay = struct((n_piece, 3 * width // 2), BF)
            left, right = call(
                split_relay, [relay, relay], tuple(packed[1:]), "split_weights", after=parts[:1]
            )
            parts = [parts[0]] + [to_hid(parts[m], m) for m in (1, 2, 3)]
        else:
            mids = [lax.all_gather(mid_low, "hid", axis=0, tiled=True)]
            (part,) = call(
                feed_shard,
                [[struct((n_hid * rows, width), BF)]],
                (mids, expand_weight, bias, reduce_weight),
                "feed_shard",
            )
            parts = [lax.psum_scatter(part[0], "hid", scatter_dimension=0, tiled=True)]
        state, low, away = call(
            feed_end, [struct((rows, width), F32), one, deal], (mid, parts, vecs, send), "feed_one"
        )
        if tuned:
            (packed,) = call(
                stack_relay,
                [struct((4 * n_piece, 3 * width), BF)],
                (packed, to_chip(left, 2), to_chip(right, 1)),
                "stack_weights",
                after=[low],
            )
            packed = [packed, to_core(packed)]
        arrived2, low2 = exchange(away), low
        first = []
        if tuned:
            (packed,) = call(
                lay_pair, [struct((8 * n_piece, 3 * width), BF)], (packed,), "lay_weights", spot=spot
            )
            first = packed = [packed]
        edge_state, act, slope1, slope2, first, summed, mid, mid_low = call(
            pass_two(rows, fanout, step),
            [
                struct((n_edges, edge_width), F32),
                struct((n_edges, hidden), BF),
                struct((n_edges, hidden), BF),
                struct((n_edges, hidden), BF),
                struct((rows, width), F32),
                struct((rows, hidden), BF),
                struct((rows, width), F32),
                one,
            ],
            (arrived2, state, low2, edges, pick, counts, mf, ms, mt, vecs, *edge_args),
            "layer_two",
            [pltpu.VMEM((rows, hidden), F32)],
            after=first,
        )
        feed_outs = [
            struct((n_hid, rows, share), BF),
            struct((rows, width), F32),
            jax.ShapeDtypeStruct((rows, width), F32),
            one,
            deal,
        ]
        slopes, second, node_result, low3, away = call(
            feed_pass, feed_outs, (mid, own, packed, vecs, send), "feed_two"
        )
        arrived3 = exchange(away)
        wide = lambda dtype: struct((n_edges, edge_width), dtype)
        edge_result, edge_grad, act1, act2, top, mid, bottom, slot, node, edge_vec = call(
            edge_turn(rows, fanout, step),
            [
                jax.ShapeDtypeStruct((n_edges, edge_width), F32),
                wide(F32), wide(BF), wide(BF), wide(BF), wide(BF), wide(BF),
                [struct((buffer // len(deal), edge_width), BF)] * len(deal),
                struct((rows, edge_width), BF),
                struct((8, edge_width), F32),
            ],
            (arrived3, low3, edge_state, edge_up, pick, *edge_args),
            "edge_turn",
            [
                pltpu.VMEM((buffer, edge_width), F32),
                pltpu.VMEM((rows, edge_width), F32),
                pltpu.VMEM((4, 8, edge_width), F32),
            ],
        )
        head = 3 * edge_width + edge_width // 2
        (pack,) = call(
            edge_weights,
            [struct((head, width), BF)],
            (arrived3, low3, edge_state, act1, act2, top, mid, bottom, slot, node),
            "edge_weights",
        )
        if tuned:
            half = struct((rows * 2, edge_width), BF)
            mine, twin = call(sort_cores, [half, half], (to_chips(slot),), "edge_sort", after=[pack])
            returned = [mine, to_core(twin)]
        else:
            returned = exchange(slot)
        sized = lambda n: -(-n // 128) * 128
        n_early, n_late = sized(head + hidden + 32), sized(mf.shape[0] + hidden + 16)
        cut = lambda n: [struct((n // 2, width), BF)] * 2 if tuned else [struct((n, width), BF)]
        pair, first_grad, pull, early = call(
            node_turn,
            [struct((rows, 2 * width), BF), struct((rows, width), F32), struct((rows, hidden), F32), cut(n_early)],
            (
                returned, node_up, node, send, second, slopes, first, counts, summed, ef, mt, vecs,
                own, packed, pack, edge_vec, mid_low,
            ),
            "node_turn",
            [pltpu.VMEM((n_early, width), BF)],
            spot=spot,
        )
        eighth = lambda n: struct((n // 8, width), BF)
        second_low, second_weight, message_vec = call(
            message_second(rows, fanout, step),
            [struct((n_edges, hidden), BF), struct((hidden, hidden), BF), struct((8, hidden), F32)],
            (pull, act, slope2),
            "message_second",
            [pltpu.VMEM((rows, hidden), F32)],
        )
        feed_own = (expand_weight, bias, reduce_weight)

        first = []
        if tuned:
            (early,) = call(
                split_chips, [[eighth(n_early)] * 4], (early[0], to_core(early[1])), "early_chips",
                after=[second_weight],
            )
            first = early[:1]
            early = to_chips(early)
        else:
            early = lax.psum(early[0].astype(F32), ("res", "hid"))
        first_low, slot, node, late = call(
            message_first(rows, fanout, step),
            [
                struct((n_edges, hidden), BF),
                [struct((buffer // len(deal), hidden), BF)] * len(deal),
                struct((rows, hidden), BF),
                struct((n_late, hidden), BF),
            ],
            (arrived2, low2, edge_state, pick, second_low, slope1, ms, second_weight, message_vec),
            "message_first",
            [
                pltpu.VMEM((buffer, hidden), F32),
                pltpu.VMEM((rows, hidden), F32),
            ],
            after=first,
        )
        final = Final
        if tuned:
            (pair,) = call(
                stack_up, [struct((2 * rows, 2 * width), BF)], ([pair, to_hid(pair, 2)],), "pair_stack",
                after=[node],
            )
            side = struct((n_early // 8, width // 2), BF)
            early, other, keep, send_late = call(
                add_up_sides, [side, side] + cut(n_late), (early, late), "early_plane",
                [pltpu.VMEM((n_early // 8, width), BF)], spot=spot, after=[pair],
            )
            (late,) = call(
                split_chips_more,
                [[struct((n_late // 8 + rows, width), BF)] * 4],
                (keep, to_core(send_late), slot),
                "late_chips",
            )
            last = late[0]
            late = to_chips(late)
            (early,) = call(add_two, [side], (early, to_hid(other, 2), []), "early_line", after=[last])
            (early,) = call(add_two, [side], (early, to_hid(early, 1), []), "early_line")
            (pair,) = call(
                stack_up, [struct((4 * rows, 2 * width), BF)], ([pair, to_hid(pair, 1)],), "pair_stack",
                after=[early],
            )
            half = struct((rows * 2, width), BF)
            late, mine, twin = call(
                add_up_more, [eighth(n_late), half, half], (late,), "late_plane", after=[pair]
            )
            pairs = [pair] + [to_chip(pair, m) for m in (1, 2, 3)]
            (late,) = call(add_two, [eighth(n_late)], (late, to_hid(late, 1), []), "late_line")
            (early,) = call(
                join_sides, [eighth(n_early)], (early, to_hid(early, 2)), "early_line", spot=spot, after=[late]
            )
            (pair,) = call(
                stack_up, [struct((16 * rows, 2 * width), BF)], (pairs,), "pair_stack", after=[early]
            )
            last = pair
            early = [early] + [to_chip(early, m) for m in (1, 2, 3)]
            edge_gradient, last = call(
                edge_end(rows, fanout, step),
                [final(n_edges, edge_width)],
                (edge_grad, first_low, mf),
                "edge_end",
                after=[last],
                token=True,
            )
            returned = [mine, to_core(twin)]
            node_gradient, last = call(
                node_end,
                [final(rows, width)],
                (returned, send, first_grad, node, mf),
                "node_end",
                after=[last],
                token=True,
            )
            (late,) = call(
                add_two, [eighth(n_late)], (late, to_hid(late, 2), []), "late_line", after=[last]
            )
            (early,) = call(
                stack_up, [struct((n_early // 2, width), BF)], (early,), "early_stack", after=[late]
            )
            early = [early, to_core(early)]
            late = [late] + [to_chip(late, m) for m in (1, 2, 3)]
            pairs = [pair, to_core(pair)]
        else:
            late = [lax.psum(late.astype(F32), ("res", "hid"))]
            early = [early]
            pairs = [lax.all_gather(pair, "hid", axis=0, tiled=True)]
            expand_grad, reduce_grad = call(
                feed_weights,
                [struct((width, share), F32), struct((share, width), F32)],
                (pairs, *feed_own),
                "feed_weights",
                after=[node],
            )
            returned = exchange(slot)
            (edge_gradient,) = call(
                edge_end(rows, fanout, step), [final(n_edges, edge_width)], (edge_grad, first_low, mf), "edge_end"
            )
            (node_gradient,) = call(
                node_end, [final(rows, width)], (returned, send, first_grad, node, mf), "node_end"
            )
        (
            edge_first_grad, edge_second_grad, edge_third_grad, third_grad, vec, edge_vecs, expand_bias_grad,
            last,
        ) = call(
            unpack_early,
            [
                final(edge_width, ef.shape[1]), final(edge_width, edge_width), final(edge_width, edge_width),
                final(hidden, width), [final(1, width)] * 6, [final(1, edge_width)] * 5, final(1, share),
            ],
            (early,),
            "unpack_early",
            [pltpu.VMEM((n_early, width), F32)],
            limit=16,
            spot=spot,
            token=True,
        )
        if tuned:
            expand_grad, reduce_grad = call(
                feed_weights,
                [struct((width, share), F32), struct((share, width), F32)],
                (pairs[:1], *feed_own),
                "feed_weights",
                after=[last],
            )
            (late,) = call(
                stack_up, [struct((n_late // 2, width), BF)], (late,), "late_stack", after=[expand_grad]
            )
            last = late
            late = [late, to_core(late)]
            expand_grad, reduce_grad, last = call(
                feed_weights_more,
                [Final(width, share), Final(share, width)],
                (pairs[1:], *feed_own, expand_grad, reduce_grad),
                "feed_weights_more",
                after=[last],
                token=True,
            )
            last = [last]
        else:
            last = []
        c = mf.shape[0]
        first_weight_grad, second_weight_grad, message_vec = call(
            unpack_late,
            [
                Cut(n_late, width, c),
                Cut(n_late, width, c + hidden, c),
                [Cut(n_late, width, c + hidden + k + 1, c + hidden + k) for k in range(2)],
            ],
            (late,),
            "unpack_late",
            spot=spot,
            after=last,
        )
        if not tuned:
            expand_grad, reduce_grad = [lax.psum(v, "res") for v in (expand_grad, reduce_grad)]
        vec, edge_vecs, message_vec = [[v[0] for v in group] for group in (vec, edge_vecs, message_vec)]

        back = lambda v: v.reshape(fanout, rows, edge_width).transpose(1, 0, 2)
        return (
            node_result,
            back(edge_result),
            node_gradient,
            back(edge_gradient),
            first_weight_grad,
            message_vec[0],
            second_weight_grad,
            message_vec[1],
            third_grad,
            vec[5],
            vec[3],
            vec[4],
            expand_grad,
            expand_bias_grad[0],
            reduce_grad,
            vec[0],
            vec[1],
            vec[2],
            edge_first_grad.T,
            edge_vecs[4],
            edge_second_grad,
            edge_vecs[3],
            edge_third_grad,
            edge_vecs[2],
            edge_vecs[0],
            edge_vecs[1],
        )

    both = ("res", "hid")
    rows2, rows3 = P(both, None), P(both, None, None)
    placed = (
        rows2, rows3, rows3, rows2, P(both),
        P(), P(), P(), P(), P(), P(), P(), P(),
        P(None, "hid"), P("hid"), P("hid", None),
        P(), P(), P(), P(), P(), P(), P(), P(), P(), P(), P(),
        rows2, rows3,
    )
    given = (
        rows2, rows3, rows2, rows3,
        P(), P(), P(), P(), P(), P(), P(), P(),
        P(None, "hid"), P("hid"), P("hid", None),
        P(), P(), P(), P(), P(), P(), P(), P(), P(), P(), P(),
    )
    return jax.shard_map(body, mesh=mesh, in_specs=placed, out_specs=given, check_vma=False)
```

```python
import jax
import jax.numpy as jnp
from jax import lax
from jax.experimental import pallas as pl
from jax.experimental.pallas import tpu as pltpu
from jax.sharding import PartitionSpec as P

BF = jnp.bfloat16
F32 = jnp.float32
LEAN = 0.7978845608028654
CUBE = LEAN * 0.044715
MIB = 1 << 20
KEEP = pl.BlockSpec(memory_space=pltpu.VMEM)


def dot(left, right):
    return jnp.dot(left, right, preferred_element_type=F32)


def dot_nt(left, right):
    return lax.dot_general(left, right, (((1,), (1,)), ((), ())), preferred_element_type=F32)


def dot_tn(left, right):
    return lax.dot_general(left, right, (((0,), (0,)), ((), ())), preferred_element_type=F32)


def smooth(v):
    t = jnp.tanh(v * (LEAN + CUBE * (v * v)))
    half = 0.5 * v
    return half + half * t


def smooth_slope(v):
    v2 = v * v
    t = jnp.tanh(v * (LEAN + CUBE * v2))
    half = 0.5 * v
    slope = (0.5 + 0.5 * t) + (half - half * (t * t)) * (LEAN + (3.0 * CUBE) * v2)
    return half + half * t, slope


def smooth_low(v):
    v = v.astype(BF)
    t = jnp.tanh(v * (BF(LEAN) + BF(CUBE) * (v * v)))
    half = BF(0.5) * v
    return half + half * t


def smooth_slope_low(v):
    v = v.astype(BF)
    v2 = v * v
    t = jnp.tanh(v * (BF(LEAN) + BF(CUBE) * v2))
    half = BF(0.5) * v
    slope = (BF(0.5) + BF(0.5) * t) + (half - half * (t * t)) * (BF(LEAN) + BF(3.0 * CUBE) * v2)
    return half + half * t, slope


def centred(x):
    center = x - jnp.mean(x, axis=-1, keepdims=True)
    rate = lax.rsqrt(jnp.mean(center * center, axis=-1, keepdims=True) + 1e-05)
    return center * rate, rate


def norm_pull(hat, rate, gain, up):
    g = up * gain
    return rate * (
        g - jnp.mean(g, axis=-1, keepdims=True) - hat * jnp.mean(g * hat, axis=-1, keepdims=True)
    )


def tiled_add(rows, part):
    n, width = part.shape
    return (rows.reshape(-1, n, width) + part[None]).reshape(rows.shape)


def over(count, chunk):
    if count == 1:
        chunk(0, 0)
    else:
        lax.fori_loop(0, count, chunk, 0)


def aligned(index, size):
    return index if isinstance(index, int) else pl.multiple_of(index, size)


def fold(rows, n):
    return jnp.sum(rows.reshape(-1, n, rows.shape[-1]), axis=0)


class Final:
    def __init__(self, *shape):
        self.shape, self.dtype = shape, F32


class Cut(Final):
    def __init__(self, n, width, stop, start=0):
        super().__init__(stop - start, width)
        self.whole, self.start = (n, width), start


def call(body, outs, args, name, scratch=(), limit=28, spot=None, after=(), far=False, token=False):
    if token:
        outs = list(outs) + [pltpu.VMEM((8, 128), F32)]
    flat_outs, out_tree = jax.tree.flatten(list(outs), is_leaf=lambda v: hasattr(v, "dtype"))
    ends = [k for k, v in enumerate(flat_outs) if isinstance(v, Final)]
    cuts = [v for v in flat_outs if isinstance(v, Cut)]
    held_outs = [pltpu.VMEM(flat_outs[k].shape, flat_outs[k].dtype) for k in ends if not cuts]
    if cuts:
        held_outs = [pltpu.VMEM(cuts[0].whole, F32)]
    if ends:
        held_outs.append(pltpu.SemaphoreType.DMA((len(ends),)))
    shapes = [pltpu.HBM(v.shape, v.dtype) if isinstance(v, Final) else v for v in flat_outs]
    out_specs = [pl.BlockSpec(memory_space=pltpu.HBM) if isinstance(v, Final) else KEEP for v in flat_outs]
    space = pltpu.HBM if far else pltpu.VMEM
    args = jax.tree.map(lambda v: pltpu.with_memory_space_constraint(v, space), list(args))
    specs = jax.tree.map(lambda v: pl.BlockSpec(memory_space=space), args)
    lead = 0
    if spot is not None:
        args, specs, lead = [spot] + args, [pl.BlockSpec(memory_space=pltpu.SMEM)] + specs, 1
    n, more = len(args), len(after)
    scratch = list(scratch)
    if far:
        flat, tree = jax.tree.flatten(args[lead:])
        scratch += [pltpu.VMEM(v.shape, v.dtype) for v in flat] + [pltpu.SemaphoreType.DMA((len(flat),))]

    def run(*refs):
        given, rest = refs[:n], refs[n + more :]
        results, rest = list(jax.tree.leaves(list(rest[: len(outs)]))), rest[len(outs) :]
        targets = [results[k] for k in ends]
        if ends:
            count = len(held_outs)
            rest, kept, out_sems = rest[:-count], rest[-count:-1], rest[-1]
            for k, v in zip(ends, kept):
                results[k] = v
        if far:
            count = len(flat)
            rest, held, sems = rest[: -count - 1], rest[-count - 1 : -1], rest[-1]
            copies = [
                pltpu.make_async_copy(src, dst, sems.at[k])
                for k, (src, dst) in enumerate(zip(jax.tree.leaves(list(given[lead:])), held))
            ]
            for copy in copies:
                copy.start()
            for copy in copies:
                copy.wait()
            given = list(given[:lead]) + jax.tree.unflatten(tree, held)
        produced = list(jax.tree.unflatten(out_tree, results))
        if token:
            produced.pop()[...] = jnp.zeros((8, 128), F32)
        if cuts:
            produced = [kept[0]]
        body(*given, *produced, *rest)
        if cuts:
            kept = [kept[0].at[v.start : v.start + v.shape[0], :] for v in cuts]
        if ends:
            copies = [
                pltpu.make_async_copy(src, dst, out_sems.at[k])
                for k, (src, dst) in enumerate(zip(kept, targets))
            ]
            for copy in copies:
                copy.start()
            for copy in copies:
                copy.wait()

    return pl.pallas_call(
        run,
        out_shape=jax.tree.unflatten(out_tree, shapes),
        in_specs=specs + [pl.BlockSpec(memory_space=pl.ANY)] * more,
        out_specs=jax.tree.unflatten(out_tree, out_specs),
        scratch_shapes=scratch + held_outs,
        compiler_params=pltpu.CompilerParams(vmem_limit_bytes=limit * MIB),
        name=name,
    )(*args, *after)


def struct(shape, dtype):
    return pltpu.VMEM(shape, dtype)


def shards(own, packed):
    if len(packed) == 3:
        we, web, wr = packed
        for h in range(we.shape[0]):
            yield we[h], web[h : h + 1, :], wr[h]
        return
    yield own[0][...], own[1][...], own[2][...]
    (ref,) = packed
    n, width = ref.shape[0] // 8, ref.shape[1] // 3
    part = n // 9 * 4
    for h in range(3):
        at = slice(h * width, (h + 1) * width)
        we = jnp.concatenate([ref[r * n : r * n + part, at] for r in range(8)], axis=0)
        wr = jnp.concatenate([ref[r * n + part : r * n + 2 * part, at] for r in range(8)], axis=0)
        bias = ref[2 * part : n, at].astype(F32)
        yield we, bias[0:1] + bias[1:2], wr


def feed(mid, own, packed, rb, slopes):
    mid_low = mid.astype(BF)
    total = mid + rb
    for h, (we, web, wr) in enumerate(shards(own, packed)):
        act, slope = smooth_slope(dot(mid_low, we) + web)
        slopes[h] = slope.astype(BF)
        total = total + dot(act.astype(BF), wr)
    return mid_low, total


def joined(parts):
    if len(parts) == 1:
        return parts[0][...]
    if len(parts) == 2:
        n = parts[0].shape[0] // 4
        return jnp.concatenate([v[m * n : (m + 1) * n] for m in range(4) for v in parts], axis=0)
    near, far = parts[: len(parts) // 2], parts[len(parts) // 2 :]
    rows = []
    for mine, other in zip(near, far):
        half = mine.shape[0] // 2
        rows += [mine[:half], other[half:]]
    return jnp.concatenate(rows, axis=0)


def dealt(outs, value):
    n = value.shape[0] // len(outs)
    for m, out in enumerate(outs):
        out[...] = value[m * n : (m + 1) * n].astype(out.dtype)


def halved(spot, pay, keep, send):
    n = keep.shape[0] // 4
    for m in range(4):
        chip = (spot[1] ^ m) * 2
        keep[m * n : (m + 1) * n, :] = pay[pl.ds(pl.multiple_of((chip + spot[0]) * n, n), n), :]
        send[m * n : (m + 1) * n, :] = pay[pl.ds(pl.multiple_of((chip + 1 - spot[0]) * n, n), n), :]


def message_mean(summed, counts, mt, mtb):
    mean = summed / counts
    high = mean.astype(BF)
    rest = (mean - high.astype(F32)).astype(BF)
    return dot(high, mt) + dot(rest, mt) + mtb


def solution(mesh):
    n_res, n_hid = mesh.shape["res"], mesh.shape["hid"]
    tuned = (n_res, n_hid) == (8, 4)
    pair = [(i, i ^ 1) for i in range(n_res)]

    def to_chip(v, m):
        return lax.ppermute(v, "res", [(i, i ^ (2 * m)) for i in range(n_res)])

    def to_core(v):
        return lax.ppermute(v, "res", pair)

    def to_hid(v, m):
        return lax.ppermute(v, "hid", [(i, i ^ m) for i in range(n_hid)])

    def exchange(parts):
        if not tuned:
            n, width = parts[0].shape
            blocks = parts[0].reshape(n_res, n // n_res, width)
            return [lax.all_to_all(blocks, "res", 0, 0, tiled=True).reshape(n, width)]
        near = [parts[0]] + [to_chip(parts[m], m) for m in (1, 2, 3)]
        return near + [to_core(v) for v in near]

    def prepare_send(spot, table, nodes, weights, away_out, send_out, piece_out):
        rows, width = nodes.shape
        n = table.shape[1]
        lines = lax.broadcasted_iota(jnp.int32, (rows, n), 0)
        same = lax.broadcasted_iota(jnp.int32, (rows, rows), 0) == lax.broadcasted_iota(
            jnp.int32, (rows, rows), 1
        )
        same = same.astype(F32).astype(BF)
        each = n_res // len(away_out)
        for q in range(n_res):
            line = table[pl.ds(q ^ spot[3], 1), :]
            chosen = (lines == line).astype(F32).astype(BF)
            at = slice(q % each * n, (q % each + 1) * n)
            away_out[q // each][at, :] = dot_tn(chosen, nodes[...]).astype(BF)
            send_out[q * n : (q + 1) * n, :] = dot_tn(chosen, same).astype(BF)
        if piece_out:
            (out,) = piece_out
            we, wr, bias = weights
            n = width // 8
            at = pl.ds(pl.multiple_of(spot[3] * n, n), n)
            out[:n, :] = we[at, :]
            out[n : 2 * n, :] = wr[at, :]
            high = bias[...].astype(BF).astype(F32)
            rest = jnp.concatenate([high, bias[...] - high, jnp.zeros((n // 4 - 2, width), F32)], axis=0)
            out[2 * n :, :] = rest.astype(BF)

    def prepare_rest(
        spot, slots, counts, vecs, edge_vecs, edges, pick_out, counts_out, vecs_out, edge_out, edges_out
    ):
        edges_out[...] = edges[...]
        rows, fanout = slots.shape
        lanes = lax.broadcasted_iota(jnp.int32, (rows, pick_out.shape[1]), 1)
        moved = slots[...] ^ (spot[3] * (pick_out.shape[1] // n_res))
        for k in range(fanout):
            chosen = (lanes == moved[:, k : k + 1]).astype(F32).astype(BF)
            pick_out[k * rows : (k + 1) * rows, :] = chosen
        same = lax.broadcasted_iota(jnp.int32, (rows, rows), 0) == lax.broadcasted_iota(
            jnp.int32, (rows, rows), 1
        )
        many = jnp.where(same, jnp.broadcast_to(counts[...].astype(F32), (rows, rows)), 0.0)
        counts_out[...] = jnp.sum(many, axis=1, keepdims=True)
        edge_out[...] = jnp.zeros_like(edge_out)
        for k, v in enumerate(vecs):
            vecs_out[k : k + 1, :] = v[...]
        for k, v in enumerate(edge_vecs):
            edge_out[k : k + 1, :] = v[...]

    def pass_one(rows, fanout, step):
        span = step * rows

        def kernel(
            arrived, nodes, edges, pick, counts, mf, ms, mt, vecs, mid_out, mid_low_out, sums,
        ):
            mfb, msb, mtb, mg, msh = [vecs[k : k + 1, :] for k in range(5)]
            width = nodes.shape[1]
            query = dot(joined(arrived), mf[width : 2 * width]).astype(BF)
            part = dot(nodes[...], mf[:width]) + mfb
            lower = mf[2 * width :]
            lots = jnp.broadcast_to(counts[...], (rows, ms.shape[1]))
            sums[...] = jnp.zeros_like(sums)

            def chunk(i, carry):
                at = pl.ds(aligned(i * span, span), span)
                pre = dot(pick[at, :], query) + dot(edges[at, :], lower)
                act = smooth_low(tiled_add(pre, part)).astype(BF)
                act = smooth_low(dot(act, ms[...]) + msb)
                total = sums[...]
                for j in range(step):
                    total = total + jnp.where(
                        lots > jnp.float32(i * step + j), act[j * rows : (j + 1) * rows], 0.0
                    )
                sums[...] = total
                return carry

            over(fanout // step, chunk)
            first = nodes[...].astype(F32) + message_mean(sums[...], counts[...], mt[...], mtb)
            mid = centred(first)[0] * mg + msh
            mid_out[...] = mid
            mid_low_out[...] = mid.astype(BF)

        return kernel

    def feed_shard(mids, we, web, wr, outs):
        mid = jnp.concatenate([v[...] for v in mids], axis=0)
        act = smooth(dot(mid, we[...]) + web[...]).astype(BF)
        dealt(outs, dot(act, wr[...]))

    def feed_end(mid, parts, vecs, send, new_out, low_out, away_out):
        rb, fg, fsh = [vecs[k : k + 1, :] for k in (5, 6, 7)]
        second = mid[...] + rb
        for v in parts:
            second = second + v[...].astype(F32)
        new = centred(second)[0] * fg + fsh
        new_out[...] = new
        low = new.astype(BF)
        low_out[...] = low
        dealt(away_out, dot(send[...], low))

    def feed_pass(mid, own, packed, vecs, send, slopes_out, second_out, new_out, low_out, away_out):
        rb, fg, fsh = [vecs[k : k + 1, :] for k in (5, 6, 7)]
        _, second = feed(mid[...], own, packed, rb, slopes_out)
        second_out[...] = second
        new = centred(second)[0] * fg + fsh
        new_out[...] = new
        low = new.astype(BF)
        low_out[...] = low
        dealt(away_out, dot(send[...], low))

    def pass_two(rows, fanout, step):
        span = step * rows

        def kernel(
            arrived, state, low, edges, pick, counts, mf, ms, mt, vecs, ef, es, et, edge_vecs,
            edge_out, act_out, slope1_out, slope2_out, first_out, summed_out, mid_out, mid_low_out, sums,
        ):
            mfb, msb, mtb, mg, msh = [vecs[k : k + 1, :] for k in range(5)]
            efb, esb, etb, eg, esh = [edge_vecs[k : k + 1, :] for k in range(5)]
            width = state.shape[1]
            received = joined(arrived)
            key = dot_nt(received, ef[:, width : 2 * width]).astype(BF)
            edge_part = dot_nt(low[...], ef[:, :width]) + efb
            edge_lower = ef[:, 2 * width :]
            query = dot(received, mf[width : 2 * width]).astype(BF)
            part = dot(low[...], mf[:width]) + mfb
            lower = mf[2 * width :]
            lots = jnp.broadcast_to(counts[...], (rows, ms.shape[1]))
            sums[...] = jnp.zeros_like(sums)

            def chunk(i, carry):
                at = pl.ds(aligned(i * span, span), span)
                chosen = pick[at, :]
                old = edges[at, :]
                pre = dot(chosen, key) + dot_nt(old, edge_lower)
                act = smooth_low(tiled_add(pre, edge_part)).astype(BF)
                act = smooth_low(dot(act, es[...]) + esb).astype(BF)
                total = old.astype(F32) + dot(act, et[...]) + etb
                fresh = centred(total)[0] * eg + esh
                edge_out[at, :] = fresh
                pre = dot(chosen, query) + dot(fresh.astype(BF), lower)
                act, slope = smooth_slope_low(tiled_add(pre, part))
                act = act.astype(BF)
                act_out[at, :] = act
                slope1_out[at, :] = slope.astype(BF)
                act, slope = smooth_slope_low(dot(act, ms[...]) + msb)
                total = sums[...]
                for j in range(step):
                    valid = lots > jnp.float32(i * step + j)
                    total = total + jnp.where(valid, act[j * rows : (j + 1) * rows], 0.0)
                    slope2_out[pl.ds(aligned(i * span + j * rows, rows), rows), :] = jnp.where(
                        valid, slope[j * rows : (j + 1) * rows], 0.0
                    ).astype(BF)
                sums[...] = total
                return carry

            over(fanout // step, chunk)
            summed_out[...] = sums[...].astype(BF)
            first = state[...] + message_mean(sums[...], counts[...], mt[...], mtb)
            first_out[...] = first
            mid = centred(first)[0] * mg + msh
            mid_out[...] = mid
            mid_low_out[...] = mid.astype(BF)

        return kernel

    def edge_turn(rows, fanout, step):
        span = step * rows

        def kernel(
            arrived, low, edges, up, pick, ef, es, et, edge_vecs,
            result_out, grad_out, act1_out, act2_out, top_out, mid_out, bottom_out,
            slot_out, node_out, vec_out, slots, node, marks,
        ):
            width = low.shape[1]
            efb, esb, etb, eg, esh = [edge_vecs[k : k + 1, :] for k in range(5)]
            key = dot_nt(joined(arrived), ef[:, width : 2 * width]).astype(BF)
            edge_part = dot_nt(low[...], ef[:, :width]) + efb
            edge_lower = ef[:, 2 * width :]
            slots[...] = jnp.zeros_like(slots)
            node[...] = jnp.zeros_like(node)
            marks[...] = jnp.zeros_like(marks)

            def chunk(i, carry):
                at = pl.ds(aligned(i * span, span), span)
                chosen = pick[at, :]
                old = edges[at, :]
                pre = dot(chosen, key) + dot_nt(old.astype(BF), edge_lower)
                act, slope1 = smooth_slope_low(tiled_add(pre, edge_part))
                act1 = act.astype(BF)
                act1_out[at, :] = act1
                act, slope2 = smooth_slope_low(dot(act1, es[...]) + esb)
                act2 = act.astype(BF)
                act2_out[at, :] = act2
                total = old + dot(act2, et[...]) + etb
                hat, rate = centred(total)
                result_out[at, :] = hat * eg + esh
                above = up[at, :].astype(F32)
                sum_grad = norm_pull(hat, rate, eg, above)
                top = sum_grad.astype(BF)
                top_out[at, :] = top
                mid = dot_nt(top, et[...]) * slope2
                mid_low = mid.astype(BF)
                mid_out[at, :] = mid_low
                bottom = dot_nt(mid_low, es[...]) * slope1
                bottom_low = bottom.astype(BF)
                bottom_out[at, :] = bottom_low
                grad_out[at, :] = sum_grad + dot(bottom_low, edge_lower)
                marks[0] += fold(above * hat, 8)
                marks[1] += fold(above, 8)
                marks[2] += fold(sum_grad, 8)
                marks[3] += fold(mid, 8)
                node[...] += fold(bottom, rows)
                slots[...] += dot_tn(chosen, bottom_low)
                return carry

            over(fanout // step, chunk)
            dealt(slot_out, slots[...])
            node_out[...] = node[...].astype(BF)
            vec_out[...] = jnp.zeros_like(vec_out)
            for j in range(4):
                vec_out[j : j + 1, :] = jnp.sum(marks[j], axis=0, keepdims=True)
            vec_out[4:5, :] = jnp.sum(node[...], axis=0, keepdims=True)

        return kernel

    def edge_weights(arrived, low, edges, act1, act2, top, mid, bottom, slot, node, pack_out):
        n, wide = act1.shape[1], low.shape[1]
        slot = jnp.concatenate([v[...] for v in slot], axis=0)
        pack_out[:n, :] = dot_tn(node[...], low[...]).astype(BF)
        pack_out[n : 2 * n, :] = dot_tn(slot, joined(arrived)).astype(BF)
        pack_out[2 * n :, :] = jnp.zeros((pack_out.shape[0] - 2 * n, wide), BF)
        pack_out[2 * n : 3 * n, :n] = dot_tn(act1[...], mid[...]).astype(BF)
        pack_out[2 * n : 3 * n, 256 : 256 + n] = dot_tn(act2[...], top[...]).astype(BF)
        lower = dot_tn(bottom[...], edges[...].astype(BF)).astype(BF)
        pack_out[3 * n :, :n] = lower[: n // 2]
        pack_out[3 * n :, 256 : 256 + n] = lower[n // 2 :]

    def node_turn(
        spot, returned, up, node, send, second, slopes, first, counts, summed, ef, mt, vecs,
        own, packed, pack, edge_vec, mid_low, pair_out, sum_out, pull_out, pay_out, pay,
    ):
        width = up.shape[1]
        key_low = dot_tn(send[...], joined(returned)).astype(BF)
        new_grad = (
            up[...].astype(F32) + dot(node[...], ef[:, :width]) + dot(key_low, ef[:, width : 2 * width])
        )
        hat, rate = centred(second[...])
        sum_grad = norm_pull(hat, rate, vecs[6:7, :], new_grad)
        marks = [sum_grad, new_grad * hat, new_grad]
        low = sum_grad.astype(BF)
        pair_out[:, :width] = mid_low[...]
        pair_out[:, width:] = low
        mid_grad = sum_grad
        bias = []
        for h, (we, _, wr) in enumerate(shards(own, packed)):
            expand = dot_nt(low, wr) * slopes[h].astype(F32)
            bias.append(jnp.sum(expand, axis=0, keepdims=True))
            mid_grad = mid_grad + dot_nt(expand.astype(BF), we)
        hat, rate = centred(first[...])
        first_grad = norm_pull(hat, rate, vecs[3:4, :], mid_grad)
        sum_out[...] = first_grad
        marks += [mid_grad * hat, mid_grad, first_grad]
        marks = [jnp.sum(v, axis=0, keepdims=True) for v in marks]
        rows_low = (first_grad / counts[...]).astype(BF)
        pull_out[...] = dot_nt(rows_low, mt[...])
        third = dot_tn(summed[...], rows_low).astype(BF)
        head, hidden = pack.shape[0], third.shape[0]
        pay[:head, :] = pack[...]
        pay[head : head + hidden, :] = third
        pay[head + hidden :, :] = jnp.zeros((pay.shape[0] - head - hidden, width), BF)
        rows = jnp.concatenate(marks + [jnp.zeros((10, width), F32)], axis=0)
        at = lax.broadcasted_iota(jnp.int32, rows.shape, 0)
        share = bias[0].shape[1]
        for h, v in enumerate(bias):
            line = 6 + ((spot[2] ^ h) if tuned else h)
            if share < width:
                v = jnp.concatenate([v, jnp.zeros((1, width - share), F32)], axis=1)
            rows = jnp.where(at == line, v, rows)
        pay[head + hidden : head + hidden + 16, :] = rows.astype(BF)
        pay[head + hidden + 16 : head + hidden + 32, : edge_vec.shape[1]] = jnp.concatenate(
            [edge_vec[...], jnp.zeros_like(edge_vec)], axis=0
        ).astype(BF)
        if len(pay_out) == 1:
            pay_out[0][...] = pay[...]
        else:
            halved(spot, pay, *pay_out)

    def message_second(rows, fanout, step):
        span = step * rows

        def kernel(pull, act, slope2, second_out, weight_out, vec_out, marks):
            marks[...] = jnp.zeros_like(marks)

            def chunk(i, carry):
                at = pl.ds(aligned(i * span, span), span)
                second = slope2[at, :].astype(F32).reshape(step, rows, -1) * pull[...][None]
                marks[...] += jnp.sum(second, axis=0)
                second_out[at, :] = second.reshape(span, -1).astype(BF)
                return carry

            over(fanout // step, chunk)
            weight_out[...] = dot_tn(act[...], second_out[...]).astype(BF)
            vec_out[...] = jnp.zeros_like(vec_out)
            vec_out[0:1, :] = jnp.sum(marks[...], axis=0, keepdims=True)

        return kernel

    def message_first(rows, fanout, step):
        span = step * rows

        def kernel(
            arrived, low, edges, pick, second, slope1, ms, weight, vec,
            first_low_out, slot_out, node_out, pay, slots, node,
        ):
            width = low.shape[1]
            slots[...] = jnp.zeros_like(slots)
            node[...] = jnp.zeros_like(node)

            def chunk(i, carry):
                at = pl.ds(aligned(i * span, span), span)
                first = dot_nt(second[at, :], ms[...]) * slope1[at, :].astype(F32)
                node[...] += fold(first, rows)
                first = first.astype(BF)
                first_low_out[at, :] = first
                slots[...] += dot_tn(pick[at, :], first)
                return carry

            over(fanout // step, chunk)
            slot = slots[...].astype(BF)
            dealt(slot_out, slot)
            node_low = node[...].astype(BF)
            node_out[...] = node_low
            hidden, last = ms.shape[0], 2 * width + edges.shape[1]
            pay[:width, :] = dot_tn(low[...], node_low).astype(BF)
            pay[width : 2 * width, :] = dot_tn(joined(arrived), slot).astype(BF)
            pay[2 * width : last, :] = dot_tn(edges[...].astype(BF), first_low_out[...]).astype(BF)
            pay[last : last + hidden, :] = weight[...]
            pay[last + hidden :, :] = jnp.zeros((pay.shape[0] - last - hidden, hidden), BF)
            vecs = [jnp.sum(node[...], axis=0, keepdims=True), vec[0:1, :], jnp.zeros((14, hidden), F32)]
            pay[last + hidden : last + hidden + 16, :] = jnp.concatenate(vecs, axis=0).astype(BF)

        return kernel

    def feed_products(pairs, we, web, wr):
        n = we.shape[0]
        mid = jnp.concatenate([v[:, :n] for v in pairs], axis=0)
        up = jnp.concatenate([v[:, n:] for v in pairs], axis=0)
        act, slope = smooth_slope_low(dot(mid, we[...]) + web[...])
        expand = dot_nt(up, wr[...]) * slope
        return dot_tn(mid, expand.astype(BF)), dot_tn(act, up)

    def feed_weights(pairs, we, web, wr, expand_out, reduce_out):
        expand_out[...], reduce_out[...] = feed_products(pairs, we, web, wr)

    def feed_weights_more(pairs, we, web, wr, expand, reduce, expand_out, reduce_out):
        left, right = feed_products(pairs, we, web, wr)
        expand_out[...], reduce_out[...] = expand[...] + left, reduce[...] + right

    def node_end(returned, send, first_grad, node, mf, out):
        width = out.shape[1]
        query_low = dot_tn(send[...], joined(returned)).astype(BF)
        out[...] = (
            first_grad[...] + dot_nt(node[...], mf[:width]) + dot_nt(query_low, mf[width : 2 * width])
        )

    def edge_end(rows, fanout, step):
        span = step * rows

        def kernel(grad, first_low, mf, out):
            lower = mf[mf.shape[0] - grad.shape[1] :]

            def chunk(i, carry):
                at = pl.ds(aligned(i * span, span), span)
                out[at, :] = grad[at, :] + dot_nt(first_low[at, :], lower)
                return carry

            over(fanout // step, chunk)

        return kernel

    def split_chips(keep, got, outs):
        n = keep.shape[0] // len(outs)
        for m, out in enumerate(outs):
            at = slice(m * n, (m + 1) * n)
            out[:n, :] = (keep[at, :].astype(F32) + got[at, :].astype(F32)).astype(BF)

    def split_chips_more(keep, got, more, outs):
        split_chips(keep, got, outs)
        for v, out in zip(more, outs):
            out[out.shape[0] - v.shape[0] :, :] = v[...]

    def add_up(parts, out):
        n = out.shape[0]
        total = parts[0][:n, :].astype(F32)
        for v in parts[1:]:
            total = total + v[:n, :].astype(F32)
        out[...] = total.astype(BF)

    def add_up_more(spot, parts, keep, send, mine, twin, out):
        add_up(parts, out)
        n, side = keep.shape[1], spot[2] % 2
        keep[...] = out[:, pl.ds(pl.multiple_of(side * n, n), n)]
        send[...] = out[:, pl.ds(pl.multiple_of((1 - side) * n, n), n)]
        n = mine.shape[0] // len(parts)
        for m, v in enumerate(parts):
            at, top = slice(m * n, (m + 1) * n), out.shape[0]
            mine[at, :] = v[top : top + n, :]
            twin[at, :] = v[top + n : top + 2 * n, :]

    def add_up_join(parts, more, out):
        n = more.shape[0]
        out[:n, :] = more[...]
        total = parts[0][...].astype(F32)
        for v in parts[1:]:
            total = total + v[...].astype(F32)
        out[n:, :] = total.astype(BF)

    def add_up_sides(spot, parts, pay, keep, send, pay_keep, pay_send, total):
        add_up(parts, total)
        halved(spot, pay, pay_keep, pay_send)
        n, side = keep.shape[1], spot[2] // 2
        keep[...] = total[:, pl.ds(pl.multiple_of(side * n, n), n)]
        send[...] = total[:, pl.ds(pl.multiple_of((1 - side) * n, n), n)]

    def join_near(spot, mine, other, out):
        join_sides(spot, mine, other, out, spot[2] % 2)

    def join_far(spot, mine, other, out):
        join_sides(spot, mine, other, out, spot[2] // 2)

    def join_sides(spot, mine, other, out, side):
        n = mine.shape[1]
        out[:, pl.ds(pl.multiple_of(side * n, n), n)] = mine[...]
        out[:, pl.ds(pl.multiple_of((1 - side) * n, n), n)] = other[...]

    def sort_cores(parts, mine, twin):
        n = mine.shape[0] // len(parts)
        for m, v in enumerate(parts):
            at = slice(m * n, (m + 1) * n)
            mine[at, :] = v[:n, :]
            twin[at, :] = v[n : 2 * n, :]

    def add_two(left, right, more, out):
        n = left.shape[0]
        out[:n, :] = (left[...].astype(F32) + right[...].astype(F32)).astype(BF)
        if more:
            out[n:, :] = more[0][...]

    def to_chips(parts):
        return [parts[0]] + [to_chip(parts[m], m) for m in (1, 2, 3)]

    def spread(own):
        parts = [own] + [to_chip(own, m) for m in (1, 2, 3)]
        return parts + [to_core(v) for v in parts]

    def laid_out(spot, parts, total):
        n = parts[0].shape[0]
        for k, v in enumerate(parts):
            at = (2 * (spot[1] ^ (k % 4)) + (spot[0] ^ (k // 4))) * n
            total[pl.ds(pl.multiple_of(at, n), n), :] = v[...].astype(total.dtype)

    def lay_pair(spot, stacks, total):
        n = total.shape[0] // 8
        for k in range(8):
            at = (2 * (spot[1] ^ (k % 4)) + (spot[0] ^ (k // 4))) * n
            top = k % 4 * n
            total[pl.ds(pl.multiple_of(at, n), n), :] = stacks[k // 4][top : top + n, :].astype(total.dtype)

    def stack_up(parts, out):
        n = parts[0].shape[0]
        for m, v in enumerate(parts):
            out[m * n : (m + 1) * n, :] = v[...]

    def unpack_early(
        spot, parts, first_out, second_out, third_out, message_out, vec_out, edge_vec_out, bias_out, total,
    ):
        if len(parts) == 1:
            total[...] = parts[0][...]
        else:
            lay_pair(spot, parts, total)
        n, wide = second_out.shape[0], message_out.shape[1]
        first_out[:, :wide] = total[:n, :]
        first_out[:, wide : 2 * wide] = total[n : 2 * n, :]
        second_out[...] = total[2 * n : 3 * n, :n]
        third_out[...] = total[2 * n : 3 * n, 256 : 256 + n]
        at = 3 * n + n // 2
        first_out[: n // 2, 2 * wide :] = total[3 * n : at, :n]
        first_out[n // 2 :, 2 * wide :] = total[3 * n : at, 256 : 256 + n]
        hidden = message_out.shape[0]
        message_out[...] = total[at : at + hidden, :]
        for k, out in enumerate(vec_out):
            out[...] = total[at + hidden + k : at + hidden + k + 1, :]
        for k, out in enumerate(edge_vec_out):
            out[...] = total[at + hidden + 16 + k : at + hidden + 17 + k, :n]
        vecs = total[at + hidden : at + hidden + 16, :]
        line = lax.broadcasted_iota(jnp.int32, vecs.shape, 0) == 6 + spot[2]
        bias = jnp.sum(jnp.where(line, vecs, 0.0), axis=0, keepdims=True)
        bias_out[...] = bias[:, : bias_out.shape[1]]

    def unpack_late(spot, parts, total):
        if len(parts) == 1:
            total[...] = parts[0][...]
        else:
            lay_pair(spot, parts, total)

    def split_relay(left, right, left_out, right_out):
        n = left_out.shape[1]
        left_out[...] = left[:, :n]
        right_out[...] = right[:, n:]

    def stack_relay(parts, left, right, out):
        n, half = left.shape
        for m, v in enumerate(parts):
            out[m * n : (m + 1) * n, :] = v[...]
        out[len(parts) * n :, :half] = left[...]
        out[len(parts) * n :, half:] = right[...]

    def join_pieces(parts, out):
        for m, v in enumerate(parts):
            n = v.shape[1]
            out[:, m * n : (m + 1) * n] = v[...]

    def body(
        nodes, edges, send_rows, neighbor_slots, neighbor_counts, mf, mfb, ms, msb, mt, mtb, mg, msh,
        expand_weight, expand_bias, reduce_weight, rb, fg, fsh, ef, efb, es, esb, et, etb, eg, esh,
        node_up, edge_up,
    ):
        rows, fanout, edge_width = edges.shape
        width, hidden = nodes.shape[1], ms.shape[0]
        share = expand_weight.shape[1]
        n_edges = rows * fanout
        step = fanout
        slots_each = send_rows.shape[2]
        buffer = n_res * slots_each
        row = lambda v: v.reshape(1, -1)
        if tuned:
            res, hid = lax.axis_index("res"), lax.axis_index("hid")
            spot = jnp.stack([res % 2, res // 2, hid, res]).astype(jnp.int32)
        else:
            spot = jnp.stack([0, 0, lax.axis_index("hid"), 0]).astype(jnp.int32)
        edges = edges.transpose(1, 0, 2).reshape(n_edges, edge_width)
        edge_up = edge_up.transpose(1, 0, 2).reshape(n_edges, edge_width)
        ef = ef.T
        bias = row(expand_bias)
        own = (expand_weight, bias, reduce_weight)
        one = struct((rows, width), BF)
        deal = [one] * 4 if tuned else [struct((buffer, width), BF)]
        n_piece = width // 8 * 9 // 4
        away, send, piece = call(
            prepare_send,
            [deal, struct((buffer, rows), BF), [struct((n_piece, width), BF)] if tuned else []],
            (send_rows[0], nodes, (expand_weight, reduce_weight, bias) if tuned else ()),
            "prepare_send",
            spot=spot,
            far=True,
        )
        pick, counts, vecs, edge_vecs, edges = call(
            prepare_rest,
            [
                struct((n_edges, buffer), BF),
                struct((rows, 1), F32),
                struct((8, width), F32),
                struct((8, edge_width), F32),
                struct((n_edges, edge_width), BF),
            ],
            (
                neighbor_slots,
                row(neighbor_counts),
                [row(v) for v in (mfb, msb, mtb, mg, msh, rb, fg, fsh)],
                [row(v) for v in (efb, esb, etb, eg, esh)],
                edges,
            ),
            "prepare_rest",
            spot=spot,
            after=away[:1],
            far=True,
        )
        if tuned:
            half = struct((rows * 2, width), BF)
            mine, twin = call(sort_cores, [half, half], (to_chips(away),), "first_sort", after=[counts])
            arrived = [mine, to_core(twin)]
        else:
            arrived = exchange(away)
        edge_args = (ef, es, et, edge_vecs)
        if tuned:
            pieces = [to_hid(piece[0], m) for m in (1, 2, 3)]
            (piece,) = call(
                join_pieces, [struct((n_piece, 3 * width), BF)], (pieces,), "join_pieces", after=[counts] + arrived
            )
            packed, first = [piece] + [to_chip(piece, m) for m in (1, 2)], [piece]
        else:
            packed, first = [
                lax.all_gather(expand_weight, "hid"),
                lax.all_gather(expand_bias, "hid"),
                lax.all_gather(reduce_weight, "hid"),
            ], []
        mid, mid_low = call(
            pass_one(rows, fanout, step),
            [struct((rows, width), F32), one],
            (arrived, nodes, edges, pick, counts, mf, ms, mt, vecs),
            "message_one",
            [pltpu.VMEM((rows, hidden), F32)],
            after=first,
        )
        if tuned:
            mids = [mid_low] + [to_hid(mid_low, m) for m in (1, 2, 3)]
            (parts,) = call(
                feed_shard, [[one] * 4], (mids, expand_weight, bias, reduce_weight), "feed_shard"
            )
            relay = struct((n_piece, 3 * width // 2), BF)
            left, right = call(
                split_relay, [relay, relay], tuple(packed[1:]), "split_weights", after=parts[:1]
            )
            parts = [parts[0]] + [to_hid(parts[m], m) for m in (1, 2, 3)]
        else:
            mids = [lax.all_gather(mid_low, "hid", axis=0, tiled=True)]
            (part,) = call(
                feed_shard,
                [[struct((n_hid * rows, width), BF)]],
                (mids, expand_weight, bias, reduce_weight),
                "feed_shard",
            )
            parts = [lax.psum_scatter(part[0], "hid", scatter_dimension=0, tiled=True)]
        state, low, away = call(
            feed_end, [struct((rows, width), F32), one, deal], (mid, parts, vecs, send), "feed_one"
        )
        if tuned:
            (packed,) = call(
                stack_relay,
                [struct((4 * n_piece, 3 * width), BF)],
                (packed, to_chip(left, 2), to_chip(right, 1)),
                "stack_weights",
                after=[low],
            )
            packed = [packed, to_core(packed)]
        arrived2, low2 = exchange(away), low
        first = []
        if tuned:
            (packed,) = call(
                lay_pair, [struct((8 * n_piece, 3 * width), BF)], (packed,), "lay_weights", spot=spot
            )
            first = packed = [packed]
        edge_state, act, slope1, slope2, first, summed, mid, mid_low = call(
            pass_two(rows, fanout, step),
            [
                struct((n_edges, edge_width), F32),
                struct((n_edges, hidden), BF),
                struct((n_edges, hidden), BF),
                struct((n_edges, hidden), BF),
                struct((rows, width), F32),
                struct((rows, hidden), BF),
                struct((rows, width), F32),
                one,
            ],
            (arrived2, state, low2, edges, pick, counts, mf, ms, mt, vecs, *edge_args),
            "layer_two",
            [pltpu.VMEM((rows, hidden), F32)],
            after=first,
        )
        feed_outs = [
            struct((n_hid, rows, share), BF),
            struct((rows, width), F32),
            jax.ShapeDtypeStruct((rows, width), F32),
            one,
            deal,
        ]
        slopes, second, node_result, low3, away = call(
            feed_pass, feed_outs, (mid, own, packed, vecs, send), "feed_two"
        )
        arrived3 = exchange(away)
        wide = lambda dtype: struct((n_edges, edge_width), dtype)
        edge_result, edge_grad, act1, act2, top, mid, bottom, slot, node, edge_vec = call(
            edge_turn(rows, fanout, step),
            [
                jax.ShapeDtypeStruct((n_edges, edge_width), F32),
                wide(F32), wide(BF), wide(BF), wide(BF), wide(BF), wide(BF),
                [struct((buffer // len(deal), edge_width), BF)] * len(deal),
                struct((rows, edge_width), BF),
                struct((8, edge_width), F32),
            ],
            (arrived3, low3, edge_state, edge_up, pick, *edge_args),
            "edge_turn",
            [
                pltpu.VMEM((buffer, edge_width), F32),
                pltpu.VMEM((rows, edge_width), F32),
                pltpu.VMEM((4, 8, edge_width), F32),
            ],
        )
        head = 3 * edge_width + edge_width // 2
        (pack,) = call(
            edge_weights,
            [struct((head, width), BF)],
            (arrived3, low3, edge_state, act1, act2, top, mid, bottom, slot, node),
            "edge_weights",
        )
        if tuned:
            half = struct((rows * 2, edge_width), BF)
            mine, twin = call(sort_cores, [half, half], (to_chips(slot),), "edge_sort", after=[pack])
            returned = [mine, to_core(twin)]
        else:
            returned = exchange(slot)
        sized = lambda n: -(-n // 128) * 128
        n_early, n_late = sized(head + hidden + 32), sized(mf.shape[0] + hidden + 16)
        cut = lambda n: [struct((n // 2, width), BF)] * 2 if tuned else [struct((n, width), BF)]
        pair, first_grad, pull, early = call(
            node_turn,
            [struct((rows, 2 * width), BF), struct((rows, width), F32), struct((rows, hidden), F32), cut(n_early)],
            (
                returned, node_up, node, send, second, slopes, first, counts, summed, ef, mt, vecs,
                own, packed, pack, edge_vec, mid_low,
            ),
            "node_turn",
            [pltpu.VMEM((n_early, width), BF)],
            spot=spot,
        )
        eighth = lambda n: struct((n // 8, width), BF)
        second_low, second_weight, message_vec = call(
            message_second(rows, fanout, step),
            [struct((n_edges, hidden), BF), struct((hidden, hidden), BF), struct((8, hidden), F32)],
            (pull, act, slope2),
            "message_second",
            [pltpu.VMEM((rows, hidden), F32)],
        )
        feed_own = (expand_weight, bias, reduce_weight)

        first = []
        if tuned:
            (early,) = call(
                split_chips, [[eighth(n_early)] * 4], (early[0], to_core(early[1])), "early_chips",
                after=[second_weight],
            )
            first = early[:1]
            early = to_chips(early)
        else:
            early = lax.psum(early[0].astype(F32), ("res", "hid"))
        first_low, slot, node, late = call(
            message_first(rows, fanout, step),
            [
                struct((n_edges, hidden), BF),
                [struct((buffer // len(deal), hidden), BF)] * len(deal),
                struct((rows, hidden), BF),
                struct((n_late, hidden), BF),
            ],
            (arrived2, low2, edge_state, pick, second_low, slope1, ms, second_weight, message_vec),
            "message_first",
            [
                pltpu.VMEM((buffer, hidden), F32),
                pltpu.VMEM((rows, hidden), F32),
            ],
            after=first,
        )
        final = Final
        if tuned:
            (pair,) = call(
                stack_up, [struct((2 * rows, 2 * width), BF)], ([pair, to_hid(pair, 2)],), "pair_stack",
                after=[node],
            )
            side = struct((n_early // 8, width // 2), BF)
            early, other, keep, send_late = call(
                add_up_sides, [side, side] + cut(n_late), (early, late), "early_plane",
                [pltpu.VMEM((n_early // 8, width), BF)], spot=spot, after=[pair],
            )
            (late,) = call(
                split_chips_more,
                [[struct((n_late // 8 + rows, width), BF)] * 4],
                (keep, to_core(send_late), slot),
                "late_chips",
            )
            last = late[0]
            late = to_chips(late)
            (early,) = call(add_two, [side], (early, to_hid(other, 2), []), "early_line", after=[last])
            (early,) = call(add_two, [side], (early, to_hid(early, 1), []), "early_line")
            (pair,) = call(
                stack_up, [struct((4 * rows, 2 * width), BF)], ([pair, to_hid(pair, 1)],), "pair_stack",
                after=[early],
            )
            half = struct((rows * 2, width), BF)
            late_side = struct((n_late // 8, width // 2), BF)
            late, other, mine, twin = call(
                add_up_more, [late_side, late_side, half, half], (late,), "late_plane",
                [pltpu.VMEM((n_late // 8, width), BF)], spot=spot, after=[pair],
            )
            pairs = [pair] + [to_chip(pair, m) for m in (1, 2, 3)]
            (late,) = call(add_two, [late_side], (late, to_hid(other, 1), []), "late_line")
            (early,) = call(
                join_far, [eighth(n_early)], (early, to_hid(early, 2)), "early_line", spot=spot, after=[late]
            )
            (pair,) = call(
                stack_up, [struct((16 * rows, 2 * width), BF)], (pairs,), "pair_stack", after=[early]
            )
            last = pair
            early = [early] + [to_chip(early, m) for m in (1, 2)]
            returned = [mine, to_core(twin)]
            node_gradient, last = call(
                node_end,
                [final(rows, width)],
                (returned, send, first_grad, node, mf),
                "node_end",
                after=[last],
                token=True,
            )
            (late,) = call(
                add_two, [late_side], (late, to_hid(late, 2), []), "late_line", after=[last]
            )
            left, right = call(split_relay, [side, side], tuple(early[1:]), "early_split", after=[late])
            edge_gradient, last = call(
                edge_end(rows, fanout, step),
                [final(n_edges, edge_width)],
                (edge_grad, first_low, mf),
                "edge_end",
                after=[left],
                token=True,
            )
            (late,) = call(
                join_near, [eighth(n_late)], (late, to_hid(late, 1)), "late_join", spot=spot, after=[last]
            )
            (early,) = call(
                stack_relay,
                [struct((n_early // 2, width), BF)],
                (early, to_chip(left, 2), to_chip(right, 1)),
                "early_stack",
                after=[late],
            )
            early = [early, to_core(early)]
            late = [late] + [to_chip(late, m) for m in (1, 2, 3)]
            pairs = [pair, to_core(pair)]
        else:
            late = [lax.psum(late.astype(F32), ("res", "hid"))]
            early = [early]
            pairs = [lax.all_gather(pair, "hid", axis=0, tiled=True)]
            expand_grad, reduce_grad = call(
                feed_weights,
                [struct((width, share), F32), struct((share, width), F32)],
                (pairs, *feed_own),
                "feed_weights",
                after=[node],
            )
            returned = exchange(slot)
            (edge_gradient,) = call(
                edge_end(rows, fanout, step), [final(n_edges, edge_width)], (edge_grad, first_low, mf), "edge_end"
            )
            (node_gradient,) = call(
                node_end, [final(rows, width)], (returned, send, first_grad, node, mf), "node_end"
            )
        (
            edge_first_grad, edge_second_grad, edge_third_grad, third_grad, vec, edge_vecs, expand_bias_grad,
            last,
        ) = call(
            unpack_early,
            [
                final(edge_width, ef.shape[1]), final(edge_width, edge_width), final(edge_width, edge_width),
                final(hidden, width), [final(1, width)] * 6, [final(1, edge_width)] * 5, final(1, share),
            ],
            (early,),
            "unpack_early",
            [pltpu.VMEM((n_early, width), F32)],
            limit=16,
            spot=spot,
            token=True,
        )
        if tuned:
            expand_grad, reduce_grad = call(
                feed_weights,
                [struct((width, share), F32), struct((share, width), F32)],
                (pairs[:1], *feed_own),
                "feed_weights",
                after=[last],
            )
            (late,) = call(
                stack_up, [struct((n_late // 2, width), BF)], (late,), "late_stack", after=[expand_grad]
            )
            last = late
            late = [late, to_core(late)]
            expand_grad, reduce_grad, last = call(
                feed_weights_more,
                [Final(width, share), Final(share, width)],
                (pairs[1:], *feed_own, expand_grad, reduce_grad),
                "feed_weights_more",
                after=[last],
                token=True,
            )
            last = [last]
        else:
            last = []
        c = mf.shape[0]
        first_weight_grad, second_weight_grad, message_vec = call(
            unpack_late,
            [
                Cut(n_late, width, c),
                Cut(n_late, width, c + hidden, c),
                [Cut(n_late, width, c + hidden + k + 1, c + hidden + k) for k in range(2)],
            ],
            (late,),
            "unpack_late",
            spot=spot,
            after=last,
        )
        if not tuned:
            expand_grad, reduce_grad = [lax.psum(v, "res") for v in (expand_grad, reduce_grad)]
        vec, edge_vecs, message_vec = [[v[0] for v in group] for group in (vec, edge_vecs, message_vec)]

        back = lambda v: v.reshape(fanout, rows, edge_width).transpose(1, 0, 2)
        return (
            node_result,
            back(edge_result),
            node_gradient,
            back(edge_gradient),
            first_weight_grad,
            message_vec[0],
            second_weight_grad,
            message_vec[1],
            third_grad,
            vec[5],
            vec[3],
            vec[4],
            expand_grad,
            expand_bias_grad[0],
            reduce_grad,
            vec[0],
            vec[1],
            vec[2],
            edge_first_grad.T,
            edge_vecs[4],
            edge_second_grad,
            edge_vecs[3],
            edge_third_grad,
            edge_vecs[2],
            edge_vecs[0],
            edge_vecs[1],
        )

    both = ("res", "hid")
    rows2, rows3 = P(both, None), P(both, None, None)
    placed = (
        rows2, rows3, rows3, rows2, P(both),
        P(), P(), P(), P(), P(), P(), P(), P(),
        P(None, "hid"), P("hid"), P("hid", None),
        P(), P(), P(), P(), P(), P(), P(), P(), P(), P(), P(),
        rows2, rows3,
    )
    given = (
        rows2, rows3, rows2, rows3,
        P(), P(), P(), P(), P(), P(), P(), P(),
        P(None, "hid"), P("hid"), P("hid", None),
        P(), P(), P(), P(), P(), P(), P(), P(), P(), P(), P(),
    )
    return jax.shard_map(body, mesh=mesh, in_specs=placed, out_specs=given, check_vma=False)
```

```python
import jax
import jax.numpy as jnp
from jax import lax
from jax.experimental import pallas as pl
from jax.experimental.pallas import tpu as pltpu
from jax.sharding import PartitionSpec as P

BF = jnp.bfloat16
F32 = jnp.float32
LEAN = 0.7978845608028654
CUBE = LEAN * 0.044715
MIB = 1 << 20
KEEP = pl.BlockSpec(memory_space=pltpu.VMEM)


def dot(left, right):
    return jnp.dot(left, right, preferred_element_type=F32)


def dot_nt(left, right):
    return lax.dot_general(left, right, (((1,), (1,)), ((), ())), preferred_element_type=F32)


def dot_tn(left, right):
    return lax.dot_general(left, right, (((0,), (0,)), ((), ())), preferred_element_type=F32)


def smooth(v):
    t = jnp.tanh(v * (LEAN + CUBE * (v * v)))
    half = 0.5 * v
    return half + half * t


def smooth_slope(v):
    v2 = v * v
    t = jnp.tanh(v * (LEAN + CUBE * v2))
    half = 0.5 * v
    slope = (0.5 + 0.5 * t) + (half - half * (t * t)) * (LEAN + (3.0 * CUBE) * v2)
    return half + half * t, slope


def smooth_low(v):
    v = v.astype(BF)
    t = jnp.tanh(v * (BF(LEAN) + BF(CUBE) * (v * v)))
    return v * (BF(0.5) + BF(0.5) * t)


def smooth_slope_low(v):
    v = v.astype(BF)
    v2 = v * v
    t = jnp.tanh(v * (BF(LEAN) + BF(CUBE) * v2))
    s = BF(0.5) + BF(0.5) * t
    act = v * s
    return act, s + (act * (BF(1.0) - s)) * (BF(2.0 * LEAN) + BF(6.0 * CUBE) * v2)


def centred(x):
    center = x - jnp.mean(x, axis=-1, keepdims=True)
    rate = lax.rsqrt(jnp.mean(center * center, axis=-1, keepdims=True) + 1e-05)
    return center * rate, rate


def norm_pull(hat, rate, gain, up):
    g = up * gain
    return rate * (
        g - jnp.mean(g, axis=-1, keepdims=True) - hat * jnp.mean(g * hat, axis=-1, keepdims=True)
    )


def tiled_add(rows, part):
    n, width = part.shape
    return (rows.reshape(-1, n, width) + part[None]).reshape(rows.shape)


def over(count, chunk):
    if count == 1:
        chunk(0, 0)
    else:
        lax.fori_loop(0, count, chunk, 0)


def aligned(index, size):
    return index if isinstance(index, int) else pl.multiple_of(index, size)


def fold(rows, n):
    return jnp.sum(rows.reshape(-1, n, rows.shape[-1]), axis=0)


class Final:
    def __init__(self, *shape):
        self.shape, self.dtype = shape, F32


class Cut(Final):
    def __init__(self, n, width, stop, start=0):
        super().__init__(stop - start, width)
        self.whole, self.start = (n, width), start


def call(body, outs, args, name, scratch=(), limit=28, spot=None, after=(), far=False, token=False):
    if token:
        outs = list(outs) + [pltpu.VMEM((8, 128), F32)]
    flat_outs, out_tree = jax.tree.flatten(list(outs), is_leaf=lambda v: hasattr(v, "dtype"))
    ends = [k for k, v in enumerate(flat_outs) if isinstance(v, Final)]
    cuts = [v for v in flat_outs if isinstance(v, Cut)]
    held_outs = [pltpu.VMEM(flat_outs[k].shape, flat_outs[k].dtype) for k in ends if not cuts]
    if cuts:
        held_outs = [pltpu.VMEM(cuts[0].whole, F32)]
    if ends:
        held_outs.append(pltpu.SemaphoreType.DMA((len(ends),)))
    shapes = [pltpu.HBM(v.shape, v.dtype) if isinstance(v, Final) else v for v in flat_outs]
    out_specs = [pl.BlockSpec(memory_space=pltpu.HBM) if isinstance(v, Final) else KEEP for v in flat_outs]
    space = pltpu.HBM if far else pltpu.VMEM
    args = jax.tree.map(lambda v: pltpu.with_memory_space_constraint(v, space), list(args))
    specs = jax.tree.map(lambda v: pl.BlockSpec(memory_space=space), args)
    lead = 0
    if spot is not None:
        args, specs, lead = [spot] + args, [pl.BlockSpec(memory_space=pltpu.SMEM)] + specs, 1
    n, more = len(args), len(after)
    scratch = list(scratch)
    if far:
        flat, tree = jax.tree.flatten(args[lead:])
        scratch += [pltpu.VMEM(v.shape, v.dtype) for v in flat] + [pltpu.SemaphoreType.DMA((len(flat),))]

    def run(*refs):
        given, rest = refs[:n], refs[n + more :]
        results, rest = list(jax.tree.leaves(list(rest[: len(outs)]))), rest[len(outs) :]
        targets = [results[k] for k in ends]
        if ends:
            count = len(held_outs)
            rest, kept, out_sems = rest[:-count], rest[-count:-1], rest[-1]
            for k, v in zip(ends, kept):
                results[k] = v
        if far:
            count = len(flat)
            rest, held, sems = rest[: -count - 1], rest[-count - 1 : -1], rest[-1]
            copies = [
                pltpu.make_async_copy(src, dst, sems.at[k])
                for k, (src, dst) in enumerate(zip(jax.tree.leaves(list(given[lead:])), held))
            ]
            for copy in copies:
                copy.start()
            for copy in copies:
                copy.wait()
            given = list(given[:lead]) + jax.tree.unflatten(tree, held)
        produced = list(jax.tree.unflatten(out_tree, results))
        if token:
            produced.pop()[...] = jnp.zeros((8, 128), F32)
        if cuts:
            produced = [kept[0]]
        body(*given, *produced, *rest)
        if cuts:
            kept = [kept[0].at[v.start : v.start + v.shape[0], :] for v in cuts]
        if ends:
            copies = [
                pltpu.make_async_copy(src, dst, out_sems.at[k])
                for k, (src, dst) in enumerate(zip(kept, targets))
            ]
            for copy in copies:
                copy.start()
            for copy in copies:
                copy.wait()

    return pl.pallas_call(
        run,
        out_shape=jax.tree.unflatten(out_tree, shapes),
        in_specs=specs + [pl.BlockSpec(memory_space=pl.ANY)] * more,
        out_specs=jax.tree.unflatten(out_tree, out_specs),
        scratch_shapes=scratch + held_outs,
        compiler_params=pltpu.CompilerParams(vmem_limit_bytes=limit * MIB),
        name=name,
    )(*args, *after)


def struct(shape, dtype):
    return pltpu.VMEM(shape, dtype)


def shards(own, packed):
    if len(packed) == 3:
        we, web, wr = packed
        for h in range(we.shape[0]):
            yield we[h], web[h : h + 1, :], wr[h]
        return
    yield own[0][...], own[1][...], own[2][...]
    (ref,) = packed
    n, width = ref.shape[0] // 8, ref.shape[1] // 3
    part = n // 9 * 4
    for h in range(3):
        at = slice(h * width, (h + 1) * width)
        we = jnp.concatenate([ref[r * n : r * n + part, at] for r in range(8)], axis=0)
        wr = jnp.concatenate([ref[r * n + part : r * n + 2 * part, at] for r in range(8)], axis=0)
        bias = ref[2 * part : n, at].astype(F32)
        yield we, bias[0:1] + bias[1:2], wr


def feed(mid, own, packed, rb, slopes):
    mid_low = mid.astype(BF)
    total = mid + rb
    for h, (we, web, wr) in enumerate(shards(own, packed)):
        act, slope = smooth_slope(dot(mid_low, we) + web)
        slopes[h] = slope.astype(BF)
        total = total + dot(act.astype(BF), wr)
    return mid_low, total


def joined(parts):
    if len(parts) == 1:
        return parts[0][...]
    if len(parts) == 2:
        n = parts[0].shape[0] // 4
        return jnp.concatenate([v[m * n : (m + 1) * n] for m in range(4) for v in parts], axis=0)
    near, far = parts[: len(parts) // 2], parts[len(parts) // 2 :]
    rows = []
    for mine, other in zip(near, far):
        half = mine.shape[0] // 2
        rows += [mine[:half], other[half:]]
    return jnp.concatenate(rows, axis=0)


def dealt(outs, value):
    n = value.shape[0] // len(outs)
    for m, out in enumerate(outs):
        out[...] = value[m * n : (m + 1) * n].astype(out.dtype)


def halved(spot, pay, keep, send):
    n = keep.shape[0] // 4
    for m in range(4):
        chip = (spot[1] ^ m) * 2
        keep[m * n : (m + 1) * n, :] = pay[pl.ds(pl.multiple_of((chip + spot[0]) * n, n), n), :]
        send[m * n : (m + 1) * n, :] = pay[pl.ds(pl.multiple_of((chip + 1 - spot[0]) * n, n), n), :]


def message_mean(summed, counts, mt, mtb):
    mean = summed / counts
    high = mean.astype(BF)
    rest = (mean - high.astype(F32)).astype(BF)
    return dot(high, mt) + dot(rest, mt) + mtb


def solution(mesh):
    n_res, n_hid = mesh.shape["res"], mesh.shape["hid"]
    tuned = (n_res, n_hid) == (8, 4)
    pair = [(i, i ^ 1) for i in range(n_res)]

    def to_chip(v, m):
        return lax.ppermute(v, "res", [(i, i ^ (2 * m)) for i in range(n_res)])

    def to_core(v):
        return lax.ppermute(v, "res", pair)

    def to_hid(v, m):
        return lax.ppermute(v, "hid", [(i, i ^ m) for i in range(n_hid)])

    def exchange(parts):
        if not tuned:
            n, width = parts[0].shape
            blocks = parts[0].reshape(n_res, n // n_res, width)
            return [lax.all_to_all(blocks, "res", 0, 0, tiled=True).reshape(n, width)]
        near = [parts[0]] + [to_chip(parts[m], m) for m in (1, 2, 3)]
        return near + [to_core(v) for v in near]

    def prepare_send(spot, table, nodes, weights, away_out, send_out, piece_out):
        rows, width = nodes.shape
        n = table.shape[1]
        lines = lax.broadcasted_iota(jnp.int32, (rows, n), 0)
        same = lax.broadcasted_iota(jnp.int32, (rows, rows), 0) == lax.broadcasted_iota(
            jnp.int32, (rows, rows), 1
        )
        same = same.astype(F32).astype(BF)
        each = n_res // len(away_out)
        for q in range(n_res):
            line = table[pl.ds(q ^ spot[3], 1), :]
            chosen = (lines == line).astype(F32).astype(BF)
            at = slice(q % each * n, (q % each + 1) * n)
            away_out[q // each][at, :] = dot_tn(chosen, nodes[...]).astype(BF)
            send_out[q * n : (q + 1) * n, :] = dot_tn(chosen, same).astype(BF)
        if piece_out:
            (out,) = piece_out
            we, wr, bias = weights
            n = width // 8
            at = pl.ds(pl.multiple_of(spot[3] * n, n), n)
            out[:n, :] = we[at, :]
            out[n : 2 * n, :] = wr[at, :]
            high = bias[...].astype(BF).astype(F32)
            rest = jnp.concatenate([high, bias[...] - high, jnp.zeros((n // 4 - 2, width), F32)], axis=0)
            out[2 * n :, :] = rest.astype(BF)

    def prepare_rest(
        spot, slots, counts, vecs, edge_vecs, edges, pick_out, counts_out, vecs_out, edge_out, edges_out
    ):
        edges_out[...] = edges[...]
        rows, fanout = slots.shape
        lanes = lax.broadcasted_iota(jnp.int32, (rows, pick_out.shape[1]), 1)
        moved = slots[...] ^ (spot[3] * (pick_out.shape[1] // n_res))
        for k in range(fanout):
            chosen = (lanes == moved[:, k : k + 1]).astype(F32).astype(BF)
            pick_out[k * rows : (k + 1) * rows, :] = chosen
        same = lax.broadcasted_iota(jnp.int32, (rows, rows), 0) == lax.broadcasted_iota(
            jnp.int32, (rows, rows), 1
        )
        many = jnp.where(same, jnp.broadcast_to(counts[...].astype(F32), (rows, rows)), 0.0)
        counts_out[...] = jnp.sum(many, axis=1, keepdims=True)
        edge_out[...] = jnp.zeros_like(edge_out)
        for k, v in enumerate(vecs):
            vecs_out[k : k + 1, :] = v[...]
        for k, v in enumerate(edge_vecs):
            edge_out[k : k + 1, :] = v[...]

    def pass_one(rows, fanout, step):
        span = step * rows

        def kernel(
            arrived, nodes, edges, pick, counts, mf, ms, mt, vecs, mid_out, mid_low_out, sums,
        ):
            mfb, msb, mtb, mg, msh = [vecs[k : k + 1, :] for k in range(5)]
            width = nodes.shape[1]
            query = dot(joined(arrived), mf[width : 2 * width]).astype(BF)
            part = dot(nodes[...], mf[:width]) + mfb
            lower = mf[2 * width :]
            lots = jnp.broadcast_to(counts[...], (rows, ms.shape[1]))
            sums[...] = jnp.zeros_like(sums)

            def chunk(i, carry):
                at = pl.ds(aligned(i * span, span), span)
                pre = dot(pick[at, :], query) + dot(edges[at, :], lower)
                act = smooth_low(tiled_add(pre, part)).astype(BF)
                act = smooth_low(dot(act, ms[...]) + msb)
                total = sums[...]
                for j in range(step):
                    total = total + jnp.where(
                        lots > jnp.float32(i * step + j), act[j * rows : (j + 1) * rows], 0.0
                    )
                sums[...] = total
                return carry

            over(fanout // step, chunk)
            first = nodes[...].astype(F32) + message_mean(sums[...], counts[...], mt[...], mtb)
            mid = centred(first)[0] * mg + msh
            mid_out[...] = mid
            mid_low_out[...] = mid.astype(BF)

        return kernel

    def feed_shard(mids, we, web, wr, outs):
        mid = jnp.concatenate([v[...] for v in mids], axis=0)
        act = smooth(dot(mid, we[...]) + web[...]).astype(BF)
        dealt(outs, dot(act, wr[...]))

    def feed_end(mid, parts, vecs, send, new_out, low_out, away_out):
        rb, fg, fsh = [vecs[k : k + 1, :] for k in (5, 6, 7)]
        second = mid[...] + rb
        for v in parts:
            second = second + v[...].astype(F32)
        new = centred(second)[0] * fg + fsh
        new_out[...] = new
        low = new.astype(BF)
        low_out[...] = low
        dealt(away_out, dot(send[...], low))

    def feed_pass(mid, own, packed, vecs, send, slopes_out, second_out, new_out, low_out, away_out):
        rb, fg, fsh = [vecs[k : k + 1, :] for k in (5, 6, 7)]
        _, second = feed(mid[...], own, packed, rb, slopes_out)
        second_out[...] = second
        new = centred(second)[0] * fg + fsh
        new_out[...] = new
        low = new.astype(BF)
        low_out[...] = low
        dealt(away_out, dot(send[...], low))

    def pass_two(rows, fanout, step):
        span = step * rows

        def kernel(
            arrived, state, low, edges, pick, counts, mf, ms, mt, vecs, ef, es, et, edge_vecs,
            edge_out, act_out, slope1_out, slope2_out, first_out, summed_out, mid_out, mid_low_out, sums,
        ):
            mfb, msb, mtb, mg, msh = [vecs[k : k + 1, :] for k in range(5)]
            efb, esb, etb, eg, esh = [edge_vecs[k : k + 1, :] for k in range(5)]
            width = state.shape[1]
            received = joined(arrived)
            key = dot_nt(received, ef[:, width : 2 * width]).astype(BF)
            edge_part = dot_nt(low[...], ef[:, :width]) + efb
            edge_lower = ef[:, 2 * width :]
            query = dot(received, mf[width : 2 * width]).astype(BF)
            part = dot(low[...], mf[:width]) + mfb
            lower = mf[2 * width :]
            lots = jnp.broadcast_to(counts[...], (rows, ms.shape[1]))
            sums[...] = jnp.zeros_like(sums)

            def chunk(i, carry):
                at = pl.ds(aligned(i * span, span), span)
                chosen = pick[at, :]
                old = edges[at, :]
                pre = dot(chosen, key) + dot_nt(old, edge_lower)
                act = smooth_low(tiled_add(pre, edge_part)).astype(BF)
                act = smooth_low(dot(act, es[...]) + esb).astype(BF)
                total = old.astype(F32) + dot(act, et[...]) + etb
                fresh = centred(total)[0] * eg + esh
                edge_out[at, :] = fresh
                pre = dot(chosen, query) + dot(fresh.astype(BF), lower)
                act, slope = smooth_slope_low(tiled_add(pre, part))
                act = act.astype(BF)
                act_out[at, :] = act
                slope1_out[at, :] = slope.astype(BF)
                act, slope = smooth_slope_low(dot(act, ms[...]) + msb)
                total = sums[...]
                for j in range(step):
                    valid = lots > jnp.float32(i * step + j)
                    total = total + jnp.where(valid, act[j * rows : (j + 1) * rows], 0.0)
                    slope2_out[pl.ds(aligned(i * span + j * rows, rows), rows), :] = jnp.where(
                        valid, slope[j * rows : (j + 1) * rows], 0.0
                    ).astype(BF)
                sums[...] = total
                return carry

            over(fanout // step, chunk)
            summed_out[...] = sums[...].astype(BF)
            first = state[...] + message_mean(sums[...], counts[...], mt[...], mtb)
            first_out[...] = first
            mid = centred(first)[0] * mg + msh
            mid_out[...] = mid
            mid_low_out[...] = mid.astype(BF)

        return kernel

    def edge_turn(rows, fanout, step):
        span = step * rows

        def kernel(
            arrived, low, edges, up, pick, ef, es, et, edge_vecs,
            result_out, grad_out, act1_out, act2_out, top_out, mid_out, bottom_out,
            slot_out, node_out, vec_out, slots, node, marks,
        ):
            width = low.shape[1]
            efb, esb, etb, eg, esh = [edge_vecs[k : k + 1, :] for k in range(5)]
            key = dot_nt(joined(arrived), ef[:, width : 2 * width]).astype(BF)
            edge_part = dot_nt(low[...], ef[:, :width]) + efb
            edge_lower = ef[:, 2 * width :]
            slots[...] = jnp.zeros_like(slots)
            node[...] = jnp.zeros_like(node)
            marks[...] = jnp.zeros_like(marks)

            def chunk(i, carry):
                at = pl.ds(aligned(i * span, span), span)
                chosen = pick[at, :]
                old = edges[at, :]
                pre = dot(chosen, key) + dot_nt(old.astype(BF), edge_lower)
                act, slope1 = smooth_slope_low(tiled_add(pre, edge_part))
                act1 = act.astype(BF)
                act1_out[at, :] = act1
                act, slope2 = smooth_slope_low(dot(act1, es[...]) + esb)
                act2 = act.astype(BF)
                act2_out[at, :] = act2
                total = old + dot(act2, et[...]) + etb
                hat, rate = centred(total)
                result_out[at, :] = hat * eg + esh
                above = up[at, :].astype(F32)
                sum_grad = norm_pull(hat, rate, eg, above)
                top = sum_grad.astype(BF)
                top_out[at, :] = top
                mid = dot_nt(top, et[...]) * slope2
                mid_low = mid.astype(BF)
                mid_out[at, :] = mid_low
                bottom = dot_nt(mid_low, es[...]) * slope1
                bottom_low = bottom.astype(BF)
                bottom_out[at, :] = bottom_low
                grad_out[at, :] = sum_grad + dot(bottom_low, edge_lower)
                marks[0] += fold(above * hat, 8)
                marks[1] += fold(above, 8)
                marks[2] += fold(sum_grad, 8)
                marks[3] += fold(mid, 8)
                node[...] += fold(bottom, rows)
                slots[...] += dot_tn(chosen, bottom_low)
                return carry

            over(fanout // step, chunk)
            dealt(slot_out, slots[...])
            node_out[...] = node[...].astype(BF)
            vec_out[...] = jnp.zeros_like(vec_out)
            for j in range(4):
                vec_out[j : j + 1, :] = jnp.sum(marks[j], axis=0, keepdims=True)
            vec_out[4:5, :] = jnp.sum(node[...], axis=0, keepdims=True)

        return kernel

    def edge_weights(arrived, low, edges, act1, act2, top, mid, bottom, slot, node, pack_out):
        n, wide = act1.shape[1], low.shape[1]
        slot = jnp.concatenate([v[...] for v in slot], axis=0)
        pack_out[:n, :] = dot_tn(node[...], low[...]).astype(BF)
        pack_out[n : 2 * n, :] = dot_tn(slot, joined(arrived)).astype(BF)
        pack_out[2 * n :, :] = jnp.zeros((pack_out.shape[0] - 2 * n, wide), BF)
        pack_out[2 * n : 3 * n, :n] = dot_tn(act1[...], mid[...]).astype(BF)
        pack_out[2 * n : 3 * n, 256 : 256 + n] = dot_tn(act2[...], top[...]).astype(BF)
        lower = dot_tn(bottom[...], edges[...].astype(BF)).astype(BF)
        pack_out[3 * n :, :n] = lower[: n // 2]
        pack_out[3 * n :, 256 : 256 + n] = lower[n // 2 :]

    def node_turn(
        spot, returned, up, node, send, second, slopes, first, counts, summed, ef, mt, vecs,
        own, packed, pack, edge_vec, mid_low, pair_out, sum_out, pull_out, pay_out, pay,
    ):
        width = up.shape[1]
        key_low = dot_tn(send[...], joined(returned)).astype(BF)
        new_grad = (
            up[...].astype(F32) + dot(node[...], ef[:, :width]) + dot(key_low, ef[:, width : 2 * width])
        )
        hat, rate = centred(second[...])
        sum_grad = norm_pull(hat, rate, vecs[6:7, :], new_grad)
        marks = [sum_grad, new_grad * hat, new_grad]
        low = sum_grad.astype(BF)
        pair_out[:, :width] = mid_low[...]
        pair_out[:, width:] = low
        mid_grad = sum_grad
        bias = []
        for h, (we, _, wr) in enumerate(shards(own, packed)):
            expand = dot_nt(low, wr) * slopes[h].astype(F32)
            bias.append(jnp.sum(expand, axis=0, keepdims=True))
            mid_grad = mid_grad + dot_nt(expand.astype(BF), we)
        hat, rate = centred(first[...])
        first_grad = norm_pull(hat, rate, vecs[3:4, :], mid_grad)
        sum_out[...] = first_grad
        marks += [mid_grad * hat, mid_grad, first_grad]
        marks = [jnp.sum(v, axis=0, keepdims=True) for v in marks]
        rows_low = (first_grad / counts[...]).astype(BF)
        pull_out[...] = dot_nt(rows_low, mt[...])
        third = dot_tn(summed[...], rows_low).astype(BF)
        head, hidden = pack.shape[0], third.shape[0]
        pay[:head, :] = pack[...]
        pay[head : head + hidden, :] = third
        pay[head + hidden :, :] = jnp.zeros((pay.shape[0] - head - hidden, width), BF)
        rows = jnp.concatenate(marks + [jnp.zeros((10, width), F32)], axis=0)
        at = lax.broadcasted_iota(jnp.int32, rows.shape, 0)
        share = bias[0].shape[1]
        for h, v in enumerate(bias):
            line = 6 + ((spot[2] ^ h) if tuned else h)
            if share < width:
                v = jnp.concatenate([v, jnp.zeros((1, width - share), F32)], axis=1)
            rows = jnp.where(at == line, v, rows)
        pay[head + hidden : head + hidden + 16, :] = rows.astype(BF)
        pay[head + hidden + 16 : head + hidden + 32, : edge_vec.shape[1]] = jnp.concatenate(
            [edge_vec[...], jnp.zeros_like(edge_vec)], axis=0
        ).astype(BF)
        if len(pay_out) == 1:
            pay_out[0][...] = pay[...]
        else:
            halved(spot, pay, *pay_out)

    def message_second(rows, fanout, step):
        span = step * rows

        def kernel(pull, act, slope2, second_out, weight_out, vec_out, marks):
            marks[...] = jnp.zeros_like(marks)

            def chunk(i, carry):
                at = pl.ds(aligned(i * span, span), span)
                second = slope2[at, :].astype(F32).reshape(step, rows, -1) * pull[...][None]
                marks[...] += jnp.sum(second, axis=0)
                second_out[at, :] = second.reshape(span, -1).astype(BF)
                return carry

            over(fanout // step, chunk)
            weight_out[...] = dot_tn(act[...], second_out[...]).astype(BF)
            vec_out[...] = jnp.zeros_like(vec_out)
            vec_out[0:1, :] = jnp.sum(marks[...], axis=0, keepdims=True)

        return kernel

    def message_first(rows, fanout, step):
        span = step * rows

        def kernel(
            arrived, low, edges, pick, second, slope1, ms, weight, vec,
            first_low_out, slot_out, node_out, pay, slots, node,
        ):
            width = low.shape[1]
            slots[...] = jnp.zeros_like(slots)
            node[...] = jnp.zeros_like(node)

            def chunk(i, carry):
                at = pl.ds(aligned(i * span, span), span)
                first = dot_nt(second[at, :], ms[...]) * slope1[at, :].astype(F32)
                node[...] += fold(first, rows)
                first = first.astype(BF)
                first_low_out[at, :] = first
                slots[...] += dot_tn(pick[at, :], first)
                return carry

            over(fanout // step, chunk)
            slot = slots[...].astype(BF)
            dealt(slot_out, slot)
            node_low = node[...].astype(BF)
            node_out[...] = node_low
            hidden, last = ms.shape[0], 2 * width + edges.shape[1]
            pay[:width, :] = dot_tn(low[...], node_low).astype(BF)
            pay[width : 2 * width, :] = dot_tn(joined(arrived), slot).astype(BF)
            pay[2 * width : last, :] = dot_tn(edges[...].astype(BF), first_low_out[...]).astype(BF)
            pay[last : last + hidden, :] = weight[...]
            pay[last + hidden :, :] = jnp.zeros((pay.shape[0] - last - hidden, hidden), BF)
            vecs = [jnp.sum(node[...], axis=0, keepdims=True), vec[0:1, :], jnp.zeros((14, hidden), F32)]
            pay[last + hidden : last + hidden + 16, :] = jnp.concatenate(vecs, axis=0).astype(BF)

        return kernel

    def feed_products(pairs, we, web, wr):
        n = we.shape[0]
        mid = jnp.concatenate([v[:, :n] for v in pairs], axis=0)
        up = jnp.concatenate([v[:, n:] for v in pairs], axis=0)
        act, slope = smooth_slope_low(dot(mid, we[...]) + web[...])
        expand = dot_nt(up, wr[...]) * slope
        return dot_tn(mid, expand.astype(BF)), dot_tn(act, up)

    def feed_weights(pairs, we, web, wr, expand_out, reduce_out):
        expand_out[...], reduce_out[...] = feed_products(pairs, we, web, wr)

    def feed_weights_more(pairs, we, web, wr, expand, reduce, expand_out, reduce_out):
        left, right = feed_products(pairs, we, web, wr)
        expand_out[...], reduce_out[...] = expand[...] + left, reduce[...] + right

    def node_end(returned, send, first_grad, node, mf, out):
        width = out.shape[1]
        query_low = dot_tn(send[...], joined(returned)).astype(BF)
        out[...] = (
            first_grad[...] + dot_nt(node[...], mf[:width]) + dot_nt(query_low, mf[width : 2 * width])
        )

    def edge_end(rows, fanout, step):
        span = step * rows

        def kernel(grad, first_low, mf, out):
            lower = mf[mf.shape[0] - grad.shape[1] :]

            def chunk(i, carry):
                at = pl.ds(aligned(i * span, span), span)
                out[at, :] = grad[at, :] + dot_nt(first_low[at, :], lower)
                return carry

            over(fanout // step, chunk)

        return kernel

    def split_chips(keep, got, outs):
        n = keep.shape[0] // len(outs)
        for m, out in enumerate(outs):
            at = slice(m * n, (m + 1) * n)
            out[:n, :] = (keep[at, :].astype(F32) + got[at, :].astype(F32)).astype(BF)

    def split_chips_more(keep, got, more, outs):
        split_chips(keep, got, outs)
        for v, out in zip(more, outs):
            out[out.shape[0] - v.shape[0] :, :] = v[...]

    def add_up(parts, out):
        n = out.shape[0]
        total = parts[0][:n, :].astype(F32)
        for v in parts[1:]:
            total = total + v[:n, :].astype(F32)
        out[...] = total.astype(BF)

    def add_up_more(spot, parts, keep, send, mine, twin, out):
        add_up(parts, out)
        n, side = keep.shape[1], spot[2] % 2
        keep[...] = out[:, pl.ds(pl.multiple_of(side * n, n), n)]
        send[...] = out[:, pl.ds(pl.multiple_of((1 - side) * n, n), n)]
        n = mine.shape[0] // len(parts)
        for m, v in enumerate(parts):
            at, top = slice(m * n, (m + 1) * n), out.shape[0]
            mine[at, :] = v[top : top + n, :]
            twin[at, :] = v[top + n : top + 2 * n, :]

    def add_up_join(parts, more, out):
        n = more.shape[0]
        out[:n, :] = more[...]
        total = parts[0][...].astype(F32)
        for v in parts[1:]:
            total = total + v[...].astype(F32)
        out[n:, :] = total.astype(BF)

    def add_up_sides(spot, parts, pay, keep, send, pay_keep, pay_send, total):
        add_up(parts, total)
        halved(spot, pay, pay_keep, pay_send)
        n, side = keep.shape[1], spot[2] // 2
        keep[...] = total[:, pl.ds(pl.multiple_of(side * n, n), n)]
        send[...] = total[:, pl.ds(pl.multiple_of((1 - side) * n, n), n)]

    def join_near(spot, mine, other, out):
        join_sides(spot, mine, other, out, spot[2] % 2)

    def join_far(spot, mine, other, out):
        join_sides(spot, mine, other, out, spot[2] // 2)

    def join_sides(spot, mine, other, out, side):
        n = mine.shape[1]
        out[:, pl.ds(pl.multiple_of(side * n, n), n)] = mine[...]
        out[:, pl.ds(pl.multiple_of((1 - side) * n, n), n)] = other[...]

    def sort_cores(parts, mine, twin):
        n = mine.shape[0] // len(parts)
        for m, v in enumerate(parts):
            at = slice(m * n, (m + 1) * n)
            mine[at, :] = v[:n, :]
            twin[at, :] = v[n : 2 * n, :]

    def add_two(left, right, more, out):
        n = left.shape[0]
        out[:n, :] = (left[...].astype(F32) + right[...].astype(F32)).astype(BF)
        if more:
            out[n:, :] = more[0][...]

    def to_chips(parts):
        return [parts[0]] + [to_chip(parts[m], m) for m in (1, 2, 3)]

    def spread(own):
        parts = [own] + [to_chip(own, m) for m in (1, 2, 3)]
        return parts + [to_core(v) for v in parts]

    def laid_out(spot, parts, total):
        n = parts[0].shape[0]
        for k, v in enumerate(parts):
            at = (2 * (spot[1] ^ (k % 4)) + (spot[0] ^ (k // 4))) * n
            total[pl.ds(pl.multiple_of(at, n), n), :] = v[...].astype(total.dtype)

    def lay_pair(spot, stacks, total):
        n = total.shape[0] // 8
        for k in range(8):
            at = (2 * (spot[1] ^ (k % 4)) + (spot[0] ^ (k // 4))) * n
            top = k % 4 * n
            total[pl.ds(pl.multiple_of(at, n), n), :] = stacks[k // 4][top : top + n, :].astype(total.dtype)

    def stack_up(parts, out):
        n = parts[0].shape[0]
        for m, v in enumerate(parts):
            out[m * n : (m + 1) * n, :] = v[...]

    def unpack_early(
        spot, parts, first_out, second_out, third_out, message_out, vec_out, edge_vec_out, bias_out, total,
    ):
        if len(parts) == 1:
            total[...] = parts[0][...]
        else:
            lay_pair(spot, parts, total)
        n, wide = second_out.shape[0], message_out.shape[1]
        first_out[:, :wide] = total[:n, :]
        first_out[:, wide : 2 * wide] = total[n : 2 * n, :]
        second_out[...] = total[2 * n : 3 * n, :n]
        third_out[...] = total[2 * n : 3 * n, 256 : 256 + n]
        at = 3 * n + n // 2
        first_out[: n // 2, 2 * wide :] = total[3 * n : at, :n]
        first_out[n // 2 :, 2 * wide :] = total[3 * n : at, 256 : 256 + n]
        hidden = message_out.shape[0]
        message_out[...] = total[at : at + hidden, :]
        for k, out in enumerate(vec_out):
            out[...] = total[at + hidden + k : at + hidden + k + 1, :]
        for k, out in enumerate(edge_vec_out):
            out[...] = total[at + hidden + 16 + k : at + hidden + 17 + k, :n]
        vecs = total[at + hidden : at + hidden + 16, :]
        line = lax.broadcasted_iota(jnp.int32, vecs.shape, 0) == 6 + spot[2]
        bias = jnp.sum(jnp.where(line, vecs, 0.0), axis=0, keepdims=True)
        bias_out[...] = bias[:, : bias_out.shape[1]]

    def unpack_late(spot, parts, total):
        if len(parts) == 1:
            total[...] = parts[0][...]
        else:
            lay_pair(spot, parts, total)

    def split_relay(left, right, left_out, right_out):
        n = left_out.shape[1]
        left_out[...] = left[:, :n]
        right_out[...] = right[:, n:]

    def stack_relay(parts, left, right, out):
        n, half = left.shape
        for m, v in enumerate(parts):
            out[m * n : (m + 1) * n, :] = v[...]
        out[len(parts) * n :, :half] = left[...]
        out[len(parts) * n :, half:] = right[...]

    def join_pieces(parts, out):
        for m, v in enumerate(parts):
            n = v.shape[1]
            out[:, m * n : (m + 1) * n] = v[...]

    def body(
        nodes, edges, send_rows, neighbor_slots, neighbor_counts, mf, mfb, ms, msb, mt, mtb, mg, msh,
        expand_weight, expand_bias, reduce_weight, rb, fg, fsh, ef, efb, es, esb, et, etb, eg, esh,
        node_up, edge_up,
    ):
        rows, fanout, edge_width = edges.shape
        width, hidden = nodes.shape[1], ms.shape[0]
        share = expand_weight.shape[1]
        n_edges = rows * fanout
        step = fanout
        slots_each = send_rows.shape[2]
        buffer = n_res * slots_each
        row = lambda v: v.reshape(1, -1)
        if tuned:
            res, hid = lax.axis_index("res"), lax.axis_index("hid")
            spot = jnp.stack([res % 2, res // 2, hid, res]).astype(jnp.int32)
        else:
            spot = jnp.stack([0, 0, lax.axis_index("hid"), 0]).astype(jnp.int32)
        edges = edges.transpose(1, 0, 2).reshape(n_edges, edge_width)
        edge_up = edge_up.transpose(1, 0, 2).reshape(n_edges, edge_width)
        ef = ef.T
        bias = row(expand_bias)
        own = (expand_weight, bias, reduce_weight)
        one = struct((rows, width), BF)
        deal = [one] * 4 if tuned else [struct((buffer, width), BF)]
        n_piece = width // 8 * 9 // 4
        away, send, piece = call(
            prepare_send,
            [deal, struct((buffer, rows), BF), [struct((n_piece, width), BF)] if tuned else []],
            (send_rows[0], nodes, (expand_weight, reduce_weight, bias) if tuned else ()),
            "prepare_send",
            spot=spot,
            far=True,
        )
        pick, counts, vecs, edge_vecs, edges = call(
            prepare_rest,
            [
                struct((n_edges, buffer), BF),
                struct((rows, 1), F32),
                struct((8, width), F32),
                struct((8, edge_width), F32),
                struct((n_edges, edge_width), BF),
            ],
            (
                neighbor_slots,
                row(neighbor_counts),
                [row(v) for v in (mfb, msb, mtb, mg, msh, rb, fg, fsh)],
                [row(v) for v in (efb, esb, etb, eg, esh)],
                edges,
            ),
            "prepare_rest",
            spot=spot,
            after=away[:1],
            far=True,
        )
        if tuned:
            half = struct((rows * 2, width), BF)
            mine, twin = call(sort_cores, [half, half], (to_chips(away),), "first_sort", after=[counts])
            arrived = [mine, to_core(twin)]
        else:
            arrived = exchange(away)
        edge_args = (ef, es, et, edge_vecs)
        if tuned:
            pieces = [to_hid(piece[0], m) for m in (1, 2, 3)]
            (piece,) = call(
                join_pieces, [struct((n_piece, 3 * width), BF)], (pieces,), "join_pieces", after=[counts] + arrived
            )
            packed, first = [piece] + [to_chip(piece, m) for m in (1, 2)], [piece]
        else:
            packed, first = [
                lax.all_gather(expand_weight, "hid"),
                lax.all_gather(expand_bias, "hid"),
                lax.all_gather(reduce_weight, "hid"),
            ], []
        mid, mid_low = call(
            pass_one(rows, fanout, step),
            [struct((rows, width), F32), one],
            (arrived, nodes, edges, pick, counts, mf, ms, mt, vecs),
            "message_one",
            [pltpu.VMEM((rows, hidden), F32)],
            after=first,
        )
        if tuned:
            mids = [mid_low] + [to_hid(mid_low, m) for m in (1, 2, 3)]
            (parts,) = call(
                feed_shard, [[one] * 4], (mids, expand_weight, bias, reduce_weight), "feed_shard"
            )
            relay = struct((n_piece, 3 * width // 2), BF)
            left, right = call(
                split_relay, [relay, relay], tuple(packed[1:]), "split_weights", after=parts[:1]
            )
            parts = [parts[0]] + [to_hid(parts[m], m) for m in (1, 2, 3)]
        else:
            mids = [lax.all_gather(mid_low, "hid", axis=0, tiled=True)]
            (part,) = call(
                feed_shard,
                [[struct((n_hid * rows, width), BF)]],
                (mids, expand_weight, bias, reduce_weight),
                "feed_shard",
            )
            parts = [lax.psum_scatter(part[0], "hid", scatter_dimension=0, tiled=True)]
        state, low, away = call(
            feed_end, [struct((rows, width), F32), one, deal], (mid, parts, vecs, send), "feed_one"
        )
        if tuned:
            (packed,) = call(
                stack_relay,
                [struct((4 * n_piece, 3 * width), BF)],
                (packed, to_chip(left, 2), to_chip(right, 1)),
                "stack_weights",
                after=[low],
            )
            packed = [packed, to_core(packed)]
        arrived2, low2 = exchange(away), low
        first = []
        if tuned:
            (packed,) = call(
                lay_pair, [struct((8 * n_piece, 3 * width), BF)], (packed,), "lay_weights", spot=spot
            )
            first = packed = [packed]
        edge_state, act, slope1, slope2, first, summed, mid, mid_low = call(
            pass_two(rows, fanout, step),
            [
                struct((n_edges, edge_width), F32),
                struct((n_edges, hidden), BF),
                struct((n_edges, hidden), BF),
                struct((n_edges, hidden), BF),
                struct((rows, width), F32),
                struct((rows, hidden), BF),
                struct((rows, width), F32),
                one,
            ],
            (arrived2, state, low2, edges, pick, counts, mf, ms, mt, vecs, *edge_args),
            "layer_two",
            [pltpu.VMEM((rows, hidden), F32)],
            after=first,
        )
        feed_outs = [
            struct((n_hid, rows, share), BF),
            struct((rows, width), F32),
            jax.ShapeDtypeStruct((rows, width), F32),
            one,
            deal,
        ]
        slopes, second, node_result, low3, away = call(
            feed_pass, feed_outs, (mid, own, packed, vecs, send), "feed_two"
        )
        arrived3 = exchange(away)
        wide = lambda dtype: struct((n_edges, edge_width), dtype)
        edge_result, edge_grad, act1, act2, top, mid, bottom, slot, node, edge_vec = call(
            edge_turn(rows, fanout, step),
            [
                jax.ShapeDtypeStruct((n_edges, edge_width), F32),
                wide(F32), wide(BF), wide(BF), wide(BF), wide(BF), wide(BF),
                [struct((buffer // len(deal), edge_width), BF)] * len(deal),
                struct((rows, edge_width), BF),
                struct((8, edge_width), F32),
            ],
            (arrived3, low3, edge_state, edge_up, pick, *edge_args),
            "edge_turn",
            [
                pltpu.VMEM((buffer, edge_width), F32),
                pltpu.VMEM((rows, edge_width), F32),
                pltpu.VMEM((4, 8, edge_width), F32),
            ],
        )
        head = 3 * edge_width + edge_width // 2
        (pack,) = call(
            edge_weights,
            [struct((head, width), BF)],
            (arrived3, low3, edge_state, act1, act2, top, mid, bottom, slot, node),
            "edge_weights",
        )
        if tuned:
            half = struct((rows * 2, edge_width), BF)
            mine, twin = call(sort_cores, [half, half], (to_chips(slot),), "edge_sort", after=[pack])
            returned = [mine, to_core(twin)]
        else:
            returned = exchange(slot)
        sized = lambda n: -(-n // 128) * 128
        n_early, n_late = sized(head + hidden + 32), sized(mf.shape[0] + hidden + 16)
        cut = lambda n: [struct((n // 2, width), BF)] * 2 if tuned else [struct((n, width), BF)]
        pair, first_grad, pull, early = call(
            node_turn,
            [struct((rows, 2 * width), BF), struct((rows, width), F32), struct((rows, hidden), F32), cut(n_early)],
            (
                returned, node_up, node, send, second, slopes, first, counts, summed, ef, mt, vecs,
                own, packed, pack, edge_vec, mid_low,
            ),
            "node_turn",
            [pltpu.VMEM((n_early, width), BF)],
            spot=spot,
        )
        eighth = lambda n: struct((n // 8, width), BF)
        second_low, second_weight, message_vec = call(
            message_second(rows, fanout, step),
            [struct((n_edges, hidden), BF), struct((hidden, hidden), BF), struct((8, hidden), F32)],
            (pull, act, slope2),
            "message_second",
            [pltpu.VMEM((rows, hidden), F32)],
        )
        feed_own = (expand_weight, bias, reduce_weight)

        first = []
        if tuned:
            (early,) = call(
                split_chips, [[eighth(n_early)] * 4], (early[0], to_core(early[1])), "early_chips",
                after=[second_weight],
            )
            first = early[:1]
            early = to_chips(early)
        else:
            early = lax.psum(early[0].astype(F32), ("res", "hid"))
        first_low, slot, node, late = call(
            message_first(rows, fanout, step),
            [
                struct((n_edges, hidden), BF),
                [struct((buffer // len(deal), hidden), BF)] * len(deal),
                struct((rows, hidden), BF),
                struct((n_late, hidden), BF),
            ],
            (arrived2, low2, edge_state, pick, second_low, slope1, ms, second_weight, message_vec),
            "message_first",
            [
                pltpu.VMEM((buffer, hidden), F32),
                pltpu.VMEM((rows, hidden), F32),
            ],
            after=first,
        )
        final = Final
        if tuned:
            (pair,) = call(
                stack_up, [struct((2 * rows, 2 * width), BF)], ([pair, to_hid(pair, 2)],), "pair_stack",
                after=[node],
            )
            side = struct((n_early // 8, width // 2), BF)
            early, other, keep, send_late = call(
                add_up_sides, [side, side] + cut(n_late), (early, late), "early_plane",
                [pltpu.VMEM((n_early // 8, width), BF)], spot=spot, after=[pair],
            )
            (late,) = call(
                split_chips_more,
                [[struct((n_late // 8 + rows, width), BF)] * 4],
                (keep, to_core(send_late), slot),
                "late_chips",
            )
            last = late[0]
            late = to_chips(late)
            (early,) = call(add_two, [side], (early, to_hid(other, 2), []), "early_line", after=[last])
            (early,) = call(add_two, [side], (early, to_hid(early, 1), []), "early_line")
            (pair,) = call(
                stack_up, [struct((4 * rows, 2 * width), BF)], ([pair, to_hid(pair, 1)],), "pair_stack",
                after=[early],
            )
            half = struct((rows * 2, width), BF)
            late_side = struct((n_late // 8, width // 2), BF)
            late, other, mine, twin = call(
                add_up_more, [late_side, late_side, half, half], (late,), "late_plane",
                [pltpu.VMEM((n_late // 8, width), BF)], spot=spot, after=[pair],
            )
            pairs = [pair] + [to_chip(pair, m) for m in (1, 2, 3)]
            (late,) = call(add_two, [late_side], (late, to_hid(other, 1), []), "late_line")
            (early,) = call(
                join_far, [eighth(n_early)], (early, to_hid(early, 2)), "early_line", spot=spot, after=[late]
            )
            (pair,) = call(
                stack_up, [struct((16 * rows, 2 * width), BF)], (pairs,), "pair_stack", after=[early]
            )
            last = pair
            early = [early] + [to_chip(early, m) for m in (1, 2)]
            returned = [mine, to_core(twin)]
            node_gradient, last = call(
                node_end,
                [final(rows, width)],
                (returned, send, first_grad, node, mf),
                "node_end",
                after=[last],
                token=True,
            )
            (late,) = call(
                add_two, [late_side], (late, to_hid(late, 2), []), "late_line", after=[last]
            )
            left, right = call(split_relay, [side, side], tuple(early[1:]), "early_split", after=[late])
            edge_gradient, last = call(
                edge_end(rows, fanout, step),
                [final(n_edges, edge_width)],
                (edge_grad, first_low, mf),
                "edge_end",
                after=[left],
                token=True,
            )
            (late,) = call(
                join_near, [eighth(n_late)], (late, to_hid(late, 1)), "late_join", spot=spot, after=[last]
            )
            (early,) = call(
                stack_relay,
                [struct((n_early // 2, width), BF)],
                (early, to_chip(left, 2), to_chip(right, 1)),
                "early_stack",
                after=[late],
            )
            early = [early, to_core(early)]
            late = [late] + [to_chip(late, m) for m in (1, 2, 3)]
            pairs = [pair, to_core(pair)]
        else:
            late = [lax.psum(late.astype(F32), ("res", "hid"))]
            early = [early]
            pairs = [lax.all_gather(pair, "hid", axis=0, tiled=True)]
            expand_grad, reduce_grad = call(
                feed_weights,
                [struct((width, share), F32), struct((share, width), F32)],
                (pairs, *feed_own),
                "feed_weights",
                after=[node],
            )
            returned = exchange(slot)
            (edge_gradient,) = call(
                edge_end(rows, fanout, step), [final(n_edges, edge_width)], (edge_grad, first_low, mf), "edge_end"
            )
            (node_gradient,) = call(
                node_end, [final(rows, width)], (returned, send, first_grad, node, mf), "node_end"
            )
        (
            edge_first_grad, edge_second_grad, edge_third_grad, third_grad, vec, edge_vecs, expand_bias_grad,
            last,
        ) = call(
            unpack_early,
            [
                final(edge_width, ef.shape[1]), final(edge_width, edge_width), final(edge_width, edge_width),
                final(hidden, width), [final(1, width)] * 6, [final(1, edge_width)] * 5, final(1, share),
            ],
            (early,),
            "unpack_early",
            [pltpu.VMEM((n_early, width), F32)],
            limit=16,
            spot=spot,
            token=True,
        )
        if tuned:
            expand_grad, reduce_grad = call(
                feed_weights,
                [struct((width, share), F32), struct((share, width), F32)],
                (pairs[:1], *feed_own),
                "feed_weights",
                after=[last],
            )
            (late,) = call(
                stack_up, [struct((n_late // 2, width), BF)], (late,), "late_stack", after=[expand_grad]
            )
            last = late
            late = [late, to_core(late)]
            expand_grad, reduce_grad, last = call(
                feed_weights_more,
                [Final(width, share), Final(share, width)],
                (pairs[1:], *feed_own, expand_grad, reduce_grad),
                "feed_weights_more",
                after=[last],
                token=True,
            )
            last = [last]
        else:
            last = []
        c = mf.shape[0]
        first_weight_grad, second_weight_grad, message_vec = call(
            unpack_late,
            [
                Cut(n_late, width, c),
                Cut(n_late, width, c + hidden, c),
                [Cut(n_late, width, c + hidden + k + 1, c + hidden + k) for k in range(2)],
            ],
            (late,),
            "unpack_late",
            spot=spot,
            after=last,
        )
        if not tuned:
            expand_grad, reduce_grad = [lax.psum(v, "res") for v in (expand_grad, reduce_grad)]
        vec, edge_vecs, message_vec = [[v[0] for v in group] for group in (vec, edge_vecs, message_vec)]

        back = lambda v: v.reshape(fanout, rows, edge_width).transpose(1, 0, 2)
        return (
            node_result,
            back(edge_result),
            node_gradient,
            back(edge_gradient),
            first_weight_grad,
            message_vec[0],
            second_weight_grad,
            message_vec[1],
            third_grad,
            vec[5],
            vec[3],
            vec[4],
            expand_grad,
            expand_bias_grad[0],
            reduce_grad,
            vec[0],
            vec[1],
            vec[2],
            edge_first_grad.T,
            edge_vecs[4],
            edge_second_grad,
            edge_vecs[3],
            edge_third_grad,
            edge_vecs[2],
            edge_vecs[0],
            edge_vecs[1],
        )

    both = ("res", "hid")
    rows2, rows3 = P(both, None), P(both, None, None)
    placed = (
        rows2, rows3, rows3, rows2, P(both),
        P(), P(), P(), P(), P(), P(), P(), P(),
        P(None, "hid"), P("hid"), P("hid", None),
        P(), P(), P(), P(), P(), P(), P(), P(), P(), P(), P(),
        rows2, rows3,
    )
    given = (
        rows2, rows3, rows2, rows3,
        P(), P(), P(), P(), P(), P(), P(), P(),
        P(None, "hid"), P("hid"), P("hid", None),
        P(), P(), P(), P(), P(), P(), P(), P(), P(), P(), P(),
    )
    return jax.shard_map(body, mesh=mesh, in_specs=placed, out_specs=given, check_vma=False)
```

```python
import jax
import jax.numpy as jnp
from jax import lax
from jax.experimental import pallas as pl
from jax.experimental.pallas import tpu as pltpu
from jax.sharding import PartitionSpec as P

BF = jnp.bfloat16
F32 = jnp.float32
LEAN = 0.7978845608028654
CUBE = LEAN * 0.044715
MIB = 1 << 20
KEEP = pl.BlockSpec(memory_space=pltpu.VMEM)


def dot(left, right):
    return jnp.dot(left, right, preferred_element_type=F32)


def dot_nt(left, right):
    return lax.dot_general(left, right, (((1,), (1,)), ((), ())), preferred_element_type=F32)


def dot_tn(left, right):
    return lax.dot_general(left, right, (((0,), (0,)), ((), ())), preferred_element_type=F32)


def smooth(v):
    t = jnp.tanh(v * (LEAN + CUBE * (v * v)))
    half = 0.5 * v
    return half + half * t


def smooth_slope(v):
    v2 = v * v
    t = jnp.tanh(v * (LEAN + CUBE * v2))
    half = 0.5 * v
    slope = (0.5 + 0.5 * t) + (half - half * (t * t)) * (LEAN + (3.0 * CUBE) * v2)
    return half + half * t, slope


def smooth_low(v):
    v = v.astype(BF)
    t = jnp.tanh(v * (BF(LEAN) + BF(CUBE) * (v * v)))
    return v * (BF(0.5) + BF(0.5) * t)


def smooth_slope_low(v):
    v = v.astype(BF)
    v2 = v * v
    t = jnp.tanh(v * (BF(LEAN) + BF(CUBE) * v2))
    s = BF(0.5) + BF(0.5) * t
    act = v * s
    return act, s + (act * (BF(1.0) - s)) * (BF(2.0 * LEAN) + BF(6.0 * CUBE) * v2)


def centred(x):
    center = x - jnp.mean(x, axis=-1, keepdims=True)
    rate = lax.rsqrt(jnp.mean(center * center, axis=-1, keepdims=True) + 1e-05)
    return center * rate, rate


def norm_pull(hat, rate, gain, up):
    g = up * gain
    return rate * (
        g - jnp.mean(g, axis=-1, keepdims=True) - hat * jnp.mean(g * hat, axis=-1, keepdims=True)
    )


def tiled_add(rows, part):
    n, width = part.shape
    return (rows.reshape(-1, n, width) + part[None]).reshape(rows.shape)


def over(count, chunk):
    if count == 1:
        chunk(0, 0)
    else:
        lax.fori_loop(0, count, chunk, 0)


def aligned(index, size):
    return index if isinstance(index, int) else pl.multiple_of(index, size)


def fold(rows, n):
    return jnp.sum(rows.reshape(-1, n, rows.shape[-1]), axis=0)


class Final:
    def __init__(self, *shape):
        self.shape, self.dtype = shape, F32


class Cut(Final):
    def __init__(self, n, width, stop, start=0):
        super().__init__(stop - start, width)
        self.whole, self.start = (n, width), start


def call(body, outs, args, name, scratch=(), limit=28, spot=None, after=(), far=False, token=False):
    if token:
        outs = list(outs) + [pltpu.VMEM((8, 128), F32)]
    flat_outs, out_tree = jax.tree.flatten(list(outs), is_leaf=lambda v: hasattr(v, "dtype"))
    ends = [k for k, v in enumerate(flat_outs) if isinstance(v, Final)]
    cuts = [v for v in flat_outs if isinstance(v, Cut)]
    held_outs = [pltpu.VMEM(flat_outs[k].shape, flat_outs[k].dtype) for k in ends if not cuts]
    if cuts:
        held_outs = [pltpu.VMEM(cuts[0].whole, F32)]
    if ends:
        held_outs.append(pltpu.SemaphoreType.DMA((len(ends),)))
    shapes = [pltpu.HBM(v.shape, v.dtype) if isinstance(v, Final) else v for v in flat_outs]
    out_specs = [pl.BlockSpec(memory_space=pltpu.HBM) if isinstance(v, Final) else KEEP for v in flat_outs]
    space = pltpu.HBM if far else pltpu.VMEM
    args = jax.tree.map(lambda v: pltpu.with_memory_space_constraint(v, space), list(args))
    specs = jax.tree.map(lambda v: pl.BlockSpec(memory_space=space), args)
    lead = 0
    if spot is not None:
        args, specs, lead = [spot] + args, [pl.BlockSpec(memory_space=pltpu.SMEM)] + specs, 1
    n, more = len(args), len(after)
    scratch = list(scratch)
    if far:
        flat, tree = jax.tree.flatten(args[lead:])
        scratch += [pltpu.VMEM(v.shape, v.dtype) for v in flat] + [pltpu.SemaphoreType.DMA((len(flat),))]

    def run(*refs):
        given, rest = refs[:n], refs[n + more :]
        results, rest = list(jax.tree.leaves(list(rest[: len(outs)]))), rest[len(outs) :]
        targets = [results[k] for k in ends]
        if ends:
            count = len(held_outs)
            rest, kept, out_sems = rest[:-count], rest[-count:-1], rest[-1]
            for k, v in zip(ends, kept):
                results[k] = v
        if far:
            count = len(flat)
            rest, held, sems = rest[: -count - 1], rest[-count - 1 : -1], rest[-1]
            copies = [
                pltpu.make_async_copy(src, dst, sems.at[k])
                for k, (src, dst) in enumerate(zip(jax.tree.leaves(list(given[lead:])), held))
            ]
            for copy in copies:
                copy.start()
            for copy in copies:
                copy.wait()
            given = list(given[:lead]) + jax.tree.unflatten(tree, held)
        produced = list(jax.tree.unflatten(out_tree, results))
        if token:
            produced.pop()[...] = jnp.zeros((8, 128), F32)
        if cuts:
            produced = [kept[0]]
        body(*given, *produced, *rest)
        if cuts:
            kept = [kept[0].at[v.start : v.start + v.shape[0], :] for v in cuts]
        if ends:
            copies = [
                pltpu.make_async_copy(src, dst, out_sems.at[k])
                for k, (src, dst) in enumerate(zip(kept, targets))
            ]
            for copy in copies:
                copy.start()
            for copy in copies:
                copy.wait()

    return pl.pallas_call(
        run,
        out_shape=jax.tree.unflatten(out_tree, shapes),
        in_specs=specs + [pl.BlockSpec(memory_space=pl.ANY)] * more,
        out_specs=jax.tree.unflatten(out_tree, out_specs),
        scratch_shapes=scratch + held_outs,
        compiler_params=pltpu.CompilerParams(vmem_limit_bytes=limit * MIB),
        name=name,
    )(*args, *after)


def struct(shape, dtype):
    return pltpu.VMEM(shape, dtype)


def shards(own, packed):
    if len(packed) == 3:
        we, web, wr = packed
        for h in range(we.shape[0]):
            yield we[h], web[h : h + 1, :], wr[h]
        return
    yield own[0][...], own[1][...], own[2][...]
    (ref,) = packed
    n, width = ref.shape[0] // 8, ref.shape[1] // 3
    part = n // 9 * 4
    for h in range(3):
        at = slice(h * width, (h + 1) * width)
        we = jnp.concatenate([ref[r * n : r * n + part, at] for r in range(8)], axis=0)
        wr = jnp.concatenate([ref[r * n + part : r * n + 2 * part, at] for r in range(8)], axis=0)
        bias = ref[2 * part : n, at].astype(F32)
        yield we, bias[0:1] + bias[1:2], wr


def feed(mid, own, packed, rb, slopes):
    mid_low = mid.astype(BF)
    total = mid + rb
    for h, (we, web, wr) in enumerate(shards(own, packed)):
        act, slope = smooth_slope(dot(mid_low, we) + web)
        slopes[h] = slope.astype(BF)
        total = total + dot(act.astype(BF), wr)
    return mid_low, total


def joined(parts):
    if len(parts) == 1:
        return parts[0][...]
    if len(parts) == 2:
        n = parts[0].shape[0] // 4
        return jnp.concatenate([v[m * n : (m + 1) * n] for m in range(4) for v in parts], axis=0)
    near, far = parts[: len(parts) // 2], parts[len(parts) // 2 :]
    rows = []
    for mine, other in zip(near, far):
        half = mine.shape[0] // 2
        rows += [mine[:half], other[half:]]
    return jnp.concatenate(rows, axis=0)


def dealt(outs, value):
    n = value.shape[0] // len(outs)
    for m, out in enumerate(outs):
        out[...] = value[m * n : (m + 1) * n].astype(out.dtype)


def halved(spot, pay, keep, send):
    n = keep.shape[0] // 4
    for m in range(4):
        chip = (spot[1] ^ m) * 2
        keep[m * n : (m + 1) * n, :] = pay[pl.ds(pl.multiple_of((chip + spot[0]) * n, n), n), :]
        send[m * n : (m + 1) * n, :] = pay[pl.ds(pl.multiple_of((chip + 1 - spot[0]) * n, n), n), :]


def message_mean(summed, counts, mt, mtb):
    mean = summed / counts
    high = mean.astype(BF)
    rest = (mean - high.astype(F32)).astype(BF)
    return dot(high, mt) + dot(rest, mt) + mtb


def solution(mesh):
    n_res, n_hid = mesh.shape["res"], mesh.shape["hid"]
    tuned = (n_res, n_hid) == (8, 4)
    pair = [(i, i ^ 1) for i in range(n_res)]

    def to_chip(v, m):
        return lax.ppermute(v, "res", [(i, i ^ (2 * m)) for i in range(n_res)])

    def to_core(v):
        return lax.ppermute(v, "res", pair)

    def to_hid(v, m):
        return lax.ppermute(v, "hid", [(i, i ^ m) for i in range(n_hid)])

    def exchange(parts):
        if not tuned:
            n, width = parts[0].shape
            blocks = parts[0].reshape(n_res, n // n_res, width)
            return [lax.all_to_all(blocks, "res", 0, 0, tiled=True).reshape(n, width)]
        far = to_chip(parts[3], 3)
        near = [parts[0], to_chip(parts[1], 1), to_chip(parts[2], 2), far]
        return near + [to_core(v) for v in near]

    def prepare_send(spot, table, nodes, weights, away_out, send_out, piece_out):
        rows, width = nodes.shape
        n = table.shape[1]
        lines = lax.broadcasted_iota(jnp.int32, (rows, n), 0)
        same = lax.broadcasted_iota(jnp.int32, (rows, rows), 0) == lax.broadcasted_iota(
            jnp.int32, (rows, rows), 1
        )
        same = same.astype(F32).astype(BF)
        each = n_res // len(away_out)
        for q in range(n_res):
            line = table[pl.ds(q ^ spot[3], 1), :]
            chosen = (lines == line).astype(F32).astype(BF)
            at = slice(q % each * n, (q % each + 1) * n)
            away_out[q // each][at, :] = dot_tn(chosen, nodes[...]).astype(BF)
            send_out[q * n : (q + 1) * n, :] = dot_tn(chosen, same).astype(BF)
        if piece_out:
            (out,) = piece_out
            we, wr, bias = weights
            n = width // 8
            at = pl.ds(pl.multiple_of(spot[3] * n, n), n)
            out[:n, :] = we[at, :]
            out[n : 2 * n, :] = wr[at, :]
            high = bias[...].astype(BF).astype(F32)
            rest = jnp.concatenate([high, bias[...] - high, jnp.zeros((n // 4 - 2, width), F32)], axis=0)
            out[2 * n :, :] = rest.astype(BF)

    def prepare_rest(
        spot, slots, counts, vecs, edge_vecs, edges, pick_out, counts_out, vecs_out, edge_out, edges_out
    ):
        edges_out[...] = edges[...]
        rows, fanout = slots.shape
        lanes = lax.broadcasted_iota(jnp.int32, (rows, pick_out.shape[1]), 1)
        moved = slots[...] ^ (spot[3] * (pick_out.shape[1] // n_res))
        for k in range(fanout):
            chosen = (lanes == moved[:, k : k + 1]).astype(F32).astype(BF)
            pick_out[k * rows : (k + 1) * rows, :] = chosen
        same = lax.broadcasted_iota(jnp.int32, (rows, rows), 0) == lax.broadcasted_iota(
            jnp.int32, (rows, rows), 1
        )
        many = jnp.where(same, jnp.broadcast_to(counts[...].astype(F32), (rows, rows)), 0.0)
        counts_out[...] = jnp.sum(many, axis=1, keepdims=True)
        edge_out[...] = jnp.zeros_like(edge_out)
        for k, v in enumerate(vecs):
            vecs_out[k : k + 1, :] = v[...]
        for k, v in enumerate(edge_vecs):
            edge_out[k : k + 1, :] = v[...]

    def pass_one(rows, fanout, step):
        span = step * rows

        def kernel(
            arrived, nodes, edges, pick, counts, mf, ms, mt, vecs, mid_out, mid_low_out, sums,
        ):
            mfb, msb, mtb, mg, msh = [vecs[k : k + 1, :] for k in range(5)]
            width = nodes.shape[1]
            query = dot(joined(arrived), mf[width : 2 * width]).astype(BF)
            part = dot(nodes[...], mf[:width]) + mfb
            lower = mf[2 * width :]
            lots = jnp.broadcast_to(counts[...], (rows, ms.shape[1]))
            sums[...] = jnp.zeros_like(sums)

            def chunk(i, carry):
                at = pl.ds(aligned(i * span, span), span)
                pre = dot(pick[at, :], query) + dot(edges[at, :], lower)
                act = smooth_low(tiled_add(pre, part)).astype(BF)
                act = smooth_low(dot(act, ms[...]) + msb)
                total = sums[...]
                for j in range(step):
                    total = total + jnp.where(
                        lots > jnp.float32(i * step + j), act[j * rows : (j + 1) * rows], 0.0
                    )
                sums[...] = total
                return carry

            over(fanout // step, chunk)
            first = nodes[...].astype(F32) + message_mean(sums[...], counts[...], mt[...], mtb)
            mid = centred(first)[0] * mg + msh
            mid_out[...] = mid
            mid_low_out[...] = mid.astype(BF)

        return kernel

    def feed_shard(mids, we, web, wr, outs):
        mid = jnp.concatenate([v[...] for v in mids], axis=0)
        act = smooth(dot(mid, we[...]) + web[...]).astype(BF)
        dealt(outs, dot(act, wr[...]))

    def feed_end(mid, parts, vecs, send, new_out, low_out, away_out):
        rb, fg, fsh = [vecs[k : k + 1, :] for k in (5, 6, 7)]
        second = mid[...] + rb
        for v in parts:
            second = second + v[...].astype(F32)
        new = centred(second)[0] * fg + fsh
        new_out[...] = new
        low = new.astype(BF)
        low_out[...] = low
        dealt(away_out, dot(send[...], low))

    def feed_pass(mid, own, packed, vecs, send, slopes_out, second_out, new_out, low_out, away_out):
        rb, fg, fsh = [vecs[k : k + 1, :] for k in (5, 6, 7)]
        _, second = feed(mid[...], own, packed, rb, slopes_out)
        second_out[...] = second
        new = centred(second)[0] * fg + fsh
        new_out[...] = new
        low = new.astype(BF)
        low_out[...] = low
        dealt(away_out, dot(send[...], low))

    def pass_two(rows, fanout, step):
        span = step * rows

        def kernel(
            arrived, state, low, edges, pick, counts, mf, ms, mt, vecs, ef, es, et, edge_vecs,
            edge_out, act_out, slope1_out, slope2_out, first_out, summed_out, mid_out, mid_low_out, sums,
        ):
            mfb, msb, mtb, mg, msh = [vecs[k : k + 1, :] for k in range(5)]
            efb, esb, etb, eg, esh = [edge_vecs[k : k + 1, :] for k in range(5)]
            width = state.shape[1]
            received = joined(arrived)
            key = dot_nt(received, ef[:, width : 2 * width]).astype(BF)
            edge_part = dot_nt(low[...], ef[:, :width]) + efb
            edge_lower = ef[:, 2 * width :]
            query = dot(received, mf[width : 2 * width]).astype(BF)
            part = dot(low[...], mf[:width]) + mfb
            lower = mf[2 * width :]
            lots = jnp.broadcast_to(counts[...], (rows, ms.shape[1]))
            sums[...] = jnp.zeros_like(sums)

            def chunk(i, carry):
                at = pl.ds(aligned(i * span, span), span)
                chosen = pick[at, :]
                old = edges[at, :]
                pre = dot(chosen, key) + dot_nt(old, edge_lower)
                act = smooth_low(tiled_add(pre, edge_part)).astype(BF)
                act = smooth_low(dot(act, es[...]) + esb).astype(BF)
                total = old.astype(F32) + dot(act, et[...]) + etb
                fresh = centred(total)[0] * eg + esh
                edge_out[at, :] = fresh
                pre = dot(chosen, query) + dot(fresh.astype(BF), lower)
                act, slope = smooth_slope_low(tiled_add(pre, part))
                act = act.astype(BF)
                act_out[at, :] = act
                slope1_out[at, :] = slope.astype(BF)
                act, slope = smooth_slope_low(dot(act, ms[...]) + msb)
                total = sums[...]
                for j in range(step):
                    valid = lots > jnp.float32(i * step + j)
                    total = total + jnp.where(valid, act[j * rows : (j + 1) * rows], 0.0)
                    slope2_out[pl.ds(aligned(i * span + j * rows, rows), rows), :] = jnp.where(
                        valid, slope[j * rows : (j + 1) * rows], 0.0
                    ).astype(BF)
                sums[...] = total
                return carry

            over(fanout // step, chunk)
            summed_out[...] = sums[...].astype(BF)
            first = state[...] + message_mean(sums[...], counts[...], mt[...], mtb)
            first_out[...] = first
            mid = centred(first)[0] * mg + msh
            mid_out[...] = mid
            mid_low_out[...] = mid.astype(BF)

        return kernel

    def edge_turn(rows, fanout, step):
        span = step * rows

        def kernel(
            arrived, low, edges, up, pick, ef, es, et, edge_vecs,
            result_out, grad_out, act1_out, act2_out, top_out, mid_out, bottom_out,
            slot_out, node_out, vec_out, slots, node, marks,
        ):
            width = low.shape[1]
            efb, esb, etb, eg, esh = [edge_vecs[k : k + 1, :] for k in range(5)]
            key = dot_nt(joined(arrived), ef[:, width : 2 * width]).astype(BF)
            edge_part = dot_nt(low[...], ef[:, :width]) + efb
            edge_lower = ef[:, 2 * width :]
            slots[...] = jnp.zeros_like(slots)
            node[...] = jnp.zeros_like(node)
            marks[...] = jnp.zeros_like(marks)

            def chunk(i, carry):
                at = pl.ds(aligned(i * span, span), span)
                chosen = pick[at, :]
                old = edges[at, :]
                pre = dot(chosen, key) + dot_nt(old.astype(BF), edge_lower)
                act, slope1 = smooth_slope_low(tiled_add(pre, edge_part))
                act1 = act.astype(BF)
                act1_out[at, :] = act1
                act, slope2 = smooth_slope_low(dot(act1, es[...]) + esb)
                act2 = act.astype(BF)
                act2_out[at, :] = act2
                total = old + dot(act2, et[...]) + etb
                hat, rate = centred(total)
                result_out[at, :] = hat * eg + esh
                above = up[at, :].astype(F32)
                sum_grad = norm_pull(hat, rate, eg, above)
                top = sum_grad.astype(BF)
                top_out[at, :] = top
                mid = dot_nt(top, et[...]) * slope2
                mid_low = mid.astype(BF)
                mid_out[at, :] = mid_low
                bottom = dot_nt(mid_low, es[...]) * slope1
                bottom_low = bottom.astype(BF)
                bottom_out[at, :] = bottom_low
                grad_out[at, :] = sum_grad + dot(bottom_low, edge_lower)
                marks[0] += fold(above * hat, 8)
                marks[1] += fold(above, 8)
                marks[2] += fold(sum_grad, 8)
                marks[3] += fold(mid, 8)
                node[...] += fold(bottom, rows)
                slots[...] += dot_tn(chosen, bottom_low)
                return carry

            over(fanout // step, chunk)
            dealt(slot_out, slots[...])
            node_out[...] = node[...].astype(BF)
            vec_out[...] = jnp.zeros_like(vec_out)
            for j in range(4):
                vec_out[j : j + 1, :] = jnp.sum(marks[j], axis=0, keepdims=True)
            vec_out[4:5, :] = jnp.sum(node[...], axis=0, keepdims=True)

        return kernel

    def edge_weights(arrived, low, edges, act1, act2, top, mid, bottom, slot, node, pack_out):
        n, wide = act1.shape[1], low.shape[1]
        slot = jnp.concatenate([v[...] for v in slot], axis=0)
        pack_out[:n, :] = dot_tn(node[...], low[...]).astype(BF)
        pack_out[n : 2 * n, :] = dot_tn(slot, joined(arrived)).astype(BF)
        pack_out[2 * n :, :] = jnp.zeros((pack_out.shape[0] - 2 * n, wide), BF)
        pack_out[2 * n : 3 * n, :n] = dot_tn(act1[...], mid[...]).astype(BF)
        pack_out[2 * n : 3 * n, 256 : 256 + n] = dot_tn(act2[...], top[...]).astype(BF)
        lower = dot_tn(bottom[...], edges[...].astype(BF)).astype(BF)
        pack_out[3 * n :, :n] = lower[: n // 2]
        pack_out[3 * n :, 256 : 256 + n] = lower[n // 2 :]

    def node_turn(
        spot, returned, up, node, send, second, slopes, first, counts, summed, ef, mt, vecs,
        own, packed, pack, edge_vec, mid_low, pair_out, sum_out, pull_out, pay_out, pay,
    ):
        width = up.shape[1]
        key_low = dot_tn(send[...], joined(returned)).astype(BF)
        new_grad = (
            up[...].astype(F32) + dot(node[...], ef[:, :width]) + dot(key_low, ef[:, width : 2 * width])
        )
        hat, rate = centred(second[...])
        sum_grad = norm_pull(hat, rate, vecs[6:7, :], new_grad)
        marks = [sum_grad, new_grad * hat, new_grad]
        low = sum_grad.astype(BF)
        pair_out[:, :width] = mid_low[...]
        pair_out[:, width:] = low
        mid_grad = sum_grad
        bias = []
        for h, (we, _, wr) in enumerate(shards(own, packed)):
            expand = dot_nt(low, wr) * slopes[h].astype(F32)
            bias.append(jnp.sum(expand, axis=0, keepdims=True))
            mid_grad = mid_grad + dot_nt(expand.astype(BF), we)
        hat, rate = centred(first[...])
        first_grad = norm_pull(hat, rate, vecs[3:4, :], mid_grad)
        sum_out[...] = first_grad
        marks += [mid_grad * hat, mid_grad, first_grad]
        marks = [jnp.sum(v, axis=0, keepdims=True) for v in marks]
        rows_low = (first_grad / counts[...]).astype(BF)
        pull_out[...] = dot_nt(rows_low, mt[...])
        third = dot_tn(summed[...], rows_low).astype(BF)
        head, hidden = pack.shape[0], third.shape[0]
        pay[:head, :] = pack[...]
        pay[head : head + hidden, :] = third
        pay[head + hidden :, :] = jnp.zeros((pay.shape[0] - head - hidden, width), BF)
        rows = jnp.concatenate(marks + [jnp.zeros((10, width), F32)], axis=0)
        at = lax.broadcasted_iota(jnp.int32, rows.shape, 0)
        share = bias[0].shape[1]
        for h, v in enumerate(bias):
            line = 6 + ((spot[2] ^ h) if tuned else h)
            if share < width:
                v = jnp.concatenate([v, jnp.zeros((1, width - share), F32)], axis=1)
            rows = jnp.where(at == line, v, rows)
        pay[head + hidden : head + hidden + 16, :] = rows.astype(BF)
        pay[head + hidden + 16 : head + hidden + 32, : edge_vec.shape[1]] = jnp.concatenate(
            [edge_vec[...], jnp.zeros_like(edge_vec)], axis=0
        ).astype(BF)
        if len(pay_out) == 1:
            pay_out[0][...] = pay[...]
        else:
            halved(spot, pay, *pay_out)

    def message_second(rows, fanout, step):
        span = step * rows

        def kernel(pull, act, slope2, second_out, weight_out, vec_out, marks):
            marks[...] = jnp.zeros_like(marks)

            def chunk(i, carry):
                at = pl.ds(aligned(i * span, span), span)
                second = slope2[at, :].astype(F32).reshape(step, rows, -1) * pull[...][None]
                marks[...] += jnp.sum(second, axis=0)
                second_out[at, :] = second.reshape(span, -1).astype(BF)
                return carry

            over(fanout // step, chunk)
            weight_out[...] = dot_tn(act[...], second_out[...]).astype(BF)
            vec_out[...] = jnp.zeros_like(vec_out)
            vec_out[0:1, :] = jnp.sum(marks[...], axis=0, keepdims=True)

        return kernel

    def message_first(rows, fanout, step):
        span = step * rows

        def kernel(
            arrived, low, edges, pick, second, slope1, ms, weight, vec,
            first_low_out, slot_out, node_out, pay, slots, node,
        ):
            width = low.shape[1]
            slots[...] = jnp.zeros_like(slots)
            node[...] = jnp.zeros_like(node)

            def chunk(i, carry):
                at = pl.ds(aligned(i * span, span), span)
                first = dot_nt(second[at, :], ms[...]) * slope1[at, :].astype(F32)
                node[...] += fold(first, rows)
                first = first.astype(BF)
                first_low_out[at, :] = first
                slots[...] += dot_tn(pick[at, :], first)
                return carry

            over(fanout // step, chunk)
            slot = slots[...].astype(BF)
            dealt(slot_out, slot)
            node_low = node[...].astype(BF)
            node_out[...] = node_low
            hidden, last = ms.shape[0], 2 * width + edges.shape[1]
            pay[:width, :] = dot_tn(low[...], node_low).astype(BF)
            pay[width : 2 * width, :] = dot_tn(joined(arrived), slot).astype(BF)
            pay[2 * width : last, :] = dot_tn(edges[...].astype(BF), first_low_out[...]).astype(BF)
            pay[last : last + hidden, :] = weight[...]
            pay[last + hidden :, :] = jnp.zeros((pay.shape[0] - last - hidden, hidden), BF)
            vecs = [jnp.sum(node[...], axis=0, keepdims=True), vec[0:1, :], jnp.zeros((14, hidden), F32)]
            pay[last + hidden : last + hidden + 16, :] = jnp.concatenate(vecs, axis=0).astype(BF)

        return kernel

    def feed_products(pairs, we, web, wr):
        n = we.shape[0]
        mid = jnp.concatenate([v[:, :n] for v in pairs], axis=0)
        up = jnp.concatenate([v[:, n:] for v in pairs], axis=0)
        act, slope = smooth_slope_low(dot(mid, we[...]) + web[...])
        expand = dot_nt(up, wr[...]) * slope
        return dot_tn(mid, expand.astype(BF)), dot_tn(act, up)

    def feed_weights(pairs, we, web, wr, expand_out, reduce_out):
        expand_out[...], reduce_out[...] = feed_products(pairs, we, web, wr)

    def feed_weights_more(pairs, we, web, wr, expand, reduce, expand_out, reduce_out):
        left, right = feed_products(pairs, we, web, wr)
        expand_out[...], reduce_out[...] = expand[...] + left, reduce[...] + right

    def node_end(returned, send, first_grad, node, mf, out):
        width = out.shape[1]
        query_low = dot_tn(send[...], joined(returned)).astype(BF)
        out[...] = (
            first_grad[...] + dot_nt(node[...], mf[:width]) + dot_nt(query_low, mf[width : 2 * width])
        )

    def edge_end(rows, fanout, step):
        span = step * rows

        def kernel(grad, first_low, mf, out):
            lower = mf[mf.shape[0] - grad.shape[1] :]

            def chunk(i, carry):
                at = pl.ds(aligned(i * span, span), span)
                out[at, :] = grad[at, :] + dot_nt(first_low[at, :], lower)
                return carry

            over(fanout // step, chunk)

        return kernel

    def split_chips(keep, got, outs):
        n = keep.shape[0] // len(outs)
        for m, out in enumerate(outs):
            at = slice(m * n, (m + 1) * n)
            out[:n, :] = (keep[at, :].astype(F32) + got[at, :].astype(F32)).astype(BF)

    def split_chips_more(keep, got, more, outs):
        split_chips(keep, got, outs)
        for v, out in zip(more, outs):
            out[out.shape[0] - v.shape[0] :, :] = v[...]

    def add_up(parts, out):
        n = out.shape[0]
        total = parts[0][:n, :].astype(F32)
        for v in parts[1:]:
            total = total + v[:n, :].astype(F32)
        out[...] = total.astype(BF)

    def add_up_more(spot, parts, keep, send, mine, twin, out):
        add_up(parts, out)
        n, side = keep.shape[1], spot[2] % 2
        keep[...] = out[:, pl.ds(pl.multiple_of(side * n, n), n)]
        send[...] = out[:, pl.ds(pl.multiple_of((1 - side) * n, n), n)]
        n = mine.shape[0] // len(parts)
        for m, v in enumerate(parts):
            at, top = slice(m * n, (m + 1) * n), out.shape[0]
            mine[at, :] = v[top : top + n, :]
            twin[at, :] = v[top + n : top + 2 * n, :]

    def add_up_join(parts, more, out):
        n = more.shape[0]
        out[:n, :] = more[...]
        total = parts[0][...].astype(F32)
        for v in parts[1:]:
            total = total + v[...].astype(F32)
        out[n:, :] = total.astype(BF)

    def add_up_sides(spot, parts, pay, keep, send, pay_keep, pay_send, total):
        add_up(parts, total)
        halved(spot, pay, pay_keep, pay_send)
        n, side = keep.shape[1], spot[2] // 2
        keep[...] = total[:, pl.ds(pl.multiple_of(side * n, n), n)]
        send[...] = total[:, pl.ds(pl.multiple_of((1 - side) * n, n), n)]

    def join_near(spot, mine, other, out):
        join_sides(spot, mine, other, out, spot[2] % 2)

    def join_far(spot, mine, other, out):
        join_sides(spot, mine, other, out, spot[2] // 2)

    def join_sides(spot, mine, other, out, side):
        n = mine.shape[1]
        out[:, pl.ds(pl.multiple_of(side * n, n), n)] = mine[...]
        out[:, pl.ds(pl.multiple_of((1 - side) * n, n), n)] = other[...]

    def sort_cores(parts, mine, twin):
        n = mine.shape[0] // len(parts)
        for m, v in enumerate(parts):
            at = slice(m * n, (m + 1) * n)
            mine[at, :] = v[:n, :]
            twin[at, :] = v[n : 2 * n, :]

    def add_two(left, right, more, out):
        n = left.shape[0]
        out[:n, :] = (left[...].astype(F32) + right[...].astype(F32)).astype(BF)
        if more:
            out[n:, :] = more[0][...]

    def to_chips(parts):
        far = to_chip(parts[3], 3)
        return [parts[0], to_chip(parts[1], 1), to_chip(parts[2], 2), far]

    def spread(own):
        parts = [own] + [to_chip(own, m) for m in (1, 2, 3)]
        return parts + [to_core(v) for v in parts]

    def laid_out(spot, parts, total):
        n = parts[0].shape[0]
        for k, v in enumerate(parts):
            at = (2 * (spot[1] ^ (k % 4)) + (spot[0] ^ (k // 4))) * n
            total[pl.ds(pl.multiple_of(at, n), n), :] = v[...].astype(total.dtype)

    def lay_pair(spot, stacks, total):
        n = total.shape[0] // 8
        for k in range(8):
            at = (2 * (spot[1] ^ (k % 4)) + (spot[0] ^ (k // 4))) * n
            top = k % 4 * n
            total[pl.ds(pl.multiple_of(at, n), n), :] = stacks[k // 4][top : top + n, :].astype(total.dtype)

    def stack_up(parts, out):
        n = parts[0].shape[0]
        for m, v in enumerate(parts):
            out[m * n : (m + 1) * n, :] = v[...]

    def unpack_early(
        spot, parts, first_out, second_out, third_out, message_out, vec_out, edge_vec_out, bias_out, total,
    ):
        if len(parts) == 1:
            total[...] = parts[0][...]
        else:
            lay_pair(spot, parts, total)
        n, wide = second_out.shape[0], message_out.shape[1]
        first_out[:, :wide] = total[:n, :]
        first_out[:, wide : 2 * wide] = total[n : 2 * n, :]
        second_out[...] = total[2 * n : 3 * n, :n]
        third_out[...] = total[2 * n : 3 * n, 256 : 256 + n]
        at = 3 * n + n // 2
        first_out[: n // 2, 2 * wide :] = total[3 * n : at, :n]
        first_out[n // 2 :, 2 * wide :] = total[3 * n : at, 256 : 256 + n]
        hidden = message_out.shape[0]
        message_out[...] = total[at : at + hidden, :]
        for k, out in enumerate(vec_out):
            out[...] = total[at + hidden + k : at + hidden + k + 1, :]
        for k, out in enumerate(edge_vec_out):
            out[...] = total[at + hidden + 16 + k : at + hidden + 17 + k, :n]
        vecs = total[at + hidden : at + hidden + 16, :]
        line = lax.broadcasted_iota(jnp.int32, vecs.shape, 0) == 6 + spot[2]
        bias = jnp.sum(jnp.where(line, vecs, 0.0), axis=0, keepdims=True)
        bias_out[...] = bias[:, : bias_out.shape[1]]

    def unpack_late(spot, parts, total):
        if len(parts) == 1:
            total[...] = parts[0][...]
        else:
            lay_pair(spot, parts, total)

    def split_relay(left, right, left_out, right_out):
        n = left_out.shape[1]
        left_out[...] = left[:, :n]
        right_out[...] = right[:, n:]

    def stack_relay(parts, left, right, out):
        n, half = left.shape
        for m, v in enumerate(parts):
            out[m * n : (m + 1) * n, :] = v[...]
        out[len(parts) * n :, :half] = left[...]
        out[len(parts) * n :, half:] = right[...]

    def join_pieces(parts, out):
        for m, v in enumerate(parts):
            n = v.shape[1]
            out[:, m * n : (m + 1) * n] = v[...]

    def body(
        nodes, edges, send_rows, neighbor_slots, neighbor_counts, mf, mfb, ms, msb, mt, mtb, mg, msh,
        expand_weight, expand_bias, reduce_weight, rb, fg, fsh, ef, efb, es, esb, et, etb, eg, esh,
        node_up, edge_up,
    ):
        rows, fanout, edge_width = edges.shape
        width, hidden = nodes.shape[1], ms.shape[0]
        share = expand_weight.shape[1]
        n_edges = rows * fanout
        step = fanout
        slots_each = send_rows.shape[2]
        buffer = n_res * slots_each
        row = lambda v: v.reshape(1, -1)
        if tuned:
            res, hid = lax.axis_index("res"), lax.axis_index("hid")
            spot = jnp.stack([res % 2, res // 2, hid, res]).astype(jnp.int32)
        else:
            spot = jnp.stack([0, 0, lax.axis_index("hid"), 0]).astype(jnp.int32)
        edges = edges.transpose(1, 0, 2).reshape(n_edges, edge_width)
        edge_up = edge_up.transpose(1, 0, 2).reshape(n_edges, edge_width)
        ef = ef.T
        bias = row(expand_bias)
        own = (expand_weight, bias, reduce_weight)
        one = struct((rows, width), BF)
        deal = [one] * 4 if tuned else [struct((buffer, width), BF)]
        n_piece = width // 8 * 9 // 4
        away, send, piece = call(
            prepare_send,
            [deal, struct((buffer, rows), BF), [struct((n_piece, width), BF)] if tuned else []],
            (send_rows[0], nodes, (expand_weight, reduce_weight, bias) if tuned else ()),
            "prepare_send",
            spot=spot,
            far=True,
        )
        pick, counts, vecs, edge_vecs, edges = call(
            prepare_rest,
            [
                struct((n_edges, buffer), BF),
                struct((rows, 1), F32),
                struct((8, width), F32),
                struct((8, edge_width), F32),
                struct((n_edges, edge_width), BF),
            ],
            (
                neighbor_slots,
                row(neighbor_counts),
                [row(v) for v in (mfb, msb, mtb, mg, msh, rb, fg, fsh)],
                [row(v) for v in (efb, esb, etb, eg, esh)],
                edges,
            ),
            "prepare_rest",
            spot=spot,
            after=away[:1],
            far=True,
        )
        if tuned:
            half = struct((rows * 2, width), BF)
            mine, twin = call(sort_cores, [half, half], (to_chips(away),), "first_sort", after=[counts])
            arrived = [mine, to_core(twin)]
        else:
            arrived = exchange(away)
        edge_args = (ef, es, et, edge_vecs)
        if tuned:
            pieces = [to_hid(piece[0], m) for m in (1, 2, 3)]
            (piece,) = call(
                join_pieces, [struct((n_piece, 3 * width), BF)], (pieces,), "join_pieces", after=[counts] + arrived
            )
            packed, first = [piece] + [to_chip(piece, m) for m in (1, 2)], [piece]
        else:
            packed, first = [
                lax.all_gather(expand_weight, "hid"),
                lax.all_gather(expand_bias, "hid"),
                lax.all_gather(reduce_weight, "hid"),
            ], []
        mid, mid_low = call(
            pass_one(rows, fanout, step),
            [struct((rows, width), F32), one],
            (arrived, nodes, edges, pick, counts, mf, ms, mt, vecs),
            "message_one",
            [pltpu.VMEM((rows, hidden), F32)],
            after=first,
        )
        if tuned:
            mids = [mid_low] + [to_hid(mid_low, m) for m in (1, 2, 3)]
            (parts,) = call(
                feed_shard, [[one] * 4], (mids, expand_weight, bias, reduce_weight), "feed_shard"
            )
            relay = struct((n_piece, 3 * width // 2), BF)
            left, right = call(
                split_relay, [relay, relay], tuple(packed[1:]), "split_weights", after=parts[:1]
            )
            parts = [parts[0]] + [to_hid(parts[m], m) for m in (1, 2, 3)]
        else:
            mids = [lax.all_gather(mid_low, "hid", axis=0, tiled=True)]
            (part,) = call(
                feed_shard,
                [[struct((n_hid * rows, width), BF)]],
                (mids, expand_weight, bias, reduce_weight),
                "feed_shard",
            )
            parts = [lax.psum_scatter(part[0], "hid", scatter_dimension=0, tiled=True)]
        state, low, away = call(
            feed_end, [struct((rows, width), F32), one, deal], (mid, parts, vecs, send), "feed_one"
        )
        if tuned:
            (packed,) = call(
                stack_relay,
                [struct((4 * n_piece, 3 * width), BF)],
                (packed, to_chip(left, 2), to_chip(right, 1)),
                "stack_weights",
                after=[low],
            )
            packed = [packed, to_core(packed)]
        arrived2, low2 = exchange(away), low
        first = []
        if tuned:
            (packed,) = call(
                lay_pair, [struct((8 * n_piece, 3 * width), BF)], (packed,), "lay_weights", spot=spot
            )
            first = packed = [packed]
        edge_state, act, slope1, slope2, first, summed, mid, mid_low = call(
            pass_two(rows, fanout, step),
            [
                struct((n_edges, edge_width), F32),
                struct((n_edges, hidden), BF),
                struct((n_edges, hidden), BF),
                struct((n_edges, hidden), BF),
                struct((rows, width), F32),
                struct((rows, hidden), BF),
                struct((rows, width), F32),
                one,
            ],
            (arrived2, state, low2, edges, pick, counts, mf, ms, mt, vecs, *edge_args),
            "layer_two",
            [pltpu.VMEM((rows, hidden), F32)],
            after=first,
        )
        feed_outs = [
            struct((n_hid, rows, share), BF),
            struct((rows, width), F32),
            jax.ShapeDtypeStruct((rows, width), F32),
            one,
            deal,
        ]
        slopes, second, node_result, low3, away = call(
            feed_pass, feed_outs, (mid, own, packed, vecs, send), "feed_two"
        )
        arrived3 = exchange(away)
        wide = lambda dtype: struct((n_edges, edge_width), dtype)
        edge_result, edge_grad, act1, act2, top, mid, bottom, slot, node, edge_vec = call(
            edge_turn(rows, fanout, step),
            [
                jax.ShapeDtypeStruct((n_edges, edge_width), F32),
                wide(F32), wide(BF), wide(BF), wide(BF), wide(BF), wide(BF),
                [struct((buffer // len(deal), edge_width), BF)] * len(deal),
                struct((rows, edge_width), BF),
                struct((8, edge_width), F32),
            ],
            (arrived3, low3, edge_state, edge_up, pick, *edge_args),
            "edge_turn",
            [
                pltpu.VMEM((buffer, edge_width), F32),
                pltpu.VMEM((rows, edge_width), F32),
                pltpu.VMEM((4, 8, edge_width), F32),
            ],
        )
        head = 3 * edge_width + edge_width // 2
        (pack,) = call(
            edge_weights,
            [struct((head, width), BF)],
            (arrived3, low3, edge_state, act1, act2, top, mid, bottom, slot, node),
            "edge_weights",
        )
        if tuned:
            half = struct((rows * 2, edge_width), BF)
            mine, twin = call(sort_cores, [half, half], (to_chips(slot),), "edge_sort", after=[pack])
            returned = [mine, to_core(twin)]
        else:
            returned = exchange(slot)
        sized = lambda n: -(-n // 128) * 128
        n_early, n_late = sized(head + hidden + 32), sized(mf.shape[0] + hidden + 16)
        cut = lambda n: [struct((n // 2, width), BF)] * 2 if tuned else [struct((n, width), BF)]
        pair, first_grad, pull, early = call(
            node_turn,
            [struct((rows, 2 * width), BF), struct((rows, width), F32), struct((rows, hidden), F32), cut(n_early)],
            (
                returned, node_up, node, send, second, slopes, first, counts, summed, ef, mt, vecs,
                own, packed, pack, edge_vec, mid_low,
            ),
            "node_turn",
            [pltpu.VMEM((n_early, width), BF)],
            spot=spot,
        )
        eighth = lambda n: struct((n // 8, width), BF)
        second_low, second_weight, message_vec = call(
            message_second(rows, fanout, step),
            [struct((n_edges, hidden), BF), struct((hidden, hidden), BF), struct((8, hidden), F32)],
            (pull, act, slope2),
            "message_second",
            [pltpu.VMEM((rows, hidden), F32)],
        )
        feed_own = (expand_weight, bias, reduce_weight)

        first = []
        if tuned:
            (early,) = call(
                split_chips, [[eighth(n_early)] * 4], (early[0], to_core(early[1])), "early_chips",
                after=[second_weight],
            )
            first = early[:1]
            early = to_chips(early)
        else:
            early = lax.psum(early[0].astype(F32), ("res", "hid"))
        first_low, slot, node, late = call(
            message_first(rows, fanout, step),
            [
                struct((n_edges, hidden), BF),
                [struct((buffer // len(deal), hidden), BF)] * len(deal),
                struct((rows, hidden), BF),
                struct((n_late, hidden), BF),
            ],
            (arrived2, low2, edge_state, pick, second_low, slope1, ms, second_weight, message_vec),
            "message_first",
            [
                pltpu.VMEM((buffer, hidden), F32),
                pltpu.VMEM((rows, hidden), F32),
            ],
            after=first,
        )
        final = Final
        if tuned:
            (pair,) = call(
                stack_up, [struct((2 * rows, 2 * width), BF)], ([pair, to_hid(pair, 2)],), "pair_stack",
                after=[node],
            )
            side = struct((n_early // 8, width // 2), BF)
            early, other, keep, send_late = call(
                add_up_sides, [side, side] + cut(n_late), (early, late), "early_plane",
                [pltpu.VMEM((n_early // 8, width), BF)], spot=spot, after=[pair],
            )
            (late,) = call(
                split_chips_more,
                [[struct((n_late // 8 + rows, width), BF)] * 4],
                (keep, to_core(send_late), slot),
                "late_chips",
            )
            last = late[0]
            late = to_chips(late)
            (early,) = call(add_two, [side], (early, to_hid(other, 2), []), "early_line", after=[last])
            (early,) = call(add_two, [side], (early, to_hid(early, 1), []), "early_line")
            (pair,) = call(
                stack_up, [struct((4 * rows, 2 * width), BF)], ([pair, to_hid(pair, 1)],), "pair_stack",
                after=[early],
            )
            half = struct((rows * 2, width), BF)
            late_side = struct((n_late // 8, width // 2), BF)
            late, other, mine, twin = call(
                add_up_more, [late_side, late_side, half, half], (late,), "late_plane",
                [pltpu.VMEM((n_late // 8, width), BF)], spot=spot, after=[pair],
            )
            pairs = [pair] + [to_chip(pair, m) for m in (1, 2, 3)]
            (late,) = call(add_two, [late_side], (late, to_hid(other, 1), []), "late_line")
            (early,) = call(
                join_far, [eighth(n_early)], (early, to_hid(early, 2)), "early_line", spot=spot, after=[late]
            )
            (pair,) = call(
                stack_up, [struct((16 * rows, 2 * width), BF)], (pairs,), "pair_stack", after=[early]
            )
            last = pair
            early = [early] + [to_chip(early, m) for m in (1, 2)]
            returned = [mine, to_core(twin)]
            node_gradient, last = call(
                node_end,
                [final(rows, width)],
                (returned, send, first_grad, node, mf),
                "node_end",
                after=[last],
                token=True,
            )
            (late,) = call(
                add_two, [late_side], (late, to_hid(late, 2), []), "late_line", after=[last]
            )
            left, right = call(split_relay, [side, side], tuple(early[1:]), "early_split", after=[late])
            edge_gradient, last = call(
                edge_end(rows, fanout, step),
                [final(n_edges, edge_width)],
                (edge_grad, first_low, mf),
                "edge_end",
                after=[left],
                token=True,
            )
            (late,) = call(
                join_near, [eighth(n_late)], (late, to_hid(late, 1)), "late_join", spot=spot, after=[last]
            )
            (early,) = call(
                stack_relay,
                [struct((n_early // 2, width), BF)],
                (early, to_chip(left, 2), to_chip(right, 1)),
                "early_stack",
                after=[late],
            )
            early = [early, to_core(early)]
            late = [late] + [to_chip(late, m) for m in (1, 2, 3)]
            pairs = [pair, to_core(pair)]
        else:
            late = [lax.psum(late.astype(F32), ("res", "hid"))]
            early = [early]
            pairs = [lax.all_gather(pair, "hid", axis=0, tiled=True)]
            expand_grad, reduce_grad = call(
                feed_weights,
                [struct((width, share), F32), struct((share, width), F32)],
                (pairs, *feed_own),
                "feed_weights",
                after=[node],
            )
            returned = exchange(slot)
            (edge_gradient,) = call(
                edge_end(rows, fanout, step), [final(n_edges, edge_width)], (edge_grad, first_low, mf), "edge_end"
            )
            (node_gradient,) = call(
                node_end, [final(rows, width)], (returned, send, first_grad, node, mf), "node_end"
            )
        (
            edge_first_grad, edge_second_grad, edge_third_grad, third_grad, vec, edge_vecs, expand_bias_grad,
            last,
        ) = call(
            unpack_early,
            [
                final(edge_width, ef.shape[1]), final(edge_width, edge_width), final(edge_width, edge_width),
                final(hidden, width), [final(1, width)] * 6, [final(1, edge_width)] * 5, final(1, share),
            ],
            (early,),
            "unpack_early",
            [pltpu.VMEM((n_early, width), F32)],
            limit=16,
            spot=spot,
            token=True,
        )
        if tuned:
            expand_grad, reduce_grad = call(
                feed_weights,
                [struct((width, share), F32), struct((share, width), F32)],
                (pairs[:1], *feed_own),
                "feed_weights",
                after=[last],
            )
            (late,) = call(
                stack_up, [struct((n_late // 2, width), BF)], (late,), "late_stack", after=[expand_grad]
            )
            last = late
            late = [late, to_core(late)]
            expand_grad, reduce_grad, last = call(
                feed_weights_more,
                [Final(width, share), Final(share, width)],
                (pairs[1:], *feed_own, expand_grad, reduce_grad),
                "feed_weights_more",
                after=[last],
                token=True,
            )
            last = [last]
        else:
            last = []
        c = mf.shape[0]
        first_weight_grad, second_weight_grad, message_vec = call(
            unpack_late,
            [
                Cut(n_late, width, c),
                Cut(n_late, width, c + hidden, c),
                [Cut(n_late, width, c + hidden + k + 1, c + hidden + k) for k in range(2)],
            ],
            (late,),
            "unpack_late",
            spot=spot,
            after=last,
        )
        if not tuned:
            expand_grad, reduce_grad = [lax.psum(v, "res") for v in (expand_grad, reduce_grad)]
        vec, edge_vecs, message_vec = [[v[0] for v in group] for group in (vec, edge_vecs, message_vec)]

        back = lambda v: v.reshape(fanout, rows, edge_width).transpose(1, 0, 2)
        return (
            node_result,
            back(edge_result),
            node_gradient,
            back(edge_gradient),
            first_weight_grad,
            message_vec[0],
            second_weight_grad,
            message_vec[1],
            third_grad,
            vec[5],
            vec[3],
            vec[4],
            expand_grad,
            expand_bias_grad[0],
            reduce_grad,
            vec[0],
            vec[1],
            vec[2],
            edge_first_grad.T,
            edge_vecs[4],
            edge_second_grad,
            edge_vecs[3],
            edge_third_grad,
            edge_vecs[2],
            edge_vecs[0],
            edge_vecs[1],
        )

    both = ("res", "hid")
    rows2, rows3 = P(both, None), P(both, None, None)
    placed = (
        rows2, rows3, rows3, rows2, P(both),
        P(), P(), P(), P(), P(), P(), P(), P(),
        P(None, "hid"), P("hid"), P("hid", None),
        P(), P(), P(), P(), P(), P(), P(), P(), P(), P(), P(),
        rows2, rows3,
    )
    given = (
        rows2, rows3, rows2, rows3,
        P(), P(), P(), P(), P(), P(), P(), P(),
        P(None, "hid"), P("hid"), P("hid", None),
        P(), P(), P(), P(), P(), P(), P(), P(), P(), P(), P(),
    )
    return jax.shard_map(body, mesh=mesh, in_specs=placed, out_specs=given, check_vma=False)
```
